128 devices in a mesh: grp: 4 (over y), sub: 32 (over x, z, core).
Axes of the slice: x: 4, y: 4, z: 4, core: 2. Of those that a mesh axis runs over, the one named last changes fastest.
Arguments:
- basis_cols: bfloat16 [128, 1024, 32, 128], P('grp', 'sub'), may hold values from -0.375 to 0.375
- diag_weight: float32 [128, 1024, 32], P('grp', 'sub'), may hold values from 0.5 to 4
- link_weight: float32 [128, 1024, 32], P('grp', 'sub'), may hold values from 0.3 to 1
- base_front: bfloat16 [16384, 16384], P('grp', 'sub'), may hold values from -4 to 4
- block_lists: int32 [16384, 2], replicated, may hold values from 0 to 127, as said below
Outputs:
- trailing: float32 [16384, 16384], P('grp', 'sub')
- panel_factor: bfloat16 [16384, 512], P(('grp', 'sub'))
The draws below stay inside these ranges and needn't reach their ends.
Inputs may be any that keep to these rules, and one draw needn't show every extreme that they name: `block_lists`: rows follow the tiles' numbering. Every row block is at least its column block, and row block times 128 is at least 512. Block (a, b) is held by the device (a // 32, b // 4) of the mesh; at most 2 tiles of one subdomain go to blocks held by one device, and in every draw some subdomain sends exactly 2 to one device.
All inputs are finite; a program needn't handle non-finite values.
Results may differ from the reference program's by a relative error of at most 0.0039.
Values may be sent and summed in bfloat16 or wider, within the bound.
A program may use at most 192 MiB of HBM per device.

```python
import math
import jax
import jax.numpy as jnp
from jax import lax

KB = 128
CX = 32
CY = 32
CZ = 32
TILES_DEV = 128
CAP = 2
REG_CELLS = 256
NX = 128
NY = 1024
NF = 16384
PANEL = 512
N_GRP = 4
N_SUB = 32
DEVICES = 128


def draw_base_front(key, part):
    keys = jax.random.split(jax.random.fold_in(key, 29), 6)
    values = jax.random.normal(keys[0], (NF, NF), jnp.float32)
    light = 0.01 * jax.random.normal(keys[2], (NF, NF), jnp.float32)
    heavy_size = jax.random.uniform(keys[3], (NF, NF), jnp.float32, 2.0, 4.0)
    values = jnp.clip(values, -4.0, 4.0)
    signs = jnp.where(jax.random.uniform(keys[4], (NF, NF), jnp.float32) < 0.5, 1.0, -1.0)
    heavy = jax.random.uniform(keys[5], (NF, NF), jnp.float32) < 4.0 / PANEL
    lead = jnp.clip(light + jnp.where(heavy, signs * heavy_size, 0.0), -4.0, 4.0)
    indices = jnp.arange(NF)
    inner = (indices[:, None] < PANEL) & (indices[None, :] < PANEL)
    return jnp.where(inner, lead, values).astype(jnp.bfloat16)


def sender_lists(key):
    keys = jax.random.split(key, 5)
    owners = jnp.arange(DEVICES, dtype=jnp.int32)
    owner_grp = owners // N_SUB
    owner_sub = owners % N_SUB
    usable = owner_grp * N_SUB + N_SUB - 1 >= jnp.maximum(owner_sub * N_GRP, N_GRP)
    forced_scores = jax.random.permutation(keys[0], DEVICES).astype(jnp.int32) + jnp.where(usable, 0, DEVICES)
    forced = jnp.argsort(forced_scores)[0]
    candidates = jnp.repeat(owners, CAP)
    total = DEVICES * CAP
    ranks = jax.random.permutation(keys[1], total).astype(jnp.int32)
    scores = ranks + jnp.where(usable[candidates], 0, total)
    scores = jnp.where(candidates == forced, -1 - jnp.arange(total, dtype=jnp.int32), scores)
    picked = candidates[jnp.argsort(scores)[:TILES_DEV]]
    picked = picked[jax.random.permutation(keys[2], TILES_DEV)]
    picked_grp = picked // N_SUB
    picked_sub = picked % N_SUB
    row_low = jnp.maximum(jnp.maximum(picked_grp * N_SUB, picked_sub * N_GRP), N_GRP)
    row_high = picked_grp * N_SUB + N_SUB
    rows = jax.random.randint(keys[3], (TILES_DEV,), row_low, row_high, dtype=jnp.int32)
    col_low = picked_sub * N_GRP
    col_high = jnp.minimum(picked_sub * N_GRP + N_GRP, rows + 1)
    cols = jax.random.randint(keys[4], (TILES_DEV,), col_low, col_high, dtype=jnp.int32)
    return jnp.stack([rows, cols], axis=1)


def draw_block_lists(key, part):
    sender_keys = jax.random.split(jax.random.fold_in(key, 17), DEVICES)
    return jax.vmap(sender_lists)(sender_keys).reshape(DEVICES * TILES_DEV, 2)


def block_scale(rng, shape, shards, smallest, top_value):
    loudness, own = 1.0, jax.random.fold_in(rng, 6)
    for position, parts in shards:
        steps = jnp.exp(jax.random.uniform(jax.random.fold_in(own, position), (parts,), jnp.float32, smallest / len(shards), top_value / len(shards)))
        loudness = loudness * jnp.repeat(steps, shape[position] // parts).reshape([-1 if axis == position else 1 for axis in range(len(shape))])
    return loudness


def noise(stream_key, shape, spread, limit, cuts=(), kind=jnp.bfloat16):
    values = spread * jax.random.normal(stream_key, shape, jnp.float32)
    if cuts:
        values = values * block_scale(stream_key, shape, cuts, -0.22, 0.18)
    return jnp.clip(values, -limit, limit).astype(kind)


def setup_inputs(seed: int = 0) -> dict:
    splits = jax.random.split(jax.random.key(seed), 6)
    basis_cols = noise(splits[0], (NX, NY, CZ, KB), REG_CELLS ** -0.5, 0.375, ((0, 4), (1, 32)))
    diag_weight = jnp.clip(jnp.exp(math.log(4.0) - 2.0794415 * jax.random.uniform(splits[1], (NX, NY, CZ), jnp.float32) ** block_scale(splits[1], (NX, NY, CZ), ((0, 4), (1, 32)), -0.2, 0.2)), 0.5, 4.0)
    link_weight = jnp.clip(jnp.exp(math.log(1.0) - 1.2039728 * jax.random.uniform(splits[2], (NX, NY, CZ), jnp.float32) ** block_scale(splits[2], (NX, NY, CZ), ((0, 4), (1, 32)), -0.2, 0.2)), 0.3, 1.0)
    base_front = draw_base_front(jax.random.fold_in(splits[5], 71), 0)
    block_lists = draw_block_lists(jax.random.fold_in(splits[5], 71), 0)
    return {"basis_cols": basis_cols, "diag_weight": diag_weight, "link_weight": link_weight, "base_front": base_front, "block_lists": block_lists}


def apply_operator(basis_cols, padded, diag_weight, link_weight):
    lifted = padded.astype(jnp.float32)
    along_x = lifted[:-2] + lifted[1:-1] + lifted[2:]
    along_y = along_x[:, :-2] + along_x[:, 1:-1] + along_x[:, 2:]
    along_z = along_y[:, :, :-2] + along_y[:, :, 1:-1] + along_y[:, :, 2:]
    neighbours = along_z - lifted[1:-1, 1:-1, 1:-1]
    return diag_weight[..., None] * basis_cols.astype(jnp.float32) - link_weight[..., None] * neighbours

def pivot_factor(lead_block):
    symmetric = jnp.tril(lead_block) + jnp.tril(lead_block, -1).T
    shifted = symmetric + jnp.diag(jnp.sum(jnp.abs(symmetric), axis=1) + 1.0)
    return jnp.linalg.cholesky(shifted)

def reference(basis_cols, diag_weight, link_weight, base_front, block_lists):
    scaled = (link_weight[..., None] * basis_cols.astype(jnp.float32)).astype(jnp.bfloat16)
    padded = jnp.pad(scaled, ((1, 1), (1, 1), (1, 1), (0, 0)))
    blocks = N_GRP * N_SUB
    segment_ids = block_lists[:, 0] * blocks + block_lists[:, 1]
    per_group = N_SUB * TILES_DEV

    def regions(field):
        return field.reshape(CX, N_SUB, CY, CZ, KB).transpose(1, 0, 2, 3, 4).reshape(per_group, REG_CELLS, KB)

    def group_step(running, group):
        start = group * CX
        slab_pad = lax.dynamic_slice_in_dim(padded, start, CX + 2, 0)
        slab_basis = lax.dynamic_slice_in_dim(basis_cols, start, CX, 0)
        slab_diag = lax.dynamic_slice_in_dim(diag_weight, start, CX, 0)
        slab_link = lax.dynamic_slice_in_dim(link_weight, start, CX, 0)
        image_field = apply_operator(slab_basis, slab_pad, slab_diag, slab_link)
        tile_set = jnp.einsum('rck,rcl->rkl', regions(slab_basis).astype(jnp.float32), regions(image_field), precision=lax.Precision.HIGHEST)
        group_ids = lax.dynamic_slice_in_dim(segment_ids, group * per_group, per_group, 0)
        added = jax.ops.segment_sum(tile_set.reshape(per_group, KB * KB), group_ids, num_segments=blocks * blocks)
        return (running + added, None)
    running = jnp.zeros((blocks * blocks, KB * KB), jnp.float32)
    running, unused = lax.scan(group_step, running, jnp.arange(N_GRP, dtype=jnp.int32))
    assembled = running.reshape(blocks, blocks, KB, KB).transpose(0, 2, 1, 3).reshape(NF, NF)
    front_full = base_front.astype(jnp.float32) + assembled
    factor = pivot_factor(front_full[:PANEL, :PANEL])
    lower_rows = lax.linalg.triangular_solve(factor, front_full[PANEL:, :PANEL], left_side=False, lower=True, transpose_a=True)
    panel_factor = jnp.concatenate([factor, lower_rows], axis=0).astype(jnp.bfloat16)
    update = jnp.dot(panel_factor.astype(jnp.float32), panel_factor.T.astype(jnp.float32), preferred_element_type=jnp.float32)
    indices = jnp.arange(NF)
    keep = (indices[:, None] >= indices[None, :]) & (indices[None, :] >= PANEL)
    trailing = jnp.where(keep, front_full - update, 0.0)
    return (trailing, panel_factor)
```

```python
import functools

import jax
import jax.numpy as jnp
from jax import lax
from jax.experimental import pallas as pl
from jax.experimental.pallas import tpu as pltpu
from jax.sharding import PartitionSpec as P

NT = (((1,), (1,)), ((), ()))
NN = (((1,), (0,)), ((), ()))
BF = jnp.bfloat16
F32 = jnp.float32


def dot32(a, b, dims):
    return lax.dot_general(a, b, dims, precision=lax.Precision.HIGHEST, preferred_element_type=F32)


def dotb(a, b, dims):
    return lax.dot_general(a, b, dims, preferred_element_type=F32)


def tile_kernel(
    slot_ref, basis_ref, link_next_ref, link_ref, diag_ref, before_y_ref, after_y_ref,
    before_x_ref, after_x_ref, stencil_ref, eye_ref, out_ref,
    scaled_t, basis_t, partial, stage, sems,
):
    step = pl.program_id(0)
    steps = pl.num_programs(0)
    here = lax.rem(step, 2)
    there = lax.rem(step + 1, 2)
    eye = eye_ref[...]
    gap = jnp.zeros((96, 128), BF)
    first = jnp.concatenate([gap, before_y_ref[0]], axis=0)
    last = jnp.concatenate([after_y_ref[0], gap], axis=0)
    scaled_t[here, :, 0:128] = dotb(eye, first, NT).astype(BF)
    scaled_t[here, :, 1152:1280] = dotb(eye, last, NT).astype(BF)

    @pl.when((step > 0) & (step < steps - 1))
    def _():
        turned = dotb(eye, basis_ref[0], NT)
        basis_t[here] = turned.astype(BF)
        scaled_t[here, :, 128:1152] = (turned * link_next_ref[0]).astype(BF)

    @pl.when(step == 0)
    def _():
        scaled_t[here, :, 128:1152] = dotb(eye, before_x_ref[...], NT).astype(BF)

    @pl.when(step == steps - 1)
    def _():
        scaled_t[here, :, 128:1152] = dotb(eye, after_x_ref[...], NT).astype(BF)

    ring = lax.rem(step, 3)
    for q in range(4):
        partial[ring, :, 256 * q:256 * q + 256] = dotb(
            scaled_t[here, :, 256 * q:256 * q + 512], stencil_ref[...], NN
        )

    def copy_out(buffer, q, slot):
        return pltpu.make_async_copy(stage.at[buffer, q], out_ref.at[slot], sems.at[buffer, q])

    @pl.when(step >= 2)
    def _():
        @pl.when(step >= 4)
        def _():
            for q in range(4):
                copy_out(here, q, 0).wait()

        for q in range(4):
            cells = slice(256 * q, 256 * q + 256)
            around = partial[0, :, cells] + partial[1, :, cells] + partial[2, :, cells]
            around = around - scaled_t[there, :, 128 + 256 * q:384 + 256 * q].astype(F32)
            own = basis_t[there, :, cells]
            image = diag_ref[0, :, cells] * own.astype(F32) - link_ref[0, :, cells] * around
            high = image.astype(BF)
            low = (image - high.astype(F32)).astype(BF)
            stage[here, q] = (dotb(own, high, NT) + dotb(own, low, NT)).astype(BF)
            copy_out(here, q, slot_ref[(step - 2) * 4 + q]).start()

    @pl.when(step == steps - 1)
    def _():
        for q in range(4):
            copy_out(there, q, 0).wait()
            copy_out(here, q, 0).wait()


def galerkin_tiles(slots, basis, link, diag, before_y, after_y, before_x, after_x):
    planes = basis.shape[0]
    k = jnp.arange(512)[:, None]
    n = jnp.arange(256)[None, :]
    stencil = (
        (jnp.abs(k // 32 - 4 - n // 32) <= 1) & (jnp.abs(k % 32 - n % 32) <= 1)
    ).astype(BF)
    eye = jnp.eye(128, dtype=BF)
    ahead = lambda t, s: (jnp.clip(t - 1, 0, planes - 1), 0, 0)
    done = lambda t, s: (jnp.clip(t - 2, 0, planes - 1), 0, 0)
    each = lambda t, s: (t, 0, 0)
    whole = lambda t, s: (0, 0)
    return pl.pallas_call(
        tile_kernel,
        out_shape=jax.ShapeDtypeStruct((256, 128, 128), BF),
        grid_spec=pltpu.PrefetchScalarGridSpec(
            num_scalar_prefetch=1,
            grid=(planes + 2,),
            in_specs=[
                pl.BlockSpec((1, 1024, 128), ahead),
                pl.BlockSpec((1, 1, 1024), ahead),
                pl.BlockSpec((1, 1, 1024), done),
                pl.BlockSpec((1, 1, 1024), done),
                pl.BlockSpec((1, 32, 128), each),
                pl.BlockSpec((1, 32, 128), each),
                pl.BlockSpec((1024, 128), whole),
                pl.BlockSpec((1024, 128), whole),
                pl.BlockSpec((512, 256), whole),
                pl.BlockSpec((128, 128), whole),
            ],
            out_specs=pl.BlockSpec(memory_space=pl.ANY),
            scratch_shapes=[
                pltpu.VMEM((2, 128, 1280), BF),
                pltpu.VMEM((2, 128, 1024), BF),
                pltpu.VMEM((3, 128, 1024), F32),
                pltpu.VMEM((2, 4, 128, 128), BF),
                pltpu.SemaphoreType.DMA((2, 4)),
            ],
        ),
        compiler_params=pltpu.CompilerParams(
            dimension_semantics=("arbitrary",), vmem_limit_bytes=32 * 2**20
        ),
        name="galerkin_tiles",
    )(slots, basis, link, link, diag, before_y, after_y, before_x, after_x, stencil, eye)


def factor_kernel(pivot_ref, factor_ref, inverse_ref, work, block):
    size = pivot_ref.shape[0]
    count = size // 128
    rows = lax.broadcasted_iota(jnp.int32, (128, 128), 0)
    lanes = lax.broadcasted_iota(jnp.int32, (128, 128), 1)
    row_ids = lax.broadcasted_iota(jnp.int32, (128, 1), 0)
    lane_ids = lax.broadcasted_iota(jnp.int32, (1, 128), 1)
    work[...] = pivot_ref[...]
    factor_ref[...] = jnp.zeros_like(factor_ref)
    inverse_ref[...] = jnp.zeros_like(inverse_ref)
    for b in range(count):
        own = slice(128 * b, 128 * b + 128)
        rest = slice(128 * b + 128, size)
        block[:, 0:128] = work[own, own]
        block[:, 128:256] = jnp.where(rows == lanes, 1.0, 0.0)

        def eliminate(j, carry):
            left = block[:, 0:128]
            right = block[:, 128:256]
            pivot_row = block[pl.ds(j, 1), :]
            pivot = jnp.sum(jnp.where(lane_ids == j, pivot_row[:, 0:128], 0.0), axis=1, keepdims=True)
            column = jnp.sum(jnp.where(lanes == j, left, 0.0), axis=1, keepdims=True)
            ratio = jnp.where(row_ids > j, column * (1.0 / pivot), 0.0)
            block[:, 0:128] = left - ratio * pivot_row[:, 0:128]
            block[:, 128:256] = right - ratio * pivot_row[:, 128:256]
            return carry

        lax.fori_loop(0, 128, eliminate, 0)
        upper = block[:, 0:128]
        pivots = jnp.sum(jnp.where(rows == lanes, upper, 0.0), axis=1, keepdims=True)
        scale = 1.0 / jnp.sqrt(pivots)
        upper = jnp.where(rows <= lanes, upper * scale, 0.0)
        inverse = jnp.where(rows >= lanes, block[:, 128:256] * scale, 0.0)
        factor_ref[own, own] = upper.T
        inverse_ref[own, own] = inverse
        if b + 1 < count:
            below = dot32(work[rest, own], inverse, NT)
            factor_ref[rest, own] = below
            work[rest, rest] = work[rest, rest] - dot32(below, below, NT)
    for b in range(1, count):
        own = slice(128 * b, 128 * b + 128)
        left = slice(0, 128 * b)
        product = dot32(factor_ref[own, left], inverse_ref[left, left], NN)
        inverse_ref[own, left] = -dot32(inverse_ref[own, own], product, NN)


def pivot_factor(pivot_matrix):
    size = pivot_matrix.shape[0]
    return pl.pallas_call(
        factor_kernel,
        out_shape=[jax.ShapeDtypeStruct((size, size), F32)] * 2,
        in_specs=[pl.BlockSpec(memory_space=pltpu.VMEM)],
        out_specs=[pl.BlockSpec(memory_space=pltpu.VMEM)] * 2,
        scratch_shapes=[pltpu.VMEM((size, size), F32), pltpu.VMEM((128, 256), F32)],
        compiler_params=pltpu.CompilerParams(vmem_limit_bytes=32 * 2**20),
        cost_estimate=pl.CostEstimate(flops=10**10, bytes_accessed=3 * 2**20, transcendentals=0),
        name="pivot_factor",
    )(pivot_matrix)


def final_kernel(place_ref, row_ref, col_ref, base_ref, received_ref, out_ref, sums):
    step = pl.program_id(0)
    group = lax.axis_index("grp")
    member = lax.axis_index("sub")
    row_start = group * 4096
    col_start = member * 512
    live = (member > 0) & (row_start + 4095 >= col_start)

    @pl.when(live & (step == 0))
    def _():
        sums[...] = jnp.zeros_like(sums)

        def add(slot, carry):
            place = place_ref[slot]

            @pl.when(place >= 0)
            def _():
                sums[place] = sums[place] + received_ref[slot].astype(F32)

            return carry

        lax.fori_loop(0, 256, add, 0)

    first_row = row_start + step * 512

    @pl.when(live & (first_row + 511 >= col_start))
    def _():
        update = dotb(row_ref[...], col_ref[...], NT)
        rows = first_row + lax.broadcasted_iota(jnp.int32, (128, 128), 0)
        cols = col_start + lax.broadcasted_iota(jnp.int32, (128, 128), 1)
        for i in range(4):
            for j in range(4):
                r = slice(128 * i, 128 * i + 128)
                c = slice(128 * j, 128 * j + 128)
                value = base_ref[r, c].astype(F32) + sums[(step * 4 + i) * 4 + j] - update[r, c]
                out_ref[r, c] = jnp.where(rows + 128 * i >= cols + 128 * j, value, 0.0)

    @pl.when(jnp.logical_not(live & (first_row + 511 >= col_start)))
    def _():
        out_ref[...] = jnp.zeros_like(out_ref)


def trailing_front(place, panel_rows, panel_cols, base, received):
    return pl.pallas_call(
        final_kernel,
        out_shape=jax.ShapeDtypeStruct((4096, 512), F32),
        grid_spec=pltpu.PrefetchScalarGridSpec(
            num_scalar_prefetch=1,
            grid=(8,),
            in_specs=[
                pl.BlockSpec((512, 512), lambda t, s: (t, 0)),
                pl.BlockSpec((512, 512), lambda t, s: (0, 0)),
                pl.BlockSpec((512, 512), lambda t, s: (t, 0)),
                pl.BlockSpec((256, 128, 128), lambda t, s: (0, 0, 0)),
            ],
            out_specs=pl.BlockSpec((512, 512), lambda t, s: (t, 0)),
            scratch_shapes=[pltpu.VMEM((128, 128, 128), F32)],
        ),
        compiler_params=pltpu.CompilerParams(
            dimension_semantics=("arbitrary",), vmem_limit_bytes=48 * 2**20
        ),
        name="trailing_front",
    )(place, panel_rows, panel_cols, base, received)


def shifted(x, axis, count, up):
    pairs = [(i, i + 1) if up else (i + 1, i) for i in range(count - 1)]
    return lax.ppermute(x, axis, pairs)


def arrivals(owner_ids, local_block, owner):
    order = jnp.arange(owner_ids.shape[1], dtype=jnp.int32)[None, :]
    here = owner_ids == owner
    first = jnp.min(jnp.where(here, order, 1 << 20), axis=1, keepdims=True)
    one = jnp.max(jnp.where(here & (order == first), local_block, -1), axis=1)
    two = jnp.max(jnp.where(here & (order > first), local_block, -1), axis=1)
    return jnp.stack([one, two], axis=1).reshape(-1)


def per_device(basis_cols, diag_weight, link_weight, base_front, block_lists):
    groups, members, devices = 4, 32, 128
    group = lax.axis_index("grp")
    member = lax.axis_index("sub")
    me = group * members + member

    lead = jnp.where(me == 0, base_front[:512], jnp.zeros((512, 512), BF))
    lead = lax.psum(lead, ("grp", "sub"))
    base_rows = lax.all_to_all(
        base_front.reshape(members, 128, 512), "sub", split_axis=0, concat_axis=0, tiled=True
    )[0]

    def scaled(b, w):
        return (w[..., None] * b.astype(F32)).astype(BF)

    before_x = shifted(scaled(basis_cols[31], link_weight[31]), "grp", groups, True)
    after_x = shifted(scaled(basis_cols[0], link_weight[0]), "grp", groups, False)
    high_y = scaled(basis_cols[:, 31], link_weight[:, 31])
    low_y = scaled(basis_cols[:, 0], link_weight[:, 0])
    high_y = jnp.concatenate([before_x[None, 31], high_y, after_x[None, 31]], axis=0)
    low_y = jnp.concatenate([before_x[None, 0], low_y, after_x[None, 0]], axis=0)
    before_y = shifted(high_y, "sub", members, True)
    after_y = shifted(low_y, "sub", members, False)

    listed = block_lists.reshape(devices, 128, 2)
    row_block = listed[:, :, 0]
    col_block = listed[:, :, 1]
    owner_ids = row_block // members * members + col_block // groups
    local_block = row_block % members * groups + col_block % groups
    own_owner = lax.dynamic_index_in_dim(owner_ids, me, 0, keepdims=False)
    order = jnp.arange(128)
    rank = jnp.sum(
        (own_owner[:, None] == own_owner[None, :]) & (order[None, :] < order[:, None]), axis=1
    )
    slots = (own_owner * 2 + rank).astype(jnp.int32)
    place = arrivals(owner_ids, local_block, me)
    panel_place = arrivals(owner_ids, local_block, group * members)

    outgoing = galerkin_tiles(
        slots,
        basis_cols.reshape(32, 1024, 128),
        link_weight.reshape(32, 1, 1024),
        diag_weight.reshape(32, 1, 1024),
        before_y,
        after_y,
        before_x.reshape(1024, 128),
        after_x.reshape(1024, 128),
    )

    strips = outgoing.reshape(groups, members, 2, 128, 128)[:, 0]
    strips = strips.reshape(groups, 2, members, 4, 128).transpose(0, 2, 1, 3, 4)
    strips = strips.reshape(devices, 2, 4, 128)
    strips = lax.all_to_all(strips, ("grp", "sub"), split_axis=0, concat_axis=0, tiled=True)
    strips, outgoing = lax.optimization_barrier((strips, outgoing))
    received = lax.all_to_all(
        outgoing.reshape(devices, 2, 128, 128), ("grp", "sub"), split_axis=0, concat_axis=0, tiled=True
    ).reshape(256, 128, 128)

    strips = jnp.where((panel_place >= 0)[:, None], strips.reshape(256, 512), 0)
    pick = (panel_place[None, :] == jnp.arange(128)[:, None]).astype(BF)
    strips = dotb(pick, strips, NN).reshape(members, groups, 4, 128)
    strips = strips.transpose(0, 2, 1, 3).reshape(members, 4, 512)
    strips = lax.all_to_all(strips, "sub", split_axis=0, concat_axis=0, tiled=True)
    front_rows = base_rows.astype(F32) + strips.reshape(128, 512)

    lead = lead.astype(F32)
    symmetric = jnp.tril(lead) + jnp.tril(lead, -1).T
    pivot_matrix = symmetric + jnp.diag(jnp.sum(jnp.abs(symmetric), axis=1) + 1.0)
    factor, inverse = pivot_factor(pivot_matrix)
    solved = dot32(front_rows, inverse, NT)
    in_lead = (group == 0) & (member < 4)
    own_factor = lax.dynamic_slice_in_dim(factor, 128 * jnp.minimum(member, 3), 128, 0)
    panel = jnp.where(in_lead, own_factor, solved).astype(BF)
    panel_rows = lax.all_gather(panel, "sub", axis=0, tiled=True)

    source = member // 8
    piece = lax.dynamic_slice_in_dim(panel_rows, member % 8 * 512, 512, 0)
    panel_cols = jnp.where(group == source, piece, jnp.zeros_like(piece))
    total = panel_cols
    for ahead in range(1, groups):
        pairs = [
            (s // 8 * members + s, (s // 8 + ahead) * members + s)
            for s in range(members)
            if s // 8 + ahead < groups
        ]
        total = total + lax.ppermute(panel_cols, ("grp", "sub"), pairs)
    trailing = trailing_front(place, panel_rows, total, base_front, received)
    return (trailing, panel)


def solution(mesh):
    return jax.shard_map(
        per_device,
        mesh=mesh,
        in_specs=(
            P("grp", "sub", None, None),
            P("grp", "sub", None),
            P("grp", "sub", None),
            P("grp", "sub"),
            P(),
        ),
        out_specs=(P("grp", "sub"), P(("grp", "sub"), None)),
        check_vma=False,
    )
```

```python
import functools

import jax
import jax.numpy as jnp
from jax import lax
from jax.experimental import pallas as pl
from jax.experimental.pallas import tpu as pltpu
from jax.sharding import PartitionSpec as P

NT = (((1,), (1,)), ((), ()))
NN = (((1,), (0,)), ((), ()))
BF = jnp.bfloat16
F32 = jnp.float32


def dot32(a, b, dims):
    return lax.dot_general(a, b, dims, precision=lax.Precision.HIGHEST, preferred_element_type=F32)


def dotb(a, b, dims):
    return lax.dot_general(a, b, dims, preferred_element_type=F32)


def tile_kernel(
    slot_ref, basis_ref, link_next_ref, link_ref, diag_ref, before_y_ref, after_y_ref,
    before_x_ref, after_x_ref, stencil_ref, eye_ref, out_ref,
    scaled_t, basis_t, partial, stage, sems,
):
    step = pl.program_id(0)
    steps = pl.num_programs(0)
    here = lax.rem(step, 2)
    there = lax.rem(step + 1, 2)
    eye = eye_ref[...]
    gap = jnp.zeros((96, 128), BF)
    first = jnp.concatenate([gap, before_y_ref[0]], axis=0)
    last = jnp.concatenate([after_y_ref[0], gap], axis=0)
    scaled_t[here, :, 0:128] = dotb(eye, first, NT).astype(BF)
    scaled_t[here, :, 1152:1280] = dotb(eye, last, NT).astype(BF)

    @pl.when((step > 0) & (step < steps - 1))
    def _():
        turned = dotb(eye, basis_ref[0], NT)
        basis_t[here] = turned.astype(BF)
        scaled_t[here, :, 128:1152] = (turned * link_next_ref[0]).astype(BF)

    @pl.when(step == 0)
    def _():
        scaled_t[here, :, 128:1152] = dotb(eye, before_x_ref[...], NT).astype(BF)

    @pl.when(step == steps - 1)
    def _():
        scaled_t[here, :, 128:1152] = dotb(eye, after_x_ref[...], NT).astype(BF)

    ring = lax.rem(step, 3)
    for q in range(4):
        partial[ring, :, 256 * q:256 * q + 256] = dotb(
            scaled_t[here, :, 256 * q:256 * q + 512], stencil_ref[...], NN
        )

    def copy_out(buffer, q, slot):
        return pltpu.make_async_copy(stage.at[buffer, q], out_ref.at[slot], sems.at[buffer, q])

    @pl.when(step >= 2)
    def _():
        @pl.when(step >= 4)
        def _():
            for q in range(4):
                copy_out(here, q, 0).wait()

        for q in range(4):
            cells = slice(256 * q, 256 * q + 256)
            around = partial[0, :, cells] + partial[1, :, cells] + partial[2, :, cells]
            around = around - scaled_t[there, :, 128 + 256 * q:384 + 256 * q].astype(F32)
            own = basis_t[there, :, cells]
            image = diag_ref[0, :, cells] * own.astype(F32) - link_ref[0, :, cells] * around
            high = image.astype(BF)
            low = (image - high.astype(F32)).astype(BF)
            stage[here, q] = (dotb(own, high, NT) + dotb(own, low, NT)).astype(BF)
            copy_out(here, q, slot_ref[(step - 2) * 4 + q]).start()

    @pl.when(step == steps - 1)
    def _():
        for q in range(4):
            copy_out(there, q, 0).wait()
            copy_out(here, q, 0).wait()


def galerkin_tiles(slots, basis, link, diag, before_y, after_y, before_x, after_x):
    planes = basis.shape[0]
    k = jnp.arange(512)[:, None]
    n = jnp.arange(256)[None, :]
    stencil = (
        (jnp.abs(k // 32 - 4 - n // 32) <= 1) & (jnp.abs(k % 32 - n % 32) <= 1)
    ).astype(BF)
    eye = jnp.eye(128, dtype=BF)
    ahead = lambda t, s: (jnp.clip(t - 1, 0, planes - 1), 0, 0)
    done = lambda t, s: (jnp.clip(t - 2, 0, planes - 1), 0, 0)
    each = lambda t, s: (t, 0, 0)
    whole = lambda t, s: (0, 0)
    return pl.pallas_call(
        tile_kernel,
        out_shape=jax.ShapeDtypeStruct((256, 128, 128), BF),
        grid_spec=pltpu.PrefetchScalarGridSpec(
            num_scalar_prefetch=1,
            grid=(planes + 2,),
            in_specs=[
                pl.BlockSpec((1, 1024, 128), ahead),
                pl.BlockSpec((1, 1, 1024), ahead),
                pl.BlockSpec((1, 1, 1024), done),
                pl.BlockSpec((1, 1, 1024), done),
                pl.BlockSpec((1, 32, 128), each),
                pl.BlockSpec((1, 32, 128), each),
                pl.BlockSpec((1024, 128), whole),
                pl.BlockSpec((1024, 128), whole),
                pl.BlockSpec((512, 256), whole),
                pl.BlockSpec((128, 128), whole),
            ],
            out_specs=pl.BlockSpec(memory_space=pl.ANY),
            scratch_shapes=[
                pltpu.VMEM((2, 128, 1280), BF),
                pltpu.VMEM((2, 128, 1024), BF),
                pltpu.VMEM((3, 128, 1024), F32),
                pltpu.VMEM((2, 4, 128, 128), BF),
                pltpu.SemaphoreType.DMA((2, 4)),
            ],
        ),
        compiler_params=pltpu.CompilerParams(
            dimension_semantics=("arbitrary",), vmem_limit_bytes=32 * 2**20
        ),
        name="galerkin_tiles",
    )(slots, basis, link, link, diag, before_y, after_y, before_x, after_x, stencil, eye)


def factor_kernel(pivot_ref, factor_ref, inverse_ref, work, block):
    size = pivot_ref.shape[0]
    count = size // 128
    rows = lax.broadcasted_iota(jnp.int32, (128, 128), 0)
    lanes = lax.broadcasted_iota(jnp.int32, (128, 128), 1)
    row_ids = lax.broadcasted_iota(jnp.int32, (128, 1), 0)
    lane_ids = lax.broadcasted_iota(jnp.int32, (1, 128), 1)
    work[...] = pivot_ref[...]
    factor_ref[...] = jnp.zeros_like(factor_ref)
    inverse_ref[...] = jnp.zeros_like(inverse_ref)
    for b in range(count):
        own = slice(128 * b, 128 * b + 128)
        rest = slice(128 * b + 128, size)
        block[:, 0:128] = work[own, own]
        block[:, 128:256] = jnp.where(rows == lanes, 1.0, 0.0)

        def eliminate(j, carry):
            left = block[:, 0:128]
            right = block[:, 128:256]
            pivot_row = block[pl.ds(j, 1), :]
            pivot = jnp.sum(jnp.where(lane_ids == j, pivot_row[:, 0:128], 0.0), axis=1, keepdims=True)
            column = jnp.sum(jnp.where(lanes == j, left, 0.0), axis=1, keepdims=True)
            ratio = jnp.where(row_ids > j, column * (1.0 / pivot), 0.0)
            block[:, 0:128] = left - ratio * pivot_row[:, 0:128]
            block[:, 128:256] = right - ratio * pivot_row[:, 128:256]
            return carry

        lax.fori_loop(0, 128, eliminate, 0)
        upper = block[:, 0:128]
        pivots = jnp.sum(jnp.where(rows == lanes, upper, 0.0), axis=1, keepdims=True)
        scale = 1.0 / jnp.sqrt(pivots)
        upper = jnp.where(rows <= lanes, upper * scale, 0.0)
        inverse = jnp.where(rows >= lanes, block[:, 128:256] * scale, 0.0)
        factor_ref[own, own] = upper.T
        inverse_ref[own, own] = inverse
        if b + 1 < count:
            below = dot32(work[rest, own], inverse, NT)
            factor_ref[rest, own] = below
            work[rest, rest] = work[rest, rest] - dot32(below, below, NT)
    for b in range(1, count):
        own = slice(128 * b, 128 * b + 128)
        left = slice(0, 128 * b)
        product = dot32(factor_ref[own, left], inverse_ref[left, left], NN)
        inverse_ref[own, left] = -dot32(inverse_ref[own, own], product, NN)


def pivot_factor(pivot_matrix):
    size = pivot_matrix.shape[0]
    return pl.pallas_call(
        factor_kernel,
        out_shape=[jax.ShapeDtypeStruct((size, size), F32)] * 2,
        in_specs=[pl.BlockSpec(memory_space=pltpu.VMEM)],
        out_specs=[pl.BlockSpec(memory_space=pltpu.VMEM)] * 2,
        scratch_shapes=[pltpu.VMEM((size, size), F32), pltpu.VMEM((128, 256), F32)],
        compiler_params=pltpu.CompilerParams(vmem_limit_bytes=32 * 2**20),
        cost_estimate=pl.CostEstimate(flops=10**10, bytes_accessed=3 * 2**20, transcendentals=0),
        name="pivot_factor",
    )(pivot_matrix)


def final_kernel(place_ref, row_ref, col_ref, base_ref, received_ref, out_ref, sums):
    step = pl.program_id(0)
    group = lax.axis_index("grp")
    member = lax.axis_index("sub")
    row_start = group * 4096
    col_start = member * 512
    live = (member > 0) & (row_start + 4095 >= col_start)

    @pl.when(live & (step == 0))
    def _():
        sums[...] = jnp.zeros_like(sums)

        def add(slot, carry):
            place = place_ref[slot]

            @pl.when(place >= 0)
            def _():
                sums[place] = sums[place] + received_ref[slot].astype(F32)

            return carry

        lax.fori_loop(0, 256, add, 0)

    first_row = row_start + step * 512

    @pl.when(live & (first_row + 511 >= col_start))
    def _():
        update = dotb(row_ref[...], col_ref[...], NT)
        rows = first_row + lax.broadcasted_iota(jnp.int32, (128, 128), 0)
        cols = col_start + lax.broadcasted_iota(jnp.int32, (128, 128), 1)
        for i in range(4):
            for j in range(4):
                r = slice(128 * i, 128 * i + 128)
                c = slice(128 * j, 128 * j + 128)
                value = base_ref[r, c].astype(F32) + sums[(step * 4 + i) * 4 + j] - update[r, c]
                out_ref[r, c] = jnp.where(rows + 128 * i >= cols + 128 * j, value, 0.0)

    @pl.when(jnp.logical_not(live & (first_row + 511 >= col_start)))
    def _():
        out_ref[...] = jnp.zeros_like(out_ref)


def trailing_front(place, panel_rows, panel_cols, base, received):
    return pl.pallas_call(
        final_kernel,
        out_shape=jax.ShapeDtypeStruct((4096, 512), F32),
        grid_spec=pltpu.PrefetchScalarGridSpec(
            num_scalar_prefetch=1,
            grid=(8,),
            in_specs=[
                pl.BlockSpec((512, 512), lambda t, s: (t, 0)),
                pl.BlockSpec((512, 512), lambda t, s: (0, 0)),
                pl.BlockSpec((512, 512), lambda t, s: (t, 0)),
                pl.BlockSpec((256, 128, 128), lambda t, s: (0, 0, 0)),
            ],
            out_specs=pl.BlockSpec((512, 512), lambda t, s: (t, 0)),
            scratch_shapes=[pltpu.VMEM((128, 128, 128), F32)],
        ),
        compiler_params=pltpu.CompilerParams(
            dimension_semantics=("arbitrary",), vmem_limit_bytes=48 * 2**20
        ),
        name="trailing_front",
    )(place, panel_rows, panel_cols, base, received)


def at(group, member):
    return {"grp": group, "sub": member}


def opening_kernel(
    high_x, low_x, high_y, low_y, base_ref,
    before_x, after_x, before_y, after_y, lead_ref, rows_ref,
    halo_send, halo_recv, lead_send, lead_recv, base_send, base_recv, own_sem,
):
    groups, members = 4, 32
    group = lax.axis_index("grp")
    member = lax.axis_index("sub")
    barrier = pltpu.get_barrier_semaphore()
    sides = [(dg, ds) for dg in (-1, 0, 1) for ds in (-1, 0, 1) if (dg, ds) != (0, 0)]

    def exists(dg, ds):
        g, s = group + dg, member + ds
        return (g >= 0) & (g < groups) & (s >= 0) & (s < members)

    def greet(d, carry):
        pl.semaphore_signal(barrier, 1, device_id=at(group, lax.rem(member + d, members)))
        return carry

    lax.fori_loop(1, members, greet, 0)
    for d in range(1, groups):
        pl.semaphore_signal(barrier, 1, device_id=at(lax.rem(group + d, groups), member))
    for dg, ds in sides:
        if dg and ds:
            @pl.when(exists(dg, ds))
            def _():
                pl.semaphore_signal(barrier, 1, device_id=at(group + dg, member + ds))

    near_groups = 2 - jnp.where(group == 0, 1, 0) - jnp.where(group == groups - 1, 1, 0)
    near_members = 2 - jnp.where(member == 0, 1, 0) - jnp.where(member == members - 1, 1, 0)
    pl.semaphore_wait(barrier, members - 1 + groups - 1 + near_groups * near_members)

    def piece(m):
        return pl.ds(pl.multiple_of(16 * m, 16), 16)

    def lead_copy(source, m, k, g, s):
        return pltpu.make_async_remote_copy(
            source.at[piece(m)], lead_ref.at[piece(m)], lead_send.at[k], lead_recv.at[m],
            device_id=at(g, s),
        )

    def base_copy(m):
        rows = pl.ds(pl.multiple_of(128 * m, 128), 128)
        return pltpu.make_async_remote_copy(
            base_ref.at[rows], rows_ref, base_send.at[m], base_recv, device_id=at(group, m)
        )

    own_lead = pltpu.make_async_copy(base_ref.at[pl.ds(0, 16)], lead_ref.at[pl.ds(0, 16)], own_sem.at[0])
    own_rows = pltpu.make_async_copy(base_ref.at[pl.ds(0, 128)], rows_ref, own_sem.at[1])
    root = (group == 0) & (member == 0)

    @pl.when(root)
    def _():
        own_lead.start()

        def send(m, carry):
            lead_copy(base_ref, m, m, 0, m).start()
            return carry

        lax.fori_loop(1, members, send, 0)

    def halo(dg, ds):
        k = sides.index((dg, ds))
        if ds == 0:
            source, target = (high_x, before_x) if dg == 1 else (low_x, after_x)
        else:
            if dg == 0:
                source = high_y if ds == 1 else low_y
                place = pl.ds(32, 1024)
            else:
                face = high_x if dg == 1 else low_x
                source = face.at[pl.ds(992 if ds == 1 else 0, 32)]
                place = pl.ds(0 if dg == 1 else 1056, 32)
            target = (before_y if ds == 1 else after_y).at[place]
        return pltpu.make_async_remote_copy(
            source, target, halo_send.at[k], halo_recv.at[k], device_id=at(group + dg, member + ds)
        )

    for dg, ds in sides:
        @pl.when(exists(dg, ds))
        def _():
            halo(dg, ds).start()

        @pl.when(jnp.logical_not(exists(-dg, -ds)))
        def _():
            if ds == 0:
                target = before_x if dg == 1 else after_x
                target[...] = jnp.zeros_like(target)
            else:
                target = before_y if ds == 1 else after_y
                place = pl.ds(32, 1024) if dg == 0 else pl.ds(0 if dg == 1 else 1056, 32)
                target[place, :] = jnp.zeros((1024 if dg == 0 else 32, 128), BF)

    @pl.when(member == 0)
    def _():
        own_rows.start()

        def send(m, carry):
            base_copy(m).start()
            return carry

        lax.fori_loop(1, members, send, 0)

    @pl.when(root)
    def _():
        own_lead.wait()

    @pl.when(jnp.logical_not(root))
    def _():
        lead_copy(lead_ref, member, 0, group, member).wait_recv()

    @pl.when(group == 0)
    def _():
        for g in range(1, groups):
            lead_copy(lead_ref, member, 64 + g, g, member).start()

    def spread(d, carry):
        lead_copy(lead_ref, member, 32 + d, group, lax.rem(member + d, members)).start()
        return carry

    lax.fori_loop(1, members, spread, 0)

    for dg, ds in sides:
        @pl.when(exists(-dg, -ds))
        def _():
            halo(dg, ds).wait_recv()

        @pl.when(exists(dg, ds))
        def _():
            halo(dg, ds).wait_send()

    def gather(d, carry):
        lead_copy(lead_ref, lax.rem(member + d, members), 0, group, member).wait_recv()
        lead_copy(lead_ref, member, 32 + d, group, member).wait_send()
        return carry

    lax.fori_loop(1, members, gather, 0)

    @pl.when(group == 0)
    def _():
        for g in range(1, groups):
            lead_copy(lead_ref, member, 64 + g, g, member).wait_send()

    @pl.when(root)
    def _():
        def sent(m, carry):
            lead_copy(base_ref, m, m, 0, m).wait_send()
            return carry

        lax.fori_loop(1, members, sent, 0)

    @pl.when(member == 0)
    def _():
        def sent(m, carry):
            base_copy(m).wait_send()
            return carry

        lax.fori_loop(1, members, sent, 0)
        own_rows.wait()

    @pl.when(member > 0)
    def _():
        base_copy(member).wait_recv()


def opening(high_x, low_x, high_y, low_y, base_front):
    vmem = pl.BlockSpec(memory_space=pltpu.VMEM)
    dma = pltpu.SemaphoreType.DMA
    return pl.pallas_call(
        opening_kernel,
        out_shape=[
            jax.ShapeDtypeStruct((1024, 128), BF),
            jax.ShapeDtypeStruct((1024, 128), BF),
            jax.ShapeDtypeStruct((1088, 128), BF),
            jax.ShapeDtypeStruct((1088, 128), BF),
            jax.ShapeDtypeStruct((512, 512), BF),
            jax.ShapeDtypeStruct((128, 512), BF),
        ],
        in_specs=[vmem] * 4 + [pl.BlockSpec(memory_space=pl.ANY)],
        out_specs=[vmem] * 6,
        scratch_shapes=[
            dma((8,)), dma((8,)), dma((68,)), dma((32,)), dma((32,)), dma, dma((2,)),
        ],
        compiler_params=pltpu.CompilerParams(
            collective_id=0, has_side_effects=True, vmem_limit_bytes=16 * 2**20
        ),
        name="opening",
    )(high_x, low_x, high_y, low_y, base_front)


def panel_kernel(
    panel_ref, rows_ref, cols_ref, send, recv, fold_send, fold_recv, col_send, col_recv, own_sem
):
    groups, members, chips = 4, 32, 16
    group = lax.axis_index("grp")
    member = lax.axis_index("sub")
    chip = member // 2
    core = lax.rem(member, 2)
    live = member // 8 <= group
    source_group = member // 8
    barrier = pltpu.get_barrier_semaphore()

    def greet(d, carry):
        pl.semaphore_signal(barrier, 1, device_id=at(group, lax.rem(member + d, members)))
        return carry

    lax.fori_loop(1, members, greet, 0)

    @pl.when(source_group < group)
    def _():
        for i in range(4):
            pl.semaphore_signal(
                barrier, 1, device_id=at(source_group, lax.rem(member, 8) * 4 + i)
            )

    pl.semaphore_wait(barrier, members - 1 + groups - 1 - group)

    def block(m):
        return pl.ds(pl.multiple_of(128 * m, 128), 128)

    def row_copy(m, k, s):
        return pltpu.make_async_remote_copy(
            panel_ref, rows_ref.at[block(m)], send.at[k], recv.at[m // 2], device_id=at(group, s)
        )

    def fold_copy(m, source):
        return pltpu.make_async_remote_copy(
            source, rows_ref.at[block(m)], fold_send.at[m // 2], fold_recv.at[m // 2],
            device_id=at(group, chip * 2 + 1 - core),
        )

    def other(d):
        return lax.rem(chip + d, chips) * 2 + core

    target = group * 8 + member // 4
    quarter = lax.rem(member, 4)

    def col_copy(g, q, s):
        return pltpu.make_async_remote_copy(
            panel_ref, cols_ref.at[block(q)], col_send.at[g], col_recv.at[q], device_id=at(g, s)
        )

    def spread(d, carry):
        @pl.when(other(d) // 8 <= group)
        def _():
            row_copy(member, d, other(d)).start()

        return carry

    lax.fori_loop(1, chips, spread, 0)

    for g in range(groups):
        @pl.when((g >= group) & jnp.logical_not((g == group) & (target == member)))
        def _():
            col_copy(g, quarter, target).start()

    own_cols = pltpu.make_async_copy(panel_ref, cols_ref.at[block(quarter)], own_sem.at[0])
    own_rows = pltpu.make_async_copy(panel_ref, rows_ref.at[block(member)], own_sem.at[1])

    @pl.when(target == member)
    def _():
        own_cols.start()

    own_rows.start()

    @pl.when(live)
    def _():
        fold_copy(member, panel_ref).start()

        def fold(d, carry):
            m = other(d)
            row_copy(m, 0, member).wait_recv()
            fold_copy(m, rows_ref.at[block(m)]).start()
            return carry

        lax.fori_loop(1, chips, fold, 0)

        def folded(d, carry):
            m = lax.rem(chip + d, chips) * 2
            fold_copy(m + 1 - core, panel_ref).wait_recv()
            fold_copy(m + core, panel_ref).wait_send()
            return carry

        lax.fori_loop(0, chips, folded, 0)

    def sent(d, carry):
        @pl.when(other(d) // 8 <= group)
        def _():
            row_copy(member, d, other(d)).wait_send()

        return carry

    lax.fori_loop(1, chips, sent, 0)
    for g in range(groups):
        @pl.when((g >= group) & jnp.logical_not((g == group) & (target == member)))
        def _():
            col_copy(g, quarter, target).wait_send()

    for i in range(4):
        source = lax.rem(member, 8) * 4 + i
        itself = (source_group == group) & (source == member)

        @pl.when((source_group <= group) & jnp.logical_not(itself))
        def _():
            col_copy(group, i, member).wait_recv()

    @pl.when(target == member)
    def _():
        own_cols.wait()

    own_rows.wait()


def panel_spread(panel):
    dma = pltpu.SemaphoreType.DMA
    anywhere = pl.BlockSpec(memory_space=pl.ANY)
    return pl.pallas_call(
        panel_kernel,
        out_shape=[jax.ShapeDtypeStruct((4096, 512), BF), jax.ShapeDtypeStruct((512, 512), BF)],
        in_specs=[pl.BlockSpec(memory_space=pltpu.VMEM)],
        out_specs=[anywhere, anywhere],
        scratch_shapes=[
            dma((16,)), dma((16,)), dma((16,)), dma((16,)), dma((4,)), dma((4,)), dma((2,)),
        ],
        compiler_params=pltpu.CompilerParams(
            collective_id=1, has_side_effects=True, vmem_limit_bytes=16 * 2**20
        ),
        name="panel_spread",
    )(panel)


def arrivals(owner_ids, local_block, owner):
    order = jnp.arange(owner_ids.shape[1], dtype=jnp.int32)[None, :]
    here = owner_ids == owner
    first = jnp.min(jnp.where(here, order, 1 << 20), axis=1, keepdims=True)
    one = jnp.max(jnp.where(here & (order == first), local_block, -1), axis=1)
    two = jnp.max(jnp.where(here & (order > first), local_block, -1), axis=1)
    return jnp.stack([one, two], axis=1).reshape(-1)


def per_device(basis_cols, diag_weight, link_weight, base_front, block_lists):
    groups, members, devices = 4, 32, 128
    group = lax.axis_index("grp")
    member = lax.axis_index("sub")
    me = group * members + member

    def scaled(b, w):
        return (w[..., None] * b.astype(F32)).astype(BF).reshape(1024, 128)

    before_x, after_x, before_y, after_y, lead, base_rows = opening(
        scaled(basis_cols[31], link_weight[31]),
        scaled(basis_cols[0], link_weight[0]),
        scaled(basis_cols[:, 31], link_weight[:, 31]),
        scaled(basis_cols[:, 0], link_weight[:, 0]),
        base_front,
    )

    listed = block_lists.reshape(devices, 128, 2)
    row_block = listed[:, :, 0]
    col_block = listed[:, :, 1]
    owner_ids = row_block // members * members + col_block // groups
    local_block = row_block % members * groups + col_block % groups
    own_owner = lax.dynamic_index_in_dim(owner_ids, me, 0, keepdims=False)
    order = jnp.arange(128)
    rank = jnp.sum(
        (own_owner[:, None] == own_owner[None, :]) & (order[None, :] < order[:, None]), axis=1
    )
    slots = (own_owner * 2 + rank).astype(jnp.int32)
    place = arrivals(owner_ids, local_block, me)
    panel_place = arrivals(owner_ids, local_block, group * members)

    outgoing = galerkin_tiles(
        slots,
        basis_cols.reshape(32, 1024, 128),
        link_weight.reshape(32, 1, 1024),
        diag_weight.reshape(32, 1, 1024),
        before_y.reshape(34, 32, 128),
        after_y.reshape(34, 32, 128),
        before_x,
        after_x,
    )

    outgoing, lead = lax.optimization_barrier((outgoing, lead))
    strips = outgoing.reshape(groups, members, 2, 128, 128)[:, 0]
    strips = strips.reshape(groups, 2, members, 4, 128).transpose(0, 2, 1, 3, 4)
    strips = strips.reshape(devices, 2, 4, 128)
    strips = lax.all_to_all(strips, ("grp", "sub"), split_axis=0, concat_axis=0, tiled=True)
    received = lax.all_to_all(
        outgoing.reshape(devices, 2, 128, 128), ("grp", "sub"), split_axis=0, concat_axis=0, tiled=True
    ).reshape(256, 128, 128)

    strips = jnp.where((panel_place >= 0)[:, None], strips.reshape(256, 512), 0)
    pick = (panel_place[None, :] == jnp.arange(128)[:, None]).astype(BF)
    strips = dotb(pick, strips, NN).reshape(members, groups, 4, 128)
    strips = strips.transpose(0, 2, 1, 3).reshape(members, 4, 512)
    strips = lax.all_to_all(strips, "sub", split_axis=0, concat_axis=0, tiled=True)
    front_rows = base_rows.astype(F32) + strips.reshape(128, 512)

    lead = lead.astype(F32)
    symmetric = jnp.tril(lead) + jnp.tril(lead, -1).T
    pivot_matrix = symmetric + jnp.diag(jnp.sum(jnp.abs(symmetric), axis=1) + 1.0)
    factor, inverse = pivot_factor(pivot_matrix)
    solved = dot32(front_rows, inverse, NT)
    in_lead = (group == 0) & (member < 4)
    own_factor = lax.dynamic_slice_in_dim(factor, 128 * jnp.minimum(member, 3), 128, 0)
    panel = jnp.where(in_lead, own_factor, solved).astype(BF)
    panel_rows, panel_cols = panel_spread(panel)
    trailing = trailing_front(place, panel_rows, panel_cols, base_front, received)
    return (trailing, panel)


def solution(mesh):
    return jax.shard_map(
        per_device,
        mesh=mesh,
        in_specs=(
            P("grp", "sub", None, None),
            P("grp", "sub", None),
            P("grp", "sub", None),
            P("grp", "sub"),
            P(),
        ),
        out_specs=(P("grp", "sub"), P(("grp", "sub"), None)),
        check_vma=False,
    )
```

```python
import functools

import jax
import jax.numpy as jnp
from jax import lax
from jax.experimental import pallas as pl
from jax.experimental.pallas import tpu as pltpu
from jax.sharding import PartitionSpec as P

NT = (((1,), (1,)), ((), ()))
NN = (((1,), (0,)), ((), ()))
BF = jnp.bfloat16
F32 = jnp.float32


def dot32(a, b, dims):
    return lax.dot_general(a, b, dims, precision=lax.Precision.HIGHEST, preferred_element_type=F32)


def dotb(a, b, dims):
    return lax.dot_general(a, b, dims, preferred_element_type=F32)


def tile_kernel(
    slot_ref, basis_ref, link_ref, diag_ref, before_y_ref, after_y_ref,
    before_x_ref, after_x_ref, stencil_ref, out_ref,
    scaled_t, basis_t, partial, stage, sems,
):
    step = pl.program_id(0)
    gap = jnp.zeros((96, 128), BF)

    def sides(slot, plane):
        first = jnp.concatenate([gap, before_y_ref[plane + 1]], axis=0)
        last = jnp.concatenate([after_y_ref[plane + 1], gap], axis=0)
        scaled_t[slot, :, 0:128] = first.T
        scaled_t[slot, :, 1152:1280] = last.T

    def spread(slot, ring):
        windows = [scaled_t[slot, :, 256 * q:256 * q + 512] for q in range(4)]
        sums = dotb(jnp.concatenate(windows, axis=0), stencil_ref[...], NN)
        for q in range(4):
            partial[ring, :, 256 * q:256 * q + 256] = sums[128 * q:128 * q + 128]

    def copy_out(slot, q, target):
        return pltpu.make_async_copy(stage.at[slot, q], out_ref.at[target], sems.at[slot, q])

    def wait(slot):
        for q in range(4):
            copy_out(slot, q, 0).wait()

    def start(slot, plane):
        for q in range(4):
            copy_out(slot, q, slot_ref[plane * 4 + q]).start()

    def finish(plane, slot, low, mid, high):
        link = link_ref[plane]
        diag = diag_ref[plane]
        for q in range(4):
            cells = slice(256 * q, 256 * q + 256)
            around = partial[low, :, cells] + partial[mid, :, cells] + partial[high, :, cells]
            around = around - scaled_t[slot, :, 128 + 256 * q:384 + 256 * q].astype(F32)
            own = basis_t[slot, :, cells]
            image = diag[:, cells] * own.astype(F32) - link[:, cells] * around
            head = image.astype(BF)
            tail = (image - head.astype(F32)).astype(BF)
            stage[slot, q] = (dotb(own, head, NT) + dotb(own, tail, NT)).astype(BF)

    @pl.when(step == 0)
    def _():
        sides(1, -1)
        scaled_t[1, :, 128:1152] = before_x_ref[...].T
        spread(1, 3)

    for u in range(4):
        plane = step * 4 + u
        slot = u % 2
        turned = basis_ref[u].T
        basis_t[slot] = turned
        scaled_t[slot, :, 128:1152] = (turned.astype(F32) * link_ref[plane]).astype(BF)
        sides(slot, plane)
        spread(slot, u)
        if u < 3:
            pl.when(step > 0)(functools.partial(wait, 1 - slot))
        else:
            wait(1 - slot)
        finish(jnp.maximum(plane - 1, 0), 1 - slot, (u + 2) % 4, (u + 3) % 4, u)
        if u == 0:
            pl.when(step > 0)(functools.partial(start, 1 - slot, plane - 1))
        else:
            start(1 - slot, plane - 1)

    @pl.when(step == pl.num_programs(0) - 1)
    def _():
        sides(0, 32)
        scaled_t[0, :, 128:1152] = after_x_ref[...].T
        spread(0, 0)
        wait(1)
        finish(31, 1, 2, 3, 0)
        start(1, 31)
        wait(0)
        wait(1)


def galerkin_tiles(slots, basis, link, diag, before_y, after_y, before_x, after_x):
    k = jnp.arange(512)[:, None]
    n = jnp.arange(256)[None, :]
    stencil = (
        (jnp.abs(k // 32 - 4 - n // 32) <= 1) & (jnp.abs(k % 32 - n % 32) <= 1)
    ).astype(BF)
    cube = lambda t, s: (0, 0, 0)
    flat = lambda t, s: (0, 0)
    return pl.pallas_call(
        tile_kernel,
        out_shape=jax.ShapeDtypeStruct((256, 128, 128), BF),
        grid_spec=pltpu.PrefetchScalarGridSpec(
            num_scalar_prefetch=1,
            grid=(8,),
            in_specs=[
                pl.BlockSpec((4, 1024, 128), lambda t, s: (t, 0, 0)),
                pl.BlockSpec((32, 1, 1024), cube),
                pl.BlockSpec((32, 1, 1024), cube),
                pl.BlockSpec((34, 32, 128), cube),
                pl.BlockSpec((34, 32, 128), cube),
                pl.BlockSpec((1024, 128), flat),
                pl.BlockSpec((1024, 128), flat),
                pl.BlockSpec((512, 256), flat),
            ],
            out_specs=pl.BlockSpec(memory_space=pl.ANY),
            scratch_shapes=[
                pltpu.VMEM((2, 128, 1280), BF),
                pltpu.VMEM((2, 128, 1024), BF),
                pltpu.VMEM((4, 128, 1024), F32),
                pltpu.VMEM((2, 4, 128, 128), BF),
                pltpu.SemaphoreType.DMA((2, 4)),
            ],
        ),
        compiler_params=pltpu.CompilerParams(
            dimension_semantics=("arbitrary",), vmem_limit_bytes=60 * 2**20
        ),
        name="galerkin_tiles",
    )(slots, basis, link, diag, before_y, after_y, before_x, after_x, stencil)


def factor_kernel(pivot_ref, factor_ref, inverse_ref, work):
    size = pivot_ref.shape[0]
    count = size // 128
    rows = lax.broadcasted_iota(jnp.int32, (128, 128), 0)
    lanes = lax.broadcasted_iota(jnp.int32, (128, 128), 1)
    sub8 = lax.broadcasted_iota(jnp.int32, (8, 128), 0)
    lane8 = lax.broadcasted_iota(jnp.int32, (8, 128), 1)
    all_rows = lax.broadcasted_iota(jnp.int32, (size, 1), 0)
    work[...] = pivot_ref[...]
    factor_ref[...] = jnp.zeros_like(factor_ref)
    inverse_ref[...] = jnp.zeros_like(inverse_ref)

    def one_block(b, carry):
        own = pl.ds(pl.multiple_of(128 * b, 128), 128)
        block = work[own, own]
        parts = [block[8 * i:8 * i + 8] for i in range(16)]
        for panel in range(16):
            cols = []
            for k in range(8):
                lane = slice(8 * panel + k, 8 * panel + k + 1)
                cols.append([jnp.broadcast_to(parts[i][:, lane], (8, 128)) for i in range(panel, 16)])
            for k in range(8):
                lane = 8 * panel + k
                pivot_row = jnp.broadcast_to(parts[panel][k:k + 1], (8, 128))
                pivot_row = jnp.where(lane8 == lane, 1.0, pivot_row)
                inverse = 1.0 / jnp.broadcast_to(cols[k][0][k:k + 1], (8, 128))
                heads = [None] * 8
                for l in range(k + 1, 8):
                    heads[l] = jnp.broadcast_to(cols[l][0][k:k + 1], (8, 128))
                for i in range(panel, 16):
                    ratio = cols[k][i - panel] * inverse
                    clear = lane8 == lane
                    if i == panel:
                        ratio = jnp.where(sub8 > k, ratio, 0.0)
                        clear = clear & (sub8 > k)
                    for l in range(k + 1, 8):
                        cols[l][i - panel] = cols[l][i - panel] - ratio * heads[l]
                    parts[i] = jnp.where(clear, 0.0, parts[i]) - ratio * pivot_row
        full = jnp.concatenate(parts, axis=0)
        pivots = jnp.sum(jnp.where(rows == lanes, full, 0.0), axis=1, keepdims=True)
        scale = 1.0 / jnp.sqrt(pivots)
        upper = jnp.where(rows <= lanes, full * scale, 0.0)
        inv = jnp.where(rows > lanes, full * scale, jnp.where(rows == lanes, scale, 0.0))
        below = dot32(work[:, own], inv, NT)
        below = jnp.where(all_rows >= 128 * b + 128, below, 0.0)
        factor_ref[:, own] = below
        factor_ref[own, own] = upper.T
        inverse_ref[own, own] = inv
        work[...] = work[...] - dot32(below, below, NT)
        return carry

    lax.fori_loop(0, count, one_block, 0)
    for b in range(1, count):
        own = slice(128 * b, 128 * b + 128)
        left = slice(0, 128 * b)
        product = dot32(factor_ref[own, left], inverse_ref[left, left], NN)
        inverse_ref[own, left] = -dot32(inverse_ref[own, own], product, NN)


def pivot_factor(pivot_matrix):
    size = pivot_matrix.shape[0]
    return pl.pallas_call(
        factor_kernel,
        out_shape=[jax.ShapeDtypeStruct((size, size), F32)] * 2,
        in_specs=[pl.BlockSpec(memory_space=pltpu.VMEM)],
        out_specs=[pl.BlockSpec(memory_space=pltpu.VMEM)] * 2,
        scratch_shapes=[pltpu.VMEM((size, size), F32)],
        compiler_params=pltpu.CompilerParams(vmem_limit_bytes=32 * 2**20),
        cost_estimate=pl.CostEstimate(flops=10**10, bytes_accessed=3 * 2**20, transcendentals=0),
        name="pivot_factor",
    )(pivot_matrix)


def final_kernel(place_ref, row_ref, col_ref, base_ref, received_ref, out_ref, sums):
    step = pl.program_id(0)
    group = lax.axis_index("grp")
    member = lax.axis_index("sub")
    row_start = group * 4096
    col_start = member * 512
    live = (member > 0) & (row_start + 4095 >= col_start)

    @pl.when(live & (step == 0))
    def _():
        sums[...] = jnp.zeros_like(sums)

        def add(slot, carry):
            place = place_ref[slot]

            @pl.when(place >= 0)
            def _():
                sums[place] = sums[place] + received_ref[slot].astype(F32)

            return carry

        lax.fori_loop(0, 256, add, 0)

    first_row = row_start + step * 512

    @pl.when(live & (first_row + 511 >= col_start))
    def _():
        update = dotb(row_ref[...], col_ref[...], NT)
        rows = first_row + lax.broadcasted_iota(jnp.int32, (128, 128), 0)
        cols = col_start + lax.broadcasted_iota(jnp.int32, (128, 128), 1)
        for i in range(4):
            for j in range(4):
                r = slice(128 * i, 128 * i + 128)
                c = slice(128 * j, 128 * j + 128)
                value = base_ref[r, c].astype(F32) + sums[(step * 4 + i) * 4 + j] - update[r, c]
                out_ref[r, c] = jnp.where(rows + 128 * i >= cols + 128 * j, value, 0.0)

    @pl.when(jnp.logical_not(live & (first_row + 511 >= col_start)))
    def _():
        out_ref[...] = jnp.zeros_like(out_ref)


def trailing_front(place, panel_rows, panel_cols, base, received):
    return pl.pallas_call(
        final_kernel,
        out_shape=jax.ShapeDtypeStruct((4096, 512), F32),
        grid_spec=pltpu.PrefetchScalarGridSpec(
            num_scalar_prefetch=1,
            grid=(8,),
            in_specs=[
                pl.BlockSpec((512, 512), lambda t, s: (t, 0)),
                pl.BlockSpec((512, 512), lambda t, s: (0, 0)),
                pl.BlockSpec((512, 512), lambda t, s: (t, 0)),
                pl.BlockSpec((256, 128, 128), lambda t, s: (0, 0, 0)),
            ],
            out_specs=pl.BlockSpec((512, 512), lambda t, s: (t, 0)),
            scratch_shapes=[pltpu.VMEM((128, 128, 128), F32)],
        ),
        compiler_params=pltpu.CompilerParams(
            dimension_semantics=("arbitrary",), vmem_limit_bytes=60 * 2**20
        ),
        name="trailing_front",
    )(place, panel_rows, panel_cols, base, received)


def at(group, member):
    return {"grp": group, "sub": member}


def opening_kernel(
    high_x, low_x, high_y, low_y, base_ref,
    before_x, after_x, before_y, after_y, lead_ref, rows_ref,
    halo_send, halo_recv, lead_send, lead_recv, base_send, base_recv, own_sem,
):
    groups, members = 4, 32
    group = lax.axis_index("grp")
    member = lax.axis_index("sub")
    barrier = pltpu.get_barrier_semaphore()
    sides = [(dg, ds) for dg in (-1, 0, 1) for ds in (-1, 0, 1) if (dg, ds) != (0, 0)]

    def exists(dg, ds):
        g, s = group + dg, member + ds
        return (g >= 0) & (g < groups) & (s >= 0) & (s < members)

    def greet(d, carry):
        pl.semaphore_signal(barrier, 1, device_id=at(group, lax.rem(member + d, members)))
        return carry

    lax.fori_loop(1, members, greet, 0)
    for d in range(1, groups):
        pl.semaphore_signal(barrier, 1, device_id=at(lax.rem(group + d, groups), member))
    for dg, ds in sides:
        if dg and ds:
            @pl.when(exists(dg, ds))
            def _():
                pl.semaphore_signal(barrier, 1, device_id=at(group + dg, member + ds))

    near_groups = 2 - jnp.where(group == 0, 1, 0) - jnp.where(group == groups - 1, 1, 0)
    near_members = 2 - jnp.where(member == 0, 1, 0) - jnp.where(member == members - 1, 1, 0)
    pl.semaphore_wait(barrier, members - 1 + groups - 1 + near_groups * near_members)

    def piece(m):
        return pl.ds(pl.multiple_of(16 * m, 16), 16)

    def lead_copy(source, m, k, g, s):
        return pltpu.make_async_remote_copy(
            source.at[piece(m)], lead_ref.at[piece(m)], lead_send.at[k], lead_recv.at[m],
            device_id=at(g, s),
        )

    def base_copy(m):
        rows = pl.ds(pl.multiple_of(128 * m, 128), 128)
        return pltpu.make_async_remote_copy(
            base_ref.at[rows], rows_ref, base_send.at[m], base_recv, device_id=at(group, m)
        )

    own_lead = pltpu.make_async_copy(base_ref.at[pl.ds(0, 16)], lead_ref.at[pl.ds(0, 16)], own_sem.at[0])
    own_rows = pltpu.make_async_copy(base_ref.at[pl.ds(0, 128)], rows_ref, own_sem.at[1])
    root = (group == 0) & (member == 0)

    @pl.when(root)
    def _():
        own_lead.start()

        def send(m, carry):
            lead_copy(base_ref, m, m, 0, m).start()
            return carry

        lax.fori_loop(1, members, send, 0)

    def halo(dg, ds):
        k = sides.index((dg, ds))
        if ds == 0:
            source, target = (high_x, before_x) if dg == 1 else (low_x, after_x)
        else:
            if dg == 0:
                source = high_y if ds == 1 else low_y
                place = pl.ds(32, 1024)
            else:
                face = high_x if dg == 1 else low_x
                source = face.at[pl.ds(992 if ds == 1 else 0, 32)]
                place = pl.ds(0 if dg == 1 else 1056, 32)
            target = (before_y if ds == 1 else after_y).at[place]
        return pltpu.make_async_remote_copy(
            source, target, halo_send.at[k], halo_recv.at[k], device_id=at(group + dg, member + ds)
        )

    for dg, ds in sides:
        @pl.when(exists(dg, ds))
        def _():
            halo(dg, ds).start()

        @pl.when(jnp.logical_not(exists(-dg, -ds)))
        def _():
            if ds == 0:
                target = before_x if dg == 1 else after_x
                target[...] = jnp.zeros_like(target)
            else:
                target = before_y if ds == 1 else after_y
                place = pl.ds(32, 1024) if dg == 0 else pl.ds(0 if dg == 1 else 1056, 32)
                target[place, :] = jnp.zeros((1024 if dg == 0 else 32, 128), BF)

    @pl.when(member == 0)
    def _():
        own_rows.start()

        def send(m, carry):
            base_copy(m).start()
            return carry

        lax.fori_loop(1, members, send, 0)

    @pl.when(root)
    def _():
        own_lead.wait()

    @pl.when(jnp.logical_not(root))
    def _():
        lead_copy(lead_ref, member, 0, group, member).wait_recv()

    @pl.when(group == 0)
    def _():
        for g in range(1, groups):
            lead_copy(lead_ref, member, 64 + g, g, member).start()

    def spread(d, carry):
        lead_copy(lead_ref, member, 32 + d, group, lax.rem(member + d, members)).start()
        return carry

    lax.fori_loop(1, members, spread, 0)

    for dg, ds in sides:
        @pl.when(exists(-dg, -ds))
        def _():
            halo(dg, ds).wait_recv()

        @pl.when(exists(dg, ds))
        def _():
            halo(dg, ds).wait_send()

    def gather(d, carry):
        lead_copy(lead_ref, lax.rem(member + d, members), 0, group, member).wait_recv()
        lead_copy(lead_ref, member, 32 + d, group, member).wait_send()
        return carry

    lax.fori_loop(1, members, gather, 0)

    @pl.when(group == 0)
    def _():
        for g in range(1, groups):
            lead_copy(lead_ref, member, 64 + g, g, member).wait_send()

    @pl.when(root)
    def _():
        def sent(m, carry):
            lead_copy(base_ref, m, m, 0, m).wait_send()
            return carry

        lax.fori_loop(1, members, sent, 0)

    @pl.when(member == 0)
    def _():
        def sent(m, carry):
            base_copy(m).wait_send()
            return carry

        lax.fori_loop(1, members, sent, 0)
        own_rows.wait()

    @pl.when(member > 0)
    def _():
        base_copy(member).wait_recv()


def opening(high_x, low_x, high_y, low_y, base_front):
    vmem = pl.BlockSpec(memory_space=pltpu.VMEM)
    dma = pltpu.SemaphoreType.DMA
    return pl.pallas_call(
        opening_kernel,
        out_shape=[
            jax.ShapeDtypeStruct((1024, 128), BF),
            jax.ShapeDtypeStruct((1024, 128), BF),
            jax.ShapeDtypeStruct((1088, 128), BF),
            jax.ShapeDtypeStruct((1088, 128), BF),
            jax.ShapeDtypeStruct((512, 512), BF),
            jax.ShapeDtypeStruct((128, 512), BF),
        ],
        in_specs=[vmem] * 4 + [pl.BlockSpec(memory_space=pl.ANY)],
        out_specs=[vmem] * 6,
        scratch_shapes=[
            dma((8,)), dma((8,)), dma((68,)), dma((32,)), dma((32,)), dma, dma((2,)),
        ],
        compiler_params=pltpu.CompilerParams(
            collective_id=0, has_side_effects=True, vmem_limit_bytes=16 * 2**20
        ),
        name="opening",
    )(high_x, low_x, high_y, low_y, base_front)


def panel_kernel(
    panel_ref, rows_ref, cols_ref, send, recv, fold_send, fold_recv, col_send, col_recv, own_sem
):
    groups, members, chips = 4, 32, 16
    group = lax.axis_index("grp")
    member = lax.axis_index("sub")
    chip = member // 2
    core = lax.rem(member, 2)
    live = member // 8 <= group
    source_group = member // 8
    barrier = pltpu.get_barrier_semaphore()

    def greet(d, carry):
        pl.semaphore_signal(barrier, 1, device_id=at(group, lax.rem(member + d, members)))
        return carry

    lax.fori_loop(1, members, greet, 0)

    @pl.when(source_group < group)
    def _():
        for i in range(4):
            pl.semaphore_signal(
                barrier, 1, device_id=at(source_group, lax.rem(member, 8) * 4 + i)
            )

    pl.semaphore_wait(barrier, members - 1 + groups - 1 - group)

    def block(m):
        return pl.ds(pl.multiple_of(128 * m, 128), 128)

    def row_copy(m, k, s):
        return pltpu.make_async_remote_copy(
            panel_ref, rows_ref.at[block(m)], send.at[k], recv.at[m // 2], device_id=at(group, s)
        )

    def fold_copy(m, source):
        return pltpu.make_async_remote_copy(
            source, rows_ref.at[block(m)], fold_send.at[m // 2], fold_recv.at[m // 2],
            device_id=at(group, chip * 2 + 1 - core),
        )

    def other(d):
        return lax.rem(chip + d, chips) * 2 + core

    target = group * 8 + member // 4
    quarter = lax.rem(member, 4)

    def col_copy(g, q, s):
        return pltpu.make_async_remote_copy(
            panel_ref, cols_ref.at[block(q)], col_send.at[g], col_recv.at[q], device_id=at(g, s)
        )

    def spread(d, carry):
        @pl.when(other(d) // 8 <= group)
        def _():
            row_copy(member, d, other(d)).start()

        return carry

    lax.fori_loop(1, chips, spread, 0)

    for g in range(groups):
        @pl.when((g >= group) & jnp.logical_not((g == group) & (target == member)))
        def _():
            col_copy(g, quarter, target).start()

    own_cols = pltpu.make_async_copy(panel_ref, cols_ref.at[block(quarter)], own_sem.at[0])
    own_rows = pltpu.make_async_copy(panel_ref, rows_ref.at[block(member)], own_sem.at[1])

    @pl.when(target == member)
    def _():
        own_cols.start()

    own_rows.start()

    @pl.when(live)
    def _():
        fold_copy(member, panel_ref).start()

        def fold(d, carry):
            m = other(d)
            row_copy(m, 0, member).wait_recv()
            fold_copy(m, rows_ref.at[block(m)]).start()
            return carry

        lax.fori_loop(1, chips, fold, 0)

        def folded(d, carry):
            m = lax.rem(chip + d, chips) * 2
            fold_copy(m + 1 - core, panel_ref).wait_recv()
            fold_copy(m + core, panel_ref).wait_send()
            return carry

        lax.fori_loop(0, chips, folded, 0)

    def sent(d, carry):
        @pl.when(other(d) // 8 <= group)
        def _():
            row_copy(member, d, other(d)).wait_send()

        return carry

    lax.fori_loop(1, chips, sent, 0)
    for g in range(groups):
        @pl.when((g >= group) & jnp.logical_not((g == group) & (target == member)))
        def _():
            col_copy(g, quarter, target).wait_send()

    for i in range(4):
        source = lax.rem(member, 8) * 4 + i
        itself = (source_group == group) & (source == member)

        @pl.when((source_group <= group) & jnp.logical_not(itself))
        def _():
            col_copy(group, i, member).wait_recv()

    @pl.when(target == member)
    def _():
        own_cols.wait()

    own_rows.wait()


def panel_spread(panel):
    dma = pltpu.SemaphoreType.DMA
    anywhere = pl.BlockSpec(memory_space=pl.ANY)
    return pl.pallas_call(
        panel_kernel,
        out_shape=[jax.ShapeDtypeStruct((4096, 512), BF), jax.ShapeDtypeStruct((512, 512), BF)],
        in_specs=[pl.BlockSpec(memory_space=pltpu.VMEM)],
        out_specs=[anywhere, anywhere],
        scratch_shapes=[
            dma((16,)), dma((16,)), dma((16,)), dma((16,)), dma((4,)), dma((4,)), dma((2,)),
        ],
        compiler_params=pltpu.CompilerParams(
            collective_id=1, has_side_effects=True, vmem_limit_bytes=16 * 2**20
        ),
        name="panel_spread",
    )(panel)


def arrivals(owner_ids, local_block, owner):
    order = jnp.arange(owner_ids.shape[1], dtype=jnp.int32)[None, :]
    here = owner_ids == owner
    first = jnp.min(jnp.where(here, order, 1 << 20), axis=1, keepdims=True)
    one = jnp.max(jnp.where(here & (order == first), local_block, -1), axis=1)
    two = jnp.max(jnp.where(here & (order > first), local_block, -1), axis=1)
    return jnp.stack([one, two], axis=1).reshape(-1)


def per_device(basis_cols, diag_weight, link_weight, base_front, block_lists):
    groups, members, devices = 4, 32, 128
    group = lax.axis_index("grp")
    member = lax.axis_index("sub")
    me = group * members + member

    def scaled(b, w):
        return (w[..., None] * b.astype(F32)).astype(BF).reshape(1024, 128)

    before_x, after_x, before_y, after_y, lead, base_rows = opening(
        scaled(basis_cols[31], link_weight[31]),
        scaled(basis_cols[0], link_weight[0]),
        scaled(basis_cols[:, 31], link_weight[:, 31]),
        scaled(basis_cols[:, 0], link_weight[:, 0]),
        base_front,
    )

    own_list = lax.dynamic_index_in_dim(block_lists.reshape(devices, 128, 2), me, 0, keepdims=False)
    own_owner = own_list[:, 0] // members * members + own_list[:, 1] // groups
    order = jnp.arange(128)
    rank = jnp.sum(
        (own_owner[:, None] == own_owner[None, :]) & (order[None, :] < order[:, None]), axis=1
    )
    slots = (own_owner * 2 + rank).astype(jnp.int32)

    outgoing = galerkin_tiles(
        slots,
        basis_cols.reshape(32, 1024, 128),
        link_weight.reshape(32, 1, 1024),
        diag_weight.reshape(32, 1, 1024),
        before_y.reshape(34, 32, 128),
        after_y.reshape(34, 32, 128),
        before_x,
        after_x,
    )

    outgoing, lead, block_lists = lax.optimization_barrier((outgoing, lead, block_lists))
    listed = block_lists.reshape(devices, 128, 2)
    row_block = listed[:, :, 0]
    col_block = listed[:, :, 1]
    owner_ids = row_block // members * members + col_block // groups
    local_block = row_block % members * groups + col_block % groups
    place = arrivals(owner_ids, local_block, me)
    panel_place = arrivals(owner_ids, local_block, group * members)
    lead = lead.astype(F32)
    symmetric = jnp.tril(lead) + jnp.tril(lead, -1).T
    pivot_matrix = symmetric + jnp.diag(jnp.sum(jnp.abs(symmetric), axis=1) + 1.0)
    factor, inverse = pivot_factor(pivot_matrix)
    strips = outgoing.reshape(groups, members, 2, 128, 128)[:, 0]
    strips = strips.reshape(groups, 2, members, 4, 128).transpose(0, 2, 1, 3, 4)
    strips = strips.reshape(devices, 2, 4, 128)
    strips = lax.all_to_all(strips, ("grp", "sub"), split_axis=0, concat_axis=0, tiled=True)
    received = lax.all_to_all(
        outgoing.reshape(devices, 2, 128, 128), ("grp", "sub"), split_axis=0, concat_axis=0, tiled=True
    ).reshape(256, 128, 128)

    strips, inverse = lax.optimization_barrier((strips, inverse))
    strips = jnp.where((panel_place >= 0)[:, None], strips.reshape(256, 512), 0)
    pick = (panel_place[None, :] == jnp.arange(128)[:, None]).astype(BF)
    strips = dotb(pick, strips, NN).reshape(members, groups, 4, 128)
    strips = strips.transpose(0, 2, 1, 3).reshape(members, 4, 512)
    strips = lax.all_to_all(strips, "sub", split_axis=0, concat_axis=0, tiled=True)
    front_rows = base_rows.astype(F32) + strips.reshape(128, 512)

    solved = dot32(front_rows, inverse, NT)
    in_lead = (group == 0) & (member < 4)
    own_factor = lax.dynamic_slice_in_dim(factor, 128 * jnp.minimum(member, 3), 128, 0)
    panel = jnp.where(in_lead, own_factor, solved).astype(BF)
    panel_rows, panel_cols = panel_spread(panel)
    trailing = trailing_front(place, panel_rows, panel_cols, base_front, received)
    return (trailing, panel)


def solution(mesh):
    return jax.shard_map(
        per_device,
        mesh=mesh,
        in_specs=(
            P("grp", "sub", None, None),
            P("grp", "sub", None),
            P("grp", "sub", None),
            P("grp", "sub"),
            P(),
        ),
        out_specs=(P("grp", "sub"), P(("grp", "sub"), None)),
        check_vma=False,
    )
```

```python
import functools

import jax
import jax.numpy as jnp
from jax import lax
from jax.experimental import pallas as pl
from jax.experimental.pallas import tpu as pltpu
from jax.sharding import PartitionSpec as P

EARLY = 13
NT = (((1,), (1,)), ((), ()))
NN = (((1,), (0,)), ((), ()))
BF = jnp.bfloat16
F32 = jnp.float32


def dot32(a, b, dims):
    return lax.dot_general(a, b, dims, precision=lax.Precision.HIGHEST, preferred_element_type=F32)


def dotb(a, b, dims):
    return lax.dot_general(a, b, dims, preferred_element_type=F32)


def tile_kernel(
    slot_ref, basis_ref, link_ref, diag_ref, before_y_ref, after_y_ref,
    before_x_ref, after_x_ref, stencil_ref, out_ref,
    scaled_t, basis_t, partial, stage, sems, clear_sems,
):
    step = pl.program_id(0)
    gap = jnp.zeros((96, 128), BF)

    def sides(slot, plane):
        first = jnp.concatenate([gap, before_y_ref[plane + 1]], axis=0)
        last = jnp.concatenate([after_y_ref[plane + 1], gap], axis=0)
        scaled_t[slot, :, 0:128] = first.T
        scaled_t[slot, :, 1152:1280] = last.T

    def spread(slot, ring):
        windows = [scaled_t[slot, :, 256 * q:256 * q + 512] for q in range(4)]
        sums = dotb(jnp.concatenate(windows, axis=0), stencil_ref[...], NN)
        for q in range(4):
            partial[ring, :, 256 * q:256 * q + 256] = sums[128 * q:128 * q + 128]

    def copy_out(slot, q, target):
        return pltpu.make_async_copy(stage.at[slot, q], out_ref.at[target], sems.at[slot, q])

    def wait(slot):
        for q in range(4):
            copy_out(slot, q, 0).wait()

    def start(slot, plane):
        for q in range(4):
            copy_out(slot, q, slot_ref[plane * 4 + q]).start()

    def finish(plane, slot, low, mid, high):
        link = link_ref[plane]
        diag = diag_ref[plane]
        for q in range(4):
            cells = slice(256 * q, 256 * q + 256)
            around = partial[low, :, cells] + partial[mid, :, cells] + partial[high, :, cells]
            around = around - scaled_t[slot, :, 128 + 256 * q:384 + 256 * q].astype(F32)
            own = basis_t[slot, :, cells]
            image = diag[:, cells] * own.astype(F32) - link[:, cells] * around
            head = image.astype(BF)
            tail = (image - head.astype(F32)).astype(BF)
            stage[slot, q] = (dotb(own, head, NT) + dotb(own, tail, NT)).astype(BF)

    def clear(n):
        return pltpu.make_async_copy(
            stage.at[0, 0], out_ref.at[64 * (n // 2) + n % 2], clear_sems.at[n]
        )

    @pl.when(step == 0)
    def _():
        stage[0, 0] = jnp.zeros((128, 128), BF)
        for n in range(8):
            clear(n).start()
        for n in range(8):
            clear(n).wait()
        sides(1, -1)
        scaled_t[1, :, 128:1152] = before_x_ref[...].T
        spread(1, 3)

    for u in range(4):
        plane = step * 4 + u
        slot = u % 2
        turned = basis_ref[u].T
        basis_t[slot] = turned
        scaled_t[slot, :, 128:1152] = (turned.astype(F32) * link_ref[plane]).astype(BF)
        sides(slot, plane)
        spread(slot, u)
        if u < 3:
            pl.when(step > 0)(functools.partial(wait, 1 - slot))
        else:
            wait(1 - slot)
        finish(jnp.maximum(plane - 1, 0), 1 - slot, (u + 2) % 4, (u + 3) % 4, u)
        if u == 0:
            pl.when(step > 0)(functools.partial(start, 1 - slot, plane - 1))
        else:
            start(1 - slot, plane - 1)

    @pl.when(step == pl.num_programs(0) - 1)
    def _():
        sides(0, 32)
        scaled_t[0, :, 128:1152] = after_x_ref[...].T
        spread(0, 0)
        wait(1)
        finish(31, 1, 2, 3, 0)
        start(1, 31)
        wait(0)
        wait(1)


def galerkin_tiles(slots, basis, link, diag, before_y, after_y, before_x, after_x):
    k = jnp.arange(512)[:, None]
    n = jnp.arange(256)[None, :]
    stencil = (
        (jnp.abs(k // 32 - 4 - n // 32) <= 1) & (jnp.abs(k % 32 - n % 32) <= 1)
    ).astype(BF)
    cube = lambda t, s: (0, 0, 0)
    flat = lambda t, s: (0, 0)
    return pl.pallas_call(
        tile_kernel,
        out_shape=jax.ShapeDtypeStruct((256, 128, 128), BF),
        grid_spec=pltpu.PrefetchScalarGridSpec(
            num_scalar_prefetch=1,
            grid=(8,),
            in_specs=[
                pl.BlockSpec((4, 1024, 128), lambda t, s: (t, 0, 0)),
                pl.BlockSpec((32, 1, 1024), cube),
                pl.BlockSpec((32, 1, 1024), cube),
                pl.BlockSpec((34, 32, 128), cube),
                pl.BlockSpec((34, 32, 128), cube),
                pl.BlockSpec((1024, 128), flat),
                pl.BlockSpec((1024, 128), flat),
                pl.BlockSpec((512, 256), flat),
            ],
            out_specs=pl.BlockSpec(memory_space=pl.ANY),
            scratch_shapes=[
                pltpu.VMEM((2, 128, 1280), BF),
                pltpu.VMEM((2, 128, 1024), BF),
                pltpu.VMEM((4, 128, 1024), F32),
                pltpu.VMEM((2, 4, 128, 128), BF),
                pltpu.SemaphoreType.DMA((2, 4)),
                pltpu.SemaphoreType.DMA((8,)),
            ],
        ),
        compiler_params=pltpu.CompilerParams(
            dimension_semantics=("arbitrary",), vmem_limit_bytes=60 * 2**20
        ),
        name="galerkin_tiles",
    )(slots, basis, link, diag, before_y, after_y, before_x, after_x, stencil)


def factor_kernel(pivot_ref, factor_ref, inverse_ref, work):
    size = pivot_ref.shape[0]
    count = size // 128
    rows = lax.broadcasted_iota(jnp.int32, (128, 128), 0)
    lanes = lax.broadcasted_iota(jnp.int32, (128, 128), 1)
    sub8 = lax.broadcasted_iota(jnp.int32, (8, 128), 0)
    lane8 = lax.broadcasted_iota(jnp.int32, (8, 128), 1)
    all_rows = lax.broadcasted_iota(jnp.int32, (size, 1), 0)
    work[...] = pivot_ref[...]
    factor_ref[...] = jnp.zeros_like(factor_ref)
    inverse_ref[...] = jnp.zeros_like(inverse_ref)

    def one_block(b, carry):
        own = pl.ds(pl.multiple_of(128 * b, 128), 128)
        block = work[own, own]
        parts = [block[8 * i:8 * i + 8] for i in range(16)]
        for panel in range(16):
            cols = []
            for k in range(8):
                lane = slice(8 * panel + k, 8 * panel + k + 1)
                cols.append([jnp.broadcast_to(parts[i][:, lane], (8, 128)) for i in range(panel, 16)])
            for k in range(8):
                lane = 8 * panel + k
                pivot_row = jnp.broadcast_to(parts[panel][k:k + 1], (8, 128))
                pivot_row = jnp.where(lane8 == lane, 1.0, pivot_row)
                inverse = 1.0 / jnp.broadcast_to(cols[k][0][k:k + 1], (8, 128))
                heads = [None] * 8
                for l in range(k + 1, 8):
                    heads[l] = jnp.broadcast_to(cols[l][0][k:k + 1], (8, 128))
                for i in range(panel, 16):
                    ratio = cols[k][i - panel] * inverse
                    clear = lane8 == lane
                    if i == panel:
                        ratio = jnp.where(sub8 > k, ratio, 0.0)
                        clear = clear & (sub8 > k)
                    for l in range(k + 1, 8):
                        cols[l][i - panel] = cols[l][i - panel] - ratio * heads[l]
                    parts[i] = jnp.where(clear, 0.0, parts[i]) - ratio * pivot_row
        full = jnp.concatenate(parts, axis=0)
        pivots = jnp.sum(jnp.where(rows == lanes, full, 0.0), axis=1, keepdims=True)
        scale = 1.0 / jnp.sqrt(pivots)
        upper = jnp.where(rows <= lanes, full * scale, 0.0)
        inv = jnp.where(rows > lanes, full * scale, jnp.where(rows == lanes, scale, 0.0))
        below = dot32(work[:, own], inv, NT)
        below = jnp.where(all_rows >= 128 * b + 128, below, 0.0)
        factor_ref[:, own] = below
        factor_ref[own, own] = upper.T
        inverse_ref[own, own] = inv
        work[...] = work[...] - dot32(below, below, NT)
        return carry

    lax.fori_loop(0, count, one_block, 0)
    for b in range(1, count):
        own = slice(128 * b, 128 * b + 128)
        left = slice(0, 128 * b)
        product = dot32(factor_ref[own, left], inverse_ref[left, left], NN)
        inverse_ref[own, left] = -dot32(inverse_ref[own, own], product, NN)


def pivot_factor(pivot_matrix):
    size = pivot_matrix.shape[0]
    return pl.pallas_call(
        factor_kernel,
        out_shape=[jax.ShapeDtypeStruct((size, size), F32)] * 2,
        in_specs=[pl.BlockSpec(memory_space=pltpu.VMEM)],
        out_specs=[pl.BlockSpec(memory_space=pltpu.VMEM)] * 2,
        scratch_shapes=[pltpu.VMEM((size, size), F32)],
        compiler_params=pltpu.CompilerParams(vmem_limit_bytes=32 * 2**20),
        name="pivot_factor",
    )(pivot_matrix)


def final_kernel(place_ref, row_ref, col_ref, base_ref, received_ref, out_ref, sums):
    step = pl.program_id(0)
    group = lax.axis_index("grp")
    member = lax.axis_index("sub")
    row_start = group * 4096
    col_start = member * 512
    live = (member > 0) & (row_start + 4095 >= col_start)

    @pl.when(live & (step == 0))
    def _():
        sums[...] = jnp.zeros_like(sums)

        def add(slot, carry):
            place = place_ref[slot]

            @pl.when(place >= 0)
            def _():
                sums[place] = sums[place] + received_ref[slot].astype(F32)

            return carry

        lax.fori_loop(0, 256, add, 0)

    first_row = row_start + step * 512

    @pl.when(live & (first_row + 511 >= col_start))
    def _():
        update = dotb(row_ref[...], col_ref[...], NT)
        rows = first_row + lax.broadcasted_iota(jnp.int32, (128, 128), 0)
        cols = col_start + lax.broadcasted_iota(jnp.int32, (128, 128), 1)
        for i in range(4):
            for j in range(4):
                r = slice(128 * i, 128 * i + 128)
                c = slice(128 * j, 128 * j + 128)
                value = base_ref[r, c].astype(F32) + sums[(step * 4 + i) * 4 + j] - update[r, c]
                out_ref[r, c] = jnp.where(rows + 128 * i >= cols + 128 * j, value, 0.0)

    @pl.when(jnp.logical_not(live & (first_row + 511 >= col_start)))
    def _():
        out_ref[...] = jnp.zeros_like(out_ref)


def trailing_front(place, panel_rows, panel_cols, base, received):
    return pl.pallas_call(
        final_kernel,
        out_shape=jax.ShapeDtypeStruct((4096, 512), F32),
        grid_spec=pltpu.PrefetchScalarGridSpec(
            num_scalar_prefetch=1,
            grid=(8,),
            in_specs=[
                pl.BlockSpec((512, 512), lambda t, s: (t, 0)),
                pl.BlockSpec((512, 512), lambda t, s: (0, 0)),
                pl.BlockSpec((512, 512), lambda t, s: (t, 0)),
                pl.BlockSpec((256, 128, 128), lambda t, s: (0, 0, 0)),
            ],
            out_specs=pl.BlockSpec((512, 512), lambda t, s: (t, 0)),
            scratch_shapes=[pltpu.VMEM((128, 128, 128), F32)],
        ),
        compiler_params=pltpu.CompilerParams(
            dimension_semantics=("arbitrary",), vmem_limit_bytes=60 * 2**20
        ),
        name="trailing_front",
    )(place, panel_rows, panel_cols, base, received)


def at(group, member):
    return {"grp": group, "sub": member}


def opening_kernel(
    high_x, low_x, high_y, low_y, base_ref,
    before_x, after_x, before_y, after_y, lead_ref, rows_ref,
    halo_send, halo_recv, lead_send, lead_recv, base_send, base_recv, own_sem,
):
    groups, members = 4, 32
    group = lax.axis_index("grp")
    member = lax.axis_index("sub")
    barrier = pltpu.get_barrier_semaphore()
    sides = [(dg, ds) for dg in (-1, 0, 1) for ds in (-1, 0, 1) if (dg, ds) != (0, 0)]

    def exists(dg, ds):
        g, s = group + dg, member + ds
        return (g >= 0) & (g < groups) & (s >= 0) & (s < members)

    def greet(d, carry):
        pl.semaphore_signal(barrier, 1, device_id=at(group, lax.rem(member + d, members)))
        return carry

    lax.fori_loop(1, members, greet, 0)
    for d in range(1, groups):
        pl.semaphore_signal(barrier, 1, device_id=at(lax.rem(group + d, groups), member))
    for dg, ds in sides:
        if dg and ds:
            @pl.when(exists(dg, ds))
            def _():
                pl.semaphore_signal(barrier, 1, device_id=at(group + dg, member + ds))

    near_groups = 2 - jnp.where(group == 0, 1, 0) - jnp.where(group == groups - 1, 1, 0)
    near_members = 2 - jnp.where(member == 0, 1, 0) - jnp.where(member == members - 1, 1, 0)
    pl.semaphore_wait(barrier, members - 1 + groups - 1 + near_groups * near_members)

    def piece(m):
        return pl.ds(pl.multiple_of(16 * m, 16), 16)

    def lead_copy(source, m, k, g, s):
        return pltpu.make_async_remote_copy(
            source.at[piece(m)], lead_ref.at[piece(m)], lead_send.at[k], lead_recv.at[m],
            device_id=at(g, s),
        )

    def base_copy(m):
        rows = pl.ds(pl.multiple_of(128 * m, 128), 128)
        return pltpu.make_async_remote_copy(
            base_ref.at[rows], rows_ref, base_send.at[m], base_recv, device_id=at(group, m)
        )

    own_lead = pltpu.make_async_copy(base_ref.at[pl.ds(0, 16)], lead_ref.at[pl.ds(0, 16)], own_sem.at[0])
    own_rows = pltpu.make_async_copy(base_ref.at[pl.ds(0, 128)], rows_ref, own_sem.at[1])
    root = (group == 0) & (member == 0)

    @pl.when(root)
    def _():
        own_lead.start()

        def send(m, carry):
            lead_copy(base_ref, m, m, 0, m).start()
            return carry

        lax.fori_loop(1, members, send, 0)

    def halo(dg, ds):
        k = sides.index((dg, ds))
        if ds == 0:
            source, target = (high_x, before_x) if dg == 1 else (low_x, after_x)
        else:
            if dg == 0:
                source = high_y if ds == 1 else low_y
                place = pl.ds(32, 1024)
            else:
                face = high_x if dg == 1 else low_x
                source = face.at[pl.ds(992 if ds == 1 else 0, 32)]
                place = pl.ds(0 if dg == 1 else 1056, 32)
            target = (before_y if ds == 1 else after_y).at[place]
        return pltpu.make_async_remote_copy(
            source, target, halo_send.at[k], halo_recv.at[k], device_id=at(group + dg, member + ds)
        )

    for dg, ds in sides:
        @pl.when(exists(dg, ds))
        def _():
            halo(dg, ds).start()

        @pl.when(jnp.logical_not(exists(-dg, -ds)))
        def _():
            if ds == 0:
                target = before_x if dg == 1 else after_x
                target[...] = jnp.zeros_like(target)
            else:
                target = before_y if ds == 1 else after_y
                place = pl.ds(32, 1024) if dg == 0 else pl.ds(0 if dg == 1 else 1056, 32)
                target[place, :] = jnp.zeros((1024 if dg == 0 else 32, 128), BF)

    @pl.when(member == 0)
    def _():
        own_rows.start()

        def send(m, carry):
            base_copy(m).start()
            return carry

        lax.fori_loop(1, EARLY, send, 0)

    @pl.when(root)
    def _():
        own_lead.wait()

    @pl.when(jnp.logical_not(root))
    def _():
        lead_copy(lead_ref, member, 0, group, member).wait_recv()

    @pl.when(group == 0)
    def _():
        for g in range(1, groups):
            lead_copy(lead_ref, member, 64 + g, g, member).start()

    def spread(d, carry):
        lead_copy(lead_ref, member, 32 + d, group, lax.rem(member + d, members)).start()
        return carry

    lax.fori_loop(1, members, spread, 0)

    for dg, ds in sides:
        @pl.when(exists(-dg, -ds))
        def _():
            halo(dg, ds).wait_recv()

        @pl.when(exists(dg, ds))
        def _():
            halo(dg, ds).wait_send()

    def gather(d, carry):
        lead_copy(lead_ref, lax.rem(member + d, members), 0, group, member).wait_recv()
        lead_copy(lead_ref, member, 32 + d, group, member).wait_send()
        return carry

    lax.fori_loop(1, members, gather, 0)

    @pl.when(group == 0)
    def _():
        for g in range(1, groups):
            lead_copy(lead_ref, member, 64 + g, g, member).wait_send()

    @pl.when(root)
    def _():
        def sent(m, carry):
            lead_copy(base_ref, m, m, 0, m).wait_send()
            return carry

        lax.fori_loop(1, members, sent, 0)

    @pl.when(member == 0)
    def _():
        def sent(m, carry):
            base_copy(m).wait_send()
            return carry

        lax.fori_loop(1, EARLY, sent, 0)
        own_rows.wait()

    @pl.when((member > 0) & (member < EARLY))
    def _():
        base_copy(member).wait_recv()


def opening(high_x, low_x, high_y, low_y, base_front):
    vmem = pl.BlockSpec(memory_space=pltpu.VMEM)
    dma = pltpu.SemaphoreType.DMA
    return pl.pallas_call(
        opening_kernel,
        out_shape=[
            jax.ShapeDtypeStruct((1024, 128), BF),
            jax.ShapeDtypeStruct((1024, 128), BF),
            jax.ShapeDtypeStruct((1088, 128), BF),
            jax.ShapeDtypeStruct((1088, 128), BF),
            jax.ShapeDtypeStruct((512, 512), BF),
            jax.ShapeDtypeStruct((128, 512), BF),
        ],
        in_specs=[vmem] * 4 + [pl.BlockSpec(memory_space=pl.ANY)],
        out_specs=[vmem] * 6,
        scratch_shapes=[
            dma((8,)), dma((8,)), dma((68,)), dma((32,)), dma((32,)), dma, dma((2,)),
        ],
        compiler_params=pltpu.CompilerParams(
            collective_id=0, has_side_effects=True, vmem_limit_bytes=16 * 2**20
        ),
        name="opening",
    )(high_x, low_x, high_y, low_y, base_front)


def front_kernel(
    key_ref, tiles_ref, base_front_ref, early_ref, front_ref, strips, sums, added, late,
    strip_send, strip_recv, sum_send, sum_recv, base_send, base_recv, own_sem,
):
    groups, members, devices, parts, base = 4, 32, 128, 8, 8
    group = lax.axis_index("grp")
    member = lax.axis_index("sub")
    me = group * members + member
    takes = (member >= base) & (member < base + parts)
    barrier = pltpu.get_barrier_semaphore()

    def greet(d, carry):
        other = lax.rem(me + d, devices)
        pl.semaphore_signal(barrier, 1, device_id=at(other // members, lax.rem(other, members)))
        return carry

    lax.fori_loop(1, devices, greet, 0)
    pl.semaphore_wait(barrier, devices - 1)

    def source(g, r):
        first = pl.ds(2 * members * g, 2)
        return tiles_ref.at[first, pl.ds(pl.multiple_of(16 * r, 16), 16)]

    def strip_copy(sender, g, r, k):
        return pltpu.make_async_remote_copy(
            source(g, r), strips.at[pl.ds(2 * sender, 2)], strip_send.at[k], strip_recv.at[sender],
            device_id=at(g, base + r),
        )

    own_rank = lax.rem(member, parts)
    own_strip = pltpu.make_async_copy(
        source(group, own_rank), strips.at[pl.ds(2 * me, 2)], own_sem.at[0]
    )

    def target(j):
        t = lax.rem(j + group * parts + own_rank, groups * parts)
        return t // parts, lax.rem(t, parts)

    def start_strip(j, carry):
        g, r = target(j)

        @pl.when((g != group) | (base + r != member))
        def _():
            strip_copy(me, g, r, j).start()

        return carry

    lax.fori_loop(0, groups * parts, start_strip, 0)

    def base_copy(m):
        rows = pl.ds(pl.multiple_of(128 * m, 128), 128)
        return pltpu.make_async_remote_copy(
            base_front_ref.at[rows], late, base_send.at[m], base_recv, device_id=at(group, m)
        )

    @pl.when(member == 0)
    def _():
        def send(m, carry):
            base_copy(m).start()
            return carry

        lax.fori_loop(EARLY, members, send, 0)

    def sum_copy(r, a):
        rows = pl.ds(pl.multiple_of(16 * r, 16), 16)
        return pltpu.make_async_remote_copy(
            sums.at[pl.ds(4 * a, 4)], added.at[:, rows], sum_send.at[a], sum_recv.at[r],
            device_id=at(group, a),
        )

    own_sum = pltpu.make_async_copy(
        sums.at[pl.ds(4 * member, 4)],
        added.at[:, pl.ds(pl.multiple_of(16 * own_rank, 16), 16)],
        own_sem.at[1],
    )

    @pl.when(takes)
    def _():
        own_strip.start()

        def arrive(d, carry):
            strip_copy(lax.rem(me + d, devices), group, own_rank, 0).wait_recv()
            return carry

        lax.fori_loop(1, devices, arrive, 0)
        own_strip.wait()
        rows = strips[...].reshape(4096, 128)
        for n in range(8):
            ids = 256 * n + lax.broadcasted_iota(jnp.int32, (256, 4096), 0)
            pick = jnp.where(key_ref[...] == ids, 1.0, 0.0).astype(BF)
            sums[16 * n:16 * n + 16] = dotb(pick, rows, NN).astype(BF).reshape(16, 16, 128)

        def send(d, carry):
            sum_copy(own_rank, lax.rem(member + d, members)).start()
            return carry

        lax.fori_loop(1, members, send, 0)
        own_sum.start()

    for r in range(parts):
        @pl.when(member != base + r)
        def _():
            sum_copy(r, member).wait_recv()

    @pl.when(takes)
    def _():
        own_sum.wait()

    @pl.when(member < EARLY)
    def _():
        for q in range(4):
            cols = slice(128 * q, 128 * q + 128)
            front_ref[:, cols] = early_ref[:, cols].astype(F32) + added[q].astype(F32)

    @pl.when(member >= EARLY)
    def _():
        base_copy(member).wait_recv()
        for q in range(4):
            cols = slice(128 * q, 128 * q + 128)
            front_ref[:, cols] = late[:, cols].astype(F32) + added[q].astype(F32)

    def sent_strip(j, carry):
        g, r = target(j)

        @pl.when((g != group) | (base + r != member))
        def _():
            strip_copy(me, g, r, j).wait_send()

        return carry

    lax.fori_loop(0, groups * parts, sent_strip, 0)

    @pl.when(takes)
    def _():
        def sent(d, carry):
            sum_copy(own_rank, lax.rem(member + d, members)).wait_send()
            return carry

        lax.fori_loop(1, members, sent, 0)

    @pl.when(member == 0)
    def _():
        def sent(m, carry):
            base_copy(m).wait_send()
            return carry

        lax.fori_loop(EARLY, members, sent, 0)


def front_rows_of(key, tiles, base_front, early):
    dma = pltpu.SemaphoreType.DMA
    anywhere = pl.BlockSpec(memory_space=pl.ANY)
    vmem = pl.BlockSpec(memory_space=pltpu.VMEM)
    return pl.pallas_call(
        front_kernel,
        out_shape=jax.ShapeDtypeStruct((128, 512), F32),
        in_specs=[vmem, anywhere, anywhere, vmem],
        out_specs=vmem,
        scratch_shapes=[
            pltpu.VMEM((256, 16, 128), BF),
            pltpu.VMEM((128, 16, 128), BF),
            pltpu.VMEM((4, 128, 128), BF),
            pltpu.VMEM((128, 512), BF),
            dma((32,)), dma((128,)), dma((32,)), dma((8,)), dma((32,)), dma, dma((2,)),
        ],
        compiler_params=pltpu.CompilerParams(
            collective_id=2, has_side_effects=True, vmem_limit_bytes=60 * 2**20
        ),
        name="front_rows",
    )(key, tiles, base_front, early)


def panel_kernel(
    panel_ref, rows_ref, cols_ref, send, recv, fold_send, fold_recv, col_send, col_recv, own_sem
):
    groups, members, chips = 4, 32, 16
    group = lax.axis_index("grp")
    member = lax.axis_index("sub")
    chip = member // 2
    core = lax.rem(member, 2)
    live = member // 8 <= group
    source_group = member // 8
    barrier = pltpu.get_barrier_semaphore()

    def greet(d, carry):
        pl.semaphore_signal(barrier, 1, device_id=at(group, lax.rem(member + d, members)))
        return carry

    lax.fori_loop(1, members, greet, 0)

    @pl.when(source_group < group)
    def _():
        for i in range(4):
            pl.semaphore_signal(
                barrier, 1, device_id=at(source_group, lax.rem(member, 8) * 4 + i)
            )

    pl.semaphore_wait(barrier, members - 1 + groups - 1 - group)

    def block(m):
        return pl.ds(pl.multiple_of(128 * m, 128), 128)

    def row_copy(m, k, s):
        return pltpu.make_async_remote_copy(
            panel_ref, rows_ref.at[block(m)], send.at[k], recv.at[m // 2], device_id=at(group, s)
        )

    def fold_copy(m, source):
        return pltpu.make_async_remote_copy(
            source, rows_ref.at[block(m)], fold_send.at[m // 2], fold_recv.at[m // 2],
            device_id=at(group, chip * 2 + 1 - core),
        )

    def other(d):
        return lax.rem(chip + d, chips) * 2 + core

    target = group * 8 + member // 4
    quarter = lax.rem(member, 4)

    def col_copy(g, q, s):
        return pltpu.make_async_remote_copy(
            panel_ref, cols_ref.at[block(q)], col_send.at[g], col_recv.at[q], device_id=at(g, s)
        )

    def spread(d, carry):
        @pl.when(other(d) // 8 <= group)
        def _():
            row_copy(member, d, other(d)).start()

        return carry

    lax.fori_loop(1, chips, spread, 0)

    for g in range(groups):
        @pl.when((g >= group) & jnp.logical_not((g == group) & (target == member)))
        def _():
            col_copy(g, quarter, target).start()

    own_cols = pltpu.make_async_copy(panel_ref, cols_ref.at[block(quarter)], own_sem.at[0])
    own_rows = pltpu.make_async_copy(panel_ref, rows_ref.at[block(member)], own_sem.at[1])

    @pl.when(target == member)
    def _():
        own_cols.start()

    own_rows.start()

    @pl.when(live)
    def _():
        fold_copy(member, panel_ref).start()

        def fold(d, carry):
            m = other(d)
            row_copy(m, 0, member).wait_recv()
            fold_copy(m, rows_ref.at[block(m)]).start()
            return carry

        lax.fori_loop(1, chips, fold, 0)

        def folded(d, carry):
            m = lax.rem(chip + d, chips) * 2
            fold_copy(m + 1 - core, panel_ref).wait_recv()
            fold_copy(m + core, panel_ref).wait_send()
            return carry

        lax.fori_loop(0, chips, folded, 0)

    def sent(d, carry):
        @pl.when(other(d) // 8 <= group)
        def _():
            row_copy(member, d, other(d)).wait_send()

        return carry

    lax.fori_loop(1, chips, sent, 0)
    for g in range(groups):
        @pl.when((g >= group) & jnp.logical_not((g == group) & (target == member)))
        def _():
            col_copy(g, quarter, target).wait_send()

    for i in range(4):
        source = lax.rem(member, 8) * 4 + i
        itself = (source_group == group) & (source == member)

        @pl.when((source_group <= group) & jnp.logical_not(itself))
        def _():
            col_copy(group, i, member).wait_recv()

    @pl.when(target == member)
    def _():
        own_cols.wait()

    own_rows.wait()


def panel_spread(panel):
    dma = pltpu.SemaphoreType.DMA
    anywhere = pl.BlockSpec(memory_space=pl.ANY)
    return pl.pallas_call(
        panel_kernel,
        out_shape=[jax.ShapeDtypeStruct((4096, 512), BF), jax.ShapeDtypeStruct((512, 512), BF)],
        in_specs=[pl.BlockSpec(memory_space=pltpu.VMEM)],
        out_specs=[anywhere, anywhere],
        scratch_shapes=[
            dma((16,)), dma((16,)), dma((16,)), dma((16,)), dma((4,)), dma((4,)), dma((2,)),
        ],
        compiler_params=pltpu.CompilerParams(
            collective_id=1, has_side_effects=True, vmem_limit_bytes=16 * 2**20
        ),
        name="panel_spread",
    )(panel)


def arrivals(owner_ids, local_block, owner):
    order = jnp.arange(owner_ids.shape[1], dtype=jnp.int32)[None, :]
    here = owner_ids == owner
    first = jnp.min(jnp.where(here, order, 1 << 20), axis=1, keepdims=True)
    one = jnp.max(jnp.where(here & (order == first), local_block, -1), axis=1)
    two = jnp.max(jnp.where(here & (order > first), local_block, -1), axis=1)
    return jnp.stack([one, two], axis=1).reshape(-1)


def per_device(basis_cols, diag_weight, link_weight, base_front, block_lists):
    groups, members, devices = 4, 32, 128
    group = lax.axis_index("grp")
    member = lax.axis_index("sub")
    me = group * members + member

    def scaled(b, w):
        return (w[..., None] * b.astype(F32)).astype(BF).reshape(1024, 128)

    before_x, after_x, before_y, after_y, lead, base_rows = opening(
        scaled(basis_cols[31], link_weight[31]),
        scaled(basis_cols[0], link_weight[0]),
        scaled(basis_cols[:, 31], link_weight[:, 31]),
        scaled(basis_cols[:, 0], link_weight[:, 0]),
        base_front,
    )

    own_list = lax.dynamic_index_in_dim(block_lists.reshape(devices, 128, 2), me, 0, keepdims=False)
    own_owner = own_list[:, 0] // members * members + own_list[:, 1] // groups
    order = jnp.arange(128)
    rank = jnp.sum(
        (own_owner[:, None] == own_owner[None, :]) & (order[None, :] < order[:, None]), axis=1
    )
    slots = (own_owner * 2 + rank).astype(jnp.int32)

    outgoing = galerkin_tiles(
        slots,
        basis_cols.reshape(32, 1024, 128),
        link_weight.reshape(32, 1, 1024),
        diag_weight.reshape(32, 1, 1024),
        before_y.reshape(34, 32, 128),
        after_y.reshape(34, 32, 128),
        before_x,
        after_x,
    )

    listed = block_lists.reshape(devices, 128, 2)
    row_block = listed[:, :, 0]
    col_block = listed[:, :, 1]
    owner_ids = row_block // members * members + col_block // groups
    local_block = row_block % members * groups + col_block % groups
    panel_place = arrivals(owner_ids, local_block, group * members)
    key = jnp.where(panel_place[:, None] < 0, -1, panel_place[:, None] * 16 + jnp.arange(16)[None, :])
    front_rows = front_rows_of(key.reshape(1, 4096), outgoing, base_front, base_rows)

    outgoing, lead, front_rows, owner_ids, local_block = lax.optimization_barrier(
        (outgoing, lead, front_rows, owner_ids, local_block)
    )
    received = lax.all_to_all(
        outgoing.reshape(devices, 2, 128, 128), ("grp", "sub"), split_axis=0, concat_axis=0, tiled=True
    ).reshape(256, 128, 128)
    place = arrivals(owner_ids, local_block, me)
    lead = lead.astype(F32)
    symmetric = jnp.tril(lead) + jnp.tril(lead, -1).T
    pivot_matrix = symmetric + jnp.diag(jnp.sum(jnp.abs(symmetric), axis=1) + 1.0)
    factor, inverse = pivot_factor(pivot_matrix)
    solved = dot32(front_rows, inverse, NT)
    in_lead = (group == 0) & (member < 4)
    own_factor = lax.dynamic_slice_in_dim(factor, 128 * jnp.minimum(member, 3), 128, 0)
    panel = jnp.where(in_lead, own_factor, solved).astype(BF)
    panel_rows, panel_cols = panel_spread(panel)
    trailing = trailing_front(place, panel_rows, panel_cols, base_front, received)
    return (trailing, panel)


def solution(mesh):
    return jax.shard_map(
        per_device,
        mesh=mesh,
        in_specs=(
            P("grp", "sub", None, None),
            P("grp", "sub", None),
            P("grp", "sub", None),
            P("grp", "sub"),
            P(),
        ),
        out_specs=(P("grp", "sub"), P(("grp", "sub"), None)),
        check_vma=False,
    )
```

```python
import functools

import jax
import jax.numpy as jnp
import numpy as np
from jax import lax
from jax.experimental import pallas as pl
from jax.experimental.pallas import tpu as pltpu
from jax.sharding import PartitionSpec as P

EARLY = 13
NT = (((1,), (1,)), ((), ()))
NN = (((1,), (0,)), ((), ()))
BF = jnp.bfloat16
F32 = jnp.float32


def dot32(a, b, dims):
    return lax.dot_general(a, b, dims, precision=lax.Precision.HIGHEST, preferred_element_type=F32)


def dotb(a, b, dims):
    return lax.dot_general(a, b, dims, preferred_element_type=F32)


def tile_kernel(
    slot_ref, basis_ref, link_ref, diag_ref, before_y_ref, after_y_ref,
    before_x_ref, after_x_ref, stencil_ref, out_ref,
    scaled_t, basis_t, partial, stage, sems, clear_sems,
):
    step = pl.program_id(0)
    gap = jnp.zeros((96, 128), BF)

    def sides(slot, plane):
        first = jnp.concatenate([gap, before_y_ref[plane + 1]], axis=0)
        last = jnp.concatenate([after_y_ref[plane + 1], gap], axis=0)
        scaled_t[slot, :, 0:128] = first.T
        scaled_t[slot, :, 1152:1280] = last.T

    def spread(slot, ring):
        windows = [scaled_t[slot, :, 256 * q:256 * q + 512] for q in range(4)]
        sums = dotb(jnp.concatenate(windows, axis=0), stencil_ref[...], NN)
        for q in range(4):
            partial[ring, :, 256 * q:256 * q + 256] = sums[128 * q:128 * q + 128]

    def copy_out(slot, q, target):
        return pltpu.make_async_copy(stage.at[slot, q], out_ref.at[target], sems.at[slot, q])

    def wait(slot):
        for q in range(4):
            copy_out(slot, q, 0).wait()

    def start(slot, plane):
        for q in range(4):
            copy_out(slot, q, slot_ref[plane * 4 + q]).start()

    def finish(plane, slot, low, mid, high):
        link = link_ref[plane]
        diag = diag_ref[plane]
        for q in range(4):
            cells = slice(256 * q, 256 * q + 256)
            around = partial[low, :, cells] + partial[mid, :, cells] + partial[high, :, cells]
            around = around - scaled_t[slot, :, 128 + 256 * q:384 + 256 * q].astype(F32)
            own = basis_t[slot, :, cells]
            image = diag[:, cells] * own.astype(F32) - link[:, cells] * around
            head = image.astype(BF)
            tail = (image - head.astype(F32)).astype(BF)
            stage[slot, q] = (dotb(own, head, NT) + dotb(own, tail, NT)).astype(BF)

    def clear(n):
        return pltpu.make_async_copy(
            stage.at[0, 0], out_ref.at[64 * (n // 2) + n % 2], clear_sems.at[n]
        )

    @pl.when(step == 0)
    def _():
        stage[0, 0] = jnp.zeros((128, 128), BF)
        for n in range(8):
            clear(n).start()
        for n in range(8):
            clear(n).wait()
        sides(1, -1)
        scaled_t[1, :, 128:1152] = before_x_ref[...].T
        spread(1, 3)

    for u in range(4):
        plane = step * 4 + u
        slot = u % 2
        turned = basis_ref[u].T
        basis_t[slot] = turned
        scaled_t[slot, :, 128:1152] = (turned.astype(F32) * link_ref[plane]).astype(BF)
        sides(slot, plane)
        spread(slot, u)
        if u < 3:
            pl.when(step > 0)(functools.partial(wait, 1 - slot))
        else:
            wait(1 - slot)
        finish(jnp.maximum(plane - 1, 0), 1 - slot, (u + 2) % 4, (u + 3) % 4, u)
        if u == 0:
            pl.when(step > 0)(functools.partial(start, 1 - slot, plane - 1))
        else:
            start(1 - slot, plane - 1)

    @pl.when(step == pl.num_programs(0) - 1)
    def _():
        sides(0, 32)
        scaled_t[0, :, 128:1152] = after_x_ref[...].T
        spread(0, 0)
        wait(1)
        finish(31, 1, 2, 3, 0)
        start(1, 31)
        wait(0)
        wait(1)


def galerkin_tiles(slots, basis, link, diag, before_y, after_y, before_x, after_x):
    k = np.arange(512)[:, None]
    n = np.arange(256)[None, :]
    near = (abs(k // 32 - 4 - n // 32) <= 1) & (abs(k % 32 - n % 32) <= 1)
    stencil = jnp.asarray(near.astype(np.float32), BF)
    cube = lambda t, s: (0, 0, 0)
    flat = lambda t, s: (0, 0)
    return pl.pallas_call(
        tile_kernel,
        out_shape=jax.ShapeDtypeStruct((256, 128, 128), BF),
        grid_spec=pltpu.PrefetchScalarGridSpec(
            num_scalar_prefetch=1,
            grid=(8,),
            in_specs=[
                pl.BlockSpec((4, 1024, 128), lambda t, s: (t, 0, 0)),
                pl.BlockSpec((32, 1, 1024), cube),
                pl.BlockSpec((32, 1, 1024), cube),
                pl.BlockSpec((34, 32, 128), cube),
                pl.BlockSpec((34, 32, 128), cube),
                pl.BlockSpec((1024, 128), flat),
                pl.BlockSpec((1024, 128), flat),
                pl.BlockSpec((512, 256), flat),
            ],
            out_specs=pl.BlockSpec(memory_space=pl.ANY),
            scratch_shapes=[
                pltpu.VMEM((2, 128, 1280), BF),
                pltpu.VMEM((2, 128, 1024), BF),
                pltpu.VMEM((4, 128, 1024), F32),
                pltpu.VMEM((2, 4, 128, 128), BF),
                pltpu.SemaphoreType.DMA((2, 4)),
                pltpu.SemaphoreType.DMA((8,)),
            ],
        ),
        compiler_params=pltpu.CompilerParams(
            dimension_semantics=("arbitrary",), vmem_limit_bytes=60 * 2**20
        ),
        name="galerkin_tiles",
    )(slots, basis, link, diag, before_y, after_y, before_x, after_x, stencil)


def factor_kernel(pivot_ref, factor_ref, inverse_ref, work):
    size = pivot_ref.shape[0]
    count = size // 128
    rows = lax.broadcasted_iota(jnp.int32, (128, 128), 0)
    lanes = lax.broadcasted_iota(jnp.int32, (128, 128), 1)
    sub8 = lax.broadcasted_iota(jnp.int32, (8, 128), 0)
    lane8 = lax.broadcasted_iota(jnp.int32, (8, 128), 1)
    all_rows = lax.broadcasted_iota(jnp.int32, (size, 1), 0)
    work[...] = pivot_ref[...]
    factor_ref[...] = jnp.zeros_like(factor_ref)
    inverse_ref[...] = jnp.zeros_like(inverse_ref)

    def one_block(b, carry):
        own = pl.ds(pl.multiple_of(128 * b, 128), 128)
        block = work[own, own]
        parts = [block[8 * i:8 * i + 8] for i in range(16)]
        for panel in range(16):
            cols = []
            for k in range(8):
                lane = slice(8 * panel + k, 8 * panel + k + 1)
                cols.append([jnp.broadcast_to(parts[i][:, lane], (8, 128)) for i in range(panel, 16)])
            for k in range(8):
                lane = 8 * panel + k
                pivot_row = jnp.broadcast_to(parts[panel][k:k + 1], (8, 128))
                pivot_row = jnp.where(lane8 == lane, 1.0, pivot_row)
                inverse = 1.0 / jnp.broadcast_to(cols[k][0][k:k + 1], (8, 128))
                heads = [None] * 8
                for l in range(k + 1, 8):
                    heads[l] = jnp.broadcast_to(cols[l][0][k:k + 1], (8, 128))
                for i in range(panel, 16):
                    ratio = cols[k][i - panel] * inverse
                    clear = lane8 == lane
                    if i == panel:
                        ratio = jnp.where(sub8 > k, ratio, 0.0)
                        clear = clear & (sub8 > k)
                    for l in range(k + 1, 8):
                        cols[l][i - panel] = cols[l][i - panel] - ratio * heads[l]
                    parts[i] = jnp.where(clear, 0.0, parts[i]) - ratio * pivot_row
        full = jnp.concatenate(parts, axis=0)
        pivots = jnp.sum(jnp.where(rows == lanes, full, 0.0), axis=1, keepdims=True)
        scale = 1.0 / jnp.sqrt(pivots)
        upper = jnp.where(rows <= lanes, full * scale, 0.0)
        inv = jnp.where(rows > lanes, full * scale, jnp.where(rows == lanes, scale, 0.0))
        below = dot32(work[:, own], inv, NT)
        below = jnp.where(all_rows >= 128 * b + 128, below, 0.0)
        factor_ref[:, own] = below
        factor_ref[own, own] = upper.T
        inverse_ref[own, own] = inv
        work[...] = work[...] - dot32(below, below, NT)
        return carry

    lax.fori_loop(0, count, one_block, 0)
    for b in range(1, count):
        own = slice(128 * b, 128 * b + 128)
        left = slice(0, 128 * b)
        product = dot32(factor_ref[own, left], inverse_ref[left, left], NN)
        inverse_ref[own, left] = -dot32(inverse_ref[own, own], product, NN)


def pivot_factor(pivot_matrix):
    size = pivot_matrix.shape[0]
    return pl.pallas_call(
        factor_kernel,
        out_shape=[jax.ShapeDtypeStruct((size, size), F32)] * 2,
        in_specs=[pl.BlockSpec(memory_space=pltpu.VMEM)],
        out_specs=[pl.BlockSpec(memory_space=pltpu.VMEM)] * 2,
        scratch_shapes=[pltpu.VMEM((size, size), F32)],
        compiler_params=pltpu.CompilerParams(vmem_limit_bytes=32 * 2**20),
        name="pivot_factor",
    )(pivot_matrix)


def final_kernel(
    place_ref, order_ref, start_ref, row_ref, col_ref, base_ref, received_ref, out_ref, sums
):
    step = pl.program_id(0)
    group = lax.axis_index("grp")
    member = lax.axis_index("sub")
    first_row = group * 4096 + step * 512
    col_start = member * 512
    live = (member > 0) & (first_row + 511 >= col_start)

    @pl.when(live)
    def _():
        sums[...] = jnp.zeros_like(sums)

        def add(k, carry):
            slot = order_ref[k]
            place = place_ref[slot] - 16 * step
            sums[place] = sums[place] + received_ref[slot].astype(F32)
            return carry

        lax.fori_loop(start_ref[step], start_ref[step + 1], add, 0)
        update = dotb(row_ref[...], col_ref[...], NT)
        rows = first_row + lax.broadcasted_iota(jnp.int32, (128, 128), 0)
        cols = col_start + lax.broadcasted_iota(jnp.int32, (128, 128), 1)
        for i in range(4):
            for j in range(4):
                r = slice(128 * i, 128 * i + 128)
                c = slice(128 * j, 128 * j + 128)
                value = base_ref[r, c].astype(F32) + sums[i * 4 + j] - update[r, c]
                out_ref[r, c] = jnp.where(rows + 128 * i >= cols + 128 * j, value, 0.0)

    @pl.when(jnp.logical_not(live))
    def _():
        out_ref[...] = jnp.zeros_like(out_ref)


def trailing_front(place, panel_rows, panel_cols, base, received):
    key = jnp.where(place < 0, 1 << 20, place)
    ids = jnp.arange(256, dtype=jnp.int32)
    before = (key[None, :] < key[:, None]) | (
        (key[None, :] == key[:, None]) & (ids[None, :] < ids[:, None])
    )
    rank = jnp.sum(before.astype(jnp.int32), axis=1)
    order = jnp.sum(jnp.where(rank[:, None] == ids[None, :], ids[:, None], 0), axis=0)
    edges = 16 * jnp.arange(9, dtype=jnp.int32)
    starts = jnp.sum((key[None, :] < edges[:, None]).astype(jnp.int32), axis=1)
    once = pl.Buffered(1)
    return pl.pallas_call(
        final_kernel,
        out_shape=jax.ShapeDtypeStruct((4096, 512), F32),
        grid_spec=pltpu.PrefetchScalarGridSpec(
            num_scalar_prefetch=3,
            grid=(8,),
            in_specs=[
                pl.BlockSpec((512, 512), lambda t, *_: (t, 0)),
                pl.BlockSpec((512, 512), lambda t, *_: (0, 0), pipeline_mode=once),
                pl.BlockSpec((512, 512), lambda t, *_: (t, 0)),
                pl.BlockSpec((256, 128, 128), lambda t, *_: (0, 0, 0), pipeline_mode=once),
            ],
            out_specs=pl.BlockSpec((512, 512), lambda t, *_: (t, 0)),
            scratch_shapes=[pltpu.VMEM((16, 128, 128), F32)],
        ),
        compiler_params=pltpu.CompilerParams(
            dimension_semantics=("arbitrary",), vmem_limit_bytes=60 * 2**20
        ),
        name="trailing_front",
    )(place, order, starts, panel_rows, panel_cols, base, received)


def at(group, member):
    return {"grp": group, "sub": member}


def opening_kernel(
    high_x, low_x, high_y, low_y, base_ref,
    before_x, after_x, before_y, after_y, lead_ref, rows_ref,
    halo_send, halo_recv, lead_send, lead_recv, base_send, base_recv, own_sem,
):
    groups, members = 4, 32
    group = lax.axis_index("grp")
    member = lax.axis_index("sub")
    barrier = pltpu.get_barrier_semaphore()
    sides = [(dg, ds) for dg in (-1, 0, 1) for ds in (-1, 0, 1) if (dg, ds) != (0, 0)]

    def exists(dg, ds):
        g, s = group + dg, member + ds
        return (g >= 0) & (g < groups) & (s >= 0) & (s < members)

    def greet(d, carry):
        pl.semaphore_signal(barrier, 1, device_id=at(group, lax.rem(member + d, members)))
        return carry

    lax.fori_loop(1, members, greet, 0)
    for d in range(1, groups):
        pl.semaphore_signal(barrier, 1, device_id=at(lax.rem(group + d, groups), member))
    for dg, ds in sides:
        if dg and ds:
            @pl.when(exists(dg, ds))
            def _():
                pl.semaphore_signal(barrier, 1, device_id=at(group + dg, member + ds))

    near_groups = 2 - jnp.where(group == 0, 1, 0) - jnp.where(group == groups - 1, 1, 0)
    near_members = 2 - jnp.where(member == 0, 1, 0) - jnp.where(member == members - 1, 1, 0)
    pl.semaphore_wait(barrier, members - 1 + groups - 1 + near_groups * near_members)

    def piece(m):
        return pl.ds(pl.multiple_of(16 * m, 16), 16)

    def lead_copy(source, m, k, g, s):
        return pltpu.make_async_remote_copy(
            source.at[piece(m)], lead_ref.at[piece(m)], lead_send.at[k], lead_recv.at[m],
            device_id=at(g, s),
        )

    def base_copy(m):
        rows = pl.ds(pl.multiple_of(128 * m, 128), 128)
        return pltpu.make_async_remote_copy(
            base_ref.at[rows], rows_ref, base_send.at[m], base_recv, device_id=at(group, m)
        )

    own_lead = pltpu.make_async_copy(base_ref.at[pl.ds(0, 16)], lead_ref.at[pl.ds(0, 16)], own_sem.at[0])
    own_rows = pltpu.make_async_copy(base_ref.at[pl.ds(0, 128)], rows_ref, own_sem.at[1])
    root = (group == 0) & (member == 0)

    @pl.when(root)
    def _():
        own_lead.start()

        def send(m, carry):
            lead_copy(base_ref, m, m, 0, m).start()
            return carry

        lax.fori_loop(1, members, send, 0)

    def halo(dg, ds):
        k = sides.index((dg, ds))
        if ds == 0:
            source, target = (high_x, before_x) if dg == 1 else (low_x, after_x)
        else:
            if dg == 0:
                source = high_y if ds == 1 else low_y
                place = pl.ds(32, 1024)
            else:
                face = high_x if dg == 1 else low_x
                source = face.at[pl.ds(992 if ds == 1 else 0, 32)]
                place = pl.ds(0 if dg == 1 else 1056, 32)
            target = (before_y if ds == 1 else after_y).at[place]
        return pltpu.make_async_remote_copy(
            source, target, halo_send.at[k], halo_recv.at[k], device_id=at(group + dg, member + ds)
        )

    for dg, ds in sides:
        @pl.when(exists(dg, ds))
        def _():
            halo(dg, ds).start()

        @pl.when(jnp.logical_not(exists(-dg, -ds)))
        def _():
            if ds == 0:
                target = before_x if dg == 1 else after_x
                target[...] = jnp.zeros_like(target)
            else:
                target = before_y if ds == 1 else after_y
                place = pl.ds(32, 1024) if dg == 0 else pl.ds(0 if dg == 1 else 1056, 32)
                target[place, :] = jnp.zeros((1024 if dg == 0 else 32, 128), BF)

    @pl.when(member == 0)
    def _():
        own_rows.start()

        def send(m, carry):
            base_copy(m).start()
            return carry

        lax.fori_loop(1, EARLY, send, 0)

    @pl.when(root)
    def _():
        own_lead.wait()

    @pl.when(jnp.logical_not(root))
    def _():
        lead_copy(lead_ref, member, 0, group, member).wait_recv()

    @pl.when(group == 0)
    def _():
        for g in range(1, groups):
            lead_copy(lead_ref, member, 64 + g, g, member).start()

    def spread(d, carry):
        lead_copy(lead_ref, member, 32 + d, group, lax.rem(member + d, members)).start()
        return carry

    lax.fori_loop(1, members, spread, 0)

    for dg, ds in sides:
        @pl.when(exists(-dg, -ds))
        def _():
            halo(dg, ds).wait_recv()

        @pl.when(exists(dg, ds))
        def _():
            halo(dg, ds).wait_send()

    def gather(d, carry):
        lead_copy(lead_ref, lax.rem(member + d, members), 0, group, member).wait_recv()
        lead_copy(lead_ref, member, 32 + d, group, member).wait_send()
        return carry

    lax.fori_loop(1, members, gather, 0)

    @pl.when(group == 0)
    def _():
        for g in range(1, groups):
            lead_copy(lead_ref, member, 64 + g, g, member).wait_send()

    @pl.when(root)
    def _():
        def sent(m, carry):
            lead_copy(base_ref, m, m, 0, m).wait_send()
            return carry

        lax.fori_loop(1, members, sent, 0)

    @pl.when(member == 0)
    def _():
        def sent(m, carry):
            base_copy(m).wait_send()
            return carry

        lax.fori_loop(1, EARLY, sent, 0)
        own_rows.wait()

    @pl.when((member > 0) & (member < EARLY))
    def _():
        base_copy(member).wait_recv()


def opening(high_x, low_x, high_y, low_y, base_front):
    vmem = pl.BlockSpec(memory_space=pltpu.VMEM)
    dma = pltpu.SemaphoreType.DMA
    return pl.pallas_call(
        opening_kernel,
        out_shape=[
            jax.ShapeDtypeStruct((1024, 128), BF),
            jax.ShapeDtypeStruct((1024, 128), BF),
            jax.ShapeDtypeStruct((1088, 128), BF),
            jax.ShapeDtypeStruct((1088, 128), BF),
            jax.ShapeDtypeStruct((512, 512), BF),
            jax.ShapeDtypeStruct((128, 512), BF),
        ],
        in_specs=[vmem] * 4 + [pl.BlockSpec(memory_space=pl.ANY)],
        out_specs=[vmem] * 6,
        scratch_shapes=[
            dma((8,)), dma((8,)), dma((68,)), dma((32,)), dma((32,)), dma, dma((2,)),
        ],
        compiler_params=pltpu.CompilerParams(
            collective_id=0, has_side_effects=True, vmem_limit_bytes=60 * 2**20
        ),
        name="opening",
    )(high_x, low_x, high_y, low_y, base_front)


def front_kernel(
    key_ref, tiles_ref, base_front_ref, early_ref, front_ref, strips, sums, added, late,
    strip_send, strip_recv, sum_send, sum_recv, base_send, base_recv, own_sem,
):
    groups, members, devices, parts, base = 4, 32, 128, 8, 8
    group = lax.axis_index("grp")
    member = lax.axis_index("sub")
    me = group * members + member
    takes = (member >= base) & (member < base + parts)
    barrier = pltpu.get_barrier_semaphore()

    @pl.when(takes)
    def _():
        def greet(d, carry):
            other = lax.rem(me + d, devices)
            pl.semaphore_signal(barrier, 1, device_id=at(other // members, lax.rem(other, members)))
            return carry

        lax.fori_loop(1, devices, greet, 0)

    @pl.when(jnp.logical_not(takes))
    def _():
        for r in range(parts):
            pl.semaphore_signal(barrier, 1, device_id=at(group, base + r))

    @pl.when(jnp.logical_not(takes) & (member > 0))
    def _():
        pl.semaphore_signal(barrier, 1, device_id=at(group, 0))

    pl.semaphore_wait(
        barrier, groups * parts + jnp.where(takes | (member == 0), members - parts - 1, 0)
    )

    def source(g, r):
        first = pl.ds(2 * members * g, 2)
        return tiles_ref.at[first, pl.ds(pl.multiple_of(16 * r, 16), 16)]

    def strip_copy(sender, g, r, k):
        return pltpu.make_async_remote_copy(
            source(g, r), strips.at[pl.ds(2 * sender, 2)], strip_send.at[k], strip_recv.at[sender],
            device_id=at(g, base + r),
        )

    own_rank = lax.rem(member, parts)
    own_strip = pltpu.make_async_copy(
        source(group, own_rank), strips.at[pl.ds(2 * me, 2)], own_sem.at[0]
    )

    def target(j):
        t = lax.rem(j + group * parts + own_rank, groups * parts)
        return t // parts, lax.rem(t, parts)

    def start_strip(j, carry):
        g, r = target(j)

        @pl.when((g != group) | (base + r != member))
        def _():
            strip_copy(me, g, r, j).start()

        return carry

    lax.fori_loop(0, groups * parts, start_strip, 0)

    def base_copy(m):
        rows = pl.ds(pl.multiple_of(128 * m, 128), 128)
        return pltpu.make_async_remote_copy(
            base_front_ref.at[rows], late, base_send.at[m], base_recv, device_id=at(group, m)
        )

    @pl.when(member == 0)
    def _():
        def send(m, carry):
            base_copy(m).start()
            return carry

        lax.fori_loop(EARLY, members, send, 0)

    def sum_copy(r, a):
        return pltpu.make_async_remote_copy(
            sums.at[pl.ds(4 * a, 4)], added.at[r], sum_send.at[a], sum_recv.at[r],
            device_id=at(group, a),
        )

    own_sum = pltpu.make_async_copy(
        sums.at[pl.ds(4 * member, 4)],
        added.at[own_rank],
        own_sem.at[1],
    )

    @pl.when(takes)
    def _():
        own_strip.start()

        def arrive(d, carry):
            strip_copy(lax.rem(me + d, devices), group, own_rank, 0).wait_recv()
            return carry

        lax.fori_loop(1, devices, arrive, 0)
        own_strip.wait()
        rows = strips[...].reshape(4096, 128)
        for n in range(8):
            ids = 256 * n + lax.broadcasted_iota(jnp.int32, (256, 4096), 0)
            pick = jnp.where(key_ref[...] == ids, 1.0, 0.0).astype(BF)
            sums[16 * n:16 * n + 16] = dotb(pick, rows, NN).astype(BF).reshape(16, 16, 128)

        def send(d, carry):
            sum_copy(own_rank, lax.rem(member + d, members)).start()
            return carry

        lax.fori_loop(1, members, send, 0)
        own_sum.start()

    for r in range(parts):
        @pl.when(member != base + r)
        def _():
            sum_copy(r, member).wait_recv()

    @pl.when(takes)
    def _():
        own_sum.wait()

    def summed(q):
        return jnp.concatenate([added[r, q] for r in range(parts)], axis=0).astype(F32)

    @pl.when(member < EARLY)
    def _():
        for q in range(4):
            cols = slice(128 * q, 128 * q + 128)
            front_ref[:, cols] = early_ref[:, cols].astype(F32) + summed(q)

    @pl.when(member >= EARLY)
    def _():
        base_copy(member).wait_recv()
        for q in range(4):
            cols = slice(128 * q, 128 * q + 128)
            front_ref[:, cols] = late[:, cols].astype(F32) + summed(q)

    def sent_strip(j, carry):
        g, r = target(j)

        @pl.when((g != group) | (base + r != member))
        def _():
            strip_copy(me, g, r, j).wait_send()

        return carry

    lax.fori_loop(0, groups * parts, sent_strip, 0)

    @pl.when(takes)
    def _():
        def sent(d, carry):
            sum_copy(own_rank, lax.rem(member + d, members)).wait_send()
            return carry

        lax.fori_loop(1, members, sent, 0)

    @pl.when(member == 0)
    def _():
        def sent(m, carry):
            base_copy(m).wait_send()
            return carry

        lax.fori_loop(EARLY, members, sent, 0)


def front_rows_of(key, tiles, base_front, early):
    dma = pltpu.SemaphoreType.DMA
    anywhere = pl.BlockSpec(memory_space=pl.ANY)
    vmem = pl.BlockSpec(memory_space=pltpu.VMEM)
    return pl.pallas_call(
        front_kernel,
        out_shape=jax.ShapeDtypeStruct((128, 512), F32),
        in_specs=[vmem, anywhere, anywhere, vmem],
        out_specs=vmem,
        scratch_shapes=[
            pltpu.VMEM((256, 16, 128), BF),
            pltpu.VMEM((128, 16, 128), BF),
            pltpu.VMEM((8, 4, 16, 128), BF),
            pltpu.VMEM((128, 512), BF),
            dma((32,)), dma((128,)), dma((32,)), dma((8,)), dma((32,)), dma, dma((2,)),
        ],
        compiler_params=pltpu.CompilerParams(
            collective_id=2, has_side_effects=True, vmem_limit_bytes=60 * 2**20
        ),
        name="front_rows",
    )(key, tiles, base_front, early)


def panel_kernel(
    panel_ref, rows_ref, cols_ref, send, recv, fold_send, fold_recv, col_send, col_recv, own_sem
):
    groups, members, chips = 4, 32, 16
    group = lax.axis_index("grp")
    member = lax.axis_index("sub")
    chip = member // 2
    core = lax.rem(member, 2)
    source_group = member // 8
    barrier = pltpu.get_barrier_semaphore()

    def greet(d, carry):
        pl.semaphore_signal(barrier, 1, device_id=at(group, lax.rem(member + d, members)))
        return carry

    lax.fori_loop(1, members, greet, 0)

    @pl.when(source_group < group)
    def _():
        for i in range(4):
            pl.semaphore_signal(
                barrier, 1, device_id=at(source_group, lax.rem(member, 8) * 4 + i)
            )

    pl.semaphore_wait(barrier, members - 1 + groups - 1 - group)

    def block(m):
        return pl.ds(pl.multiple_of(128 * m, 128), 128)

    def row_copy(m, k, s):
        return pltpu.make_async_remote_copy(
            panel_ref, rows_ref.at[block(m)], send.at[k], recv.at[m // 2], device_id=at(group, s)
        )

    def fold_copy(m, source):
        return pltpu.make_async_remote_copy(
            source, rows_ref.at[block(m)], fold_send.at[m // 2], fold_recv.at[m // 2],
            device_id=at(group, chip * 2 + 1 - core),
        )

    def used(m, c):
        return (c // 4 < group) | ((c // 4 == group) & (m >= 8 * lax.rem(c, 4)))

    def other(d):
        return lax.rem(chip + d, chips) * 2 + core

    target = group * 8 + member // 4
    quarter = lax.rem(member, 4)

    def col_copy(g, q, s):
        return pltpu.make_async_remote_copy(
            panel_ref, cols_ref.at[block(q)], col_send.at[g], col_recv.at[q], device_id=at(g, s)
        )

    def spread(d, carry):
        @pl.when(used(member, other(d) // 2))
        def _():
            row_copy(member, d, other(d)).start()

        return carry

    lax.fori_loop(1, chips, spread, 0)

    for g in range(groups):
        @pl.when((g >= group) & jnp.logical_not((g == group) & (target == member)))
        def _():
            col_copy(g, quarter, target).start()

    own_cols = pltpu.make_async_copy(panel_ref, cols_ref.at[block(quarter)], own_sem.at[0])
    own_rows = pltpu.make_async_copy(panel_ref, rows_ref.at[block(member)], own_sem.at[1])

    @pl.when(target == member)
    def _():
        own_cols.start()

    own_rows.start()

    @pl.when(used(member, chip))
    def _():
        fold_copy(member, panel_ref).start()

    def fold(d, carry):
        m = other(d)

        @pl.when(used(m, chip))
        def _():
            row_copy(m, 0, member).wait_recv()
            fold_copy(m, rows_ref.at[block(m)]).start()

        return carry

    lax.fori_loop(1, chips, fold, 0)

    def folded(d, carry):
        m = lax.rem(chip + d, chips) * 2

        @pl.when(used(m + 1 - core, chip))
        def _():
            fold_copy(m + 1 - core, panel_ref).wait_recv()

        @pl.when(used(m + core, chip))
        def _():
            fold_copy(m + core, panel_ref).wait_send()

        return carry

    lax.fori_loop(0, chips, folded, 0)

    def sent(d, carry):
        @pl.when(used(member, other(d) // 2))
        def _():
            row_copy(member, d, other(d)).wait_send()

        return carry

    lax.fori_loop(1, chips, sent, 0)
    for g in range(groups):
        @pl.when((g >= group) & jnp.logical_not((g == group) & (target == member)))
        def _():
            col_copy(g, quarter, target).wait_send()

    for i in range(4):
        source = lax.rem(member, 8) * 4 + i
        itself = (source_group == group) & (source == member)

        @pl.when((source_group <= group) & jnp.logical_not(itself))
        def _():
            col_copy(group, i, member).wait_recv()

    @pl.when(target == member)
    def _():
        own_cols.wait()

    own_rows.wait()


def panel_spread(panel):
    dma = pltpu.SemaphoreType.DMA
    anywhere = pl.BlockSpec(memory_space=pl.ANY)
    return pl.pallas_call(
        panel_kernel,
        out_shape=[jax.ShapeDtypeStruct((4096, 512), BF), jax.ShapeDtypeStruct((512, 512), BF)],
        in_specs=[pl.BlockSpec(memory_space=pltpu.VMEM)],
        out_specs=[anywhere, anywhere],
        scratch_shapes=[
            dma((16,)), dma((16,)), dma((16,)), dma((16,)), dma((4,)), dma((4,)), dma((2,)),
        ],
        compiler_params=pltpu.CompilerParams(
            collective_id=1, has_side_effects=True, vmem_limit_bytes=60 * 2**20
        ),
        name="panel_spread",
    )(panel)


def arrivals(owner_ids, local_block, owner):
    order = jnp.arange(owner_ids.shape[1], dtype=jnp.int32)[None, :]
    here = owner_ids == owner
    first = jnp.min(jnp.where(here, order, 1 << 20), axis=1, keepdims=True)
    one = jnp.max(jnp.where(here & (order == first), local_block, -1), axis=1)
    two = jnp.max(jnp.where(here & (order > first), local_block, -1), axis=1)
    return jnp.stack([one, two], axis=1).reshape(-1)


def per_device(basis_cols, diag_weight, link_weight, base_front, block_lists):
    groups, members, devices = 4, 32, 128
    group = lax.axis_index("grp")
    member = lax.axis_index("sub")
    me = group * members + member

    def scaled(b, w):
        return (w[..., None] * b.astype(F32)).astype(BF).reshape(1024, 128)

    before_x, after_x, before_y, after_y, lead, base_rows = opening(
        scaled(basis_cols[31], link_weight[31]),
        scaled(basis_cols[0], link_weight[0]),
        scaled(basis_cols[:, 31], link_weight[:, 31]),
        scaled(basis_cols[:, 0], link_weight[:, 0]),
        base_front,
    )

    own_list = lax.dynamic_index_in_dim(block_lists.reshape(devices, 128, 2), me, 0, keepdims=False)
    own_owner = own_list[:, 0] // members * members + own_list[:, 1] // groups
    order = jnp.arange(128)
    rank = jnp.sum(
        (own_owner[:, None] == own_owner[None, :]) & (order[None, :] < order[:, None]), axis=1
    )
    slots = (own_owner * 2 + rank).astype(jnp.int32)

    outgoing = galerkin_tiles(
        slots,
        basis_cols.reshape(32, 1024, 128),
        link_weight.reshape(32, 1, 1024),
        diag_weight.reshape(32, 1, 1024),
        before_y.reshape(34, 32, 128),
        after_y.reshape(34, 32, 128),
        before_x,
        after_x,
    )

    listed = block_lists.reshape(devices, 128, 2)
    row_block = listed[:, :, 0]
    col_block = listed[:, :, 1]
    owner_ids = row_block // members * members + col_block // groups
    local_block = row_block % members * groups + col_block % groups
    panel_place = arrivals(owner_ids, local_block, group * members)
    key = jnp.where(panel_place[:, None] < 0, -1, panel_place[:, None] * 16 + jnp.arange(16)[None, :])
    front_rows = front_rows_of(key.reshape(1, 4096), outgoing, base_front, base_rows)

    outgoing, lead, front_rows, owner_ids, local_block = lax.optimization_barrier(
        (outgoing, lead, front_rows, owner_ids, local_block)
    )
    received = lax.all_to_all(
        outgoing.reshape(devices, 2, 128, 128), ("grp", "sub"), split_axis=0, concat_axis=0, tiled=True
    ).reshape(256, 128, 128)
    place = arrivals(owner_ids, local_block, me)
    lead = lead.astype(F32)
    symmetric = jnp.tril(lead) + jnp.tril(lead, -1).T
    pivot_matrix = symmetric + jnp.diag(jnp.sum(jnp.abs(symmetric), axis=1) + 1.0)
    factor, inverse = pivot_factor(pivot_matrix)
    solved = dot32(front_rows, inverse, NT)
    in_lead = (group == 0) & (member < 4)
    own_factor = lax.dynamic_slice_in_dim(factor, 128 * jnp.minimum(member, 3), 128, 0)
    panel = jnp.where(in_lead, own_factor, solved).astype(BF)
    panel_rows, panel_cols = panel_spread(panel)
    trailing = trailing_front(place, panel_rows, panel_cols, base_front, received)
    return (trailing, panel)


def solution(mesh):
    return jax.shard_map(
        per_device,
        mesh=mesh,
        in_specs=(
            P("grp", "sub", None, None),
            P("grp", "sub", None),
            P("grp", "sub", None),
            P("grp", "sub"),
            P(),
        ),
        out_specs=(P("grp", "sub"), P(("grp", "sub"), None)),
        check_vma=False,
    )
```

```python
import functools

import jax
import jax.numpy as jnp
import numpy as np
from jax import lax
from jax.experimental import pallas as pl
from jax.experimental.pallas import tpu as pltpu
from jax.sharding import PartitionSpec as P

EARLY = 13
NT = (((1,), (1,)), ((), ()))
NN = (((1,), (0,)), ((), ()))
BF = jnp.bfloat16
F32 = jnp.float32


def dot32(a, b, dims):
    return lax.dot_general(a, b, dims, precision=lax.Precision.HIGHEST, preferred_element_type=F32)


def dotb(a, b, dims):
    return lax.dot_general(a, b, dims, preferred_element_type=F32)


def tile_kernel(
    slot_ref, basis_ref, link_ref, diag_ref, before_y_ref, after_y_ref,
    before_x_ref, after_x_ref, stencil_ref, out_ref,
    scaled_t, basis_t, partial, stage, sems, clear_sems,
):
    step = pl.program_id(0)
    gap = jnp.zeros((96, 128), BF)

    def sides(slot, plane):
        first = jnp.concatenate([gap, before_y_ref[plane + 1]], axis=0)
        last = jnp.concatenate([after_y_ref[plane + 1], gap], axis=0)
        scaled_t[slot, :, 0:128] = first.T
        scaled_t[slot, :, 1152:1280] = last.T

    def spread(slot, ring):
        windows = [scaled_t[slot, :, 256 * q:256 * q + 512] for q in range(4)]
        sums = dotb(jnp.concatenate(windows, axis=0), stencil_ref[...], NN)
        for q in range(4):
            partial[ring, :, 256 * q:256 * q + 256] = sums[128 * q:128 * q + 128]

    def copy_out(slot, q, target):
        return pltpu.make_async_copy(stage.at[slot, q], out_ref.at[target], sems.at[slot, q])

    def wait(slot):
        for q in range(4):
            copy_out(slot, q, 0).wait()

    def start(slot, plane):
        for q in range(4):
            copy_out(slot, q, slot_ref[plane * 4 + q]).start()

    def finish(plane, slot, low, mid, high):
        link = link_ref[plane]
        diag = diag_ref[plane]
        for q in range(4):
            cells = slice(256 * q, 256 * q + 256)
            around = partial[low, :, cells] + partial[mid, :, cells] + partial[high, :, cells]
            around = around - scaled_t[slot, :, 128 + 256 * q:384 + 256 * q].astype(F32)
            own = basis_t[slot, :, cells]
            image = diag[:, cells] * own.astype(F32) - link[:, cells] * around
            head = image.astype(BF)
            tail = (image - head.astype(F32)).astype(BF)
            stage[slot, q] = (dotb(own, head, NT) + dotb(own, tail, NT)).astype(BF)

    def clear(n):
        return pltpu.make_async_copy(
            stage.at[0, 0], out_ref.at[64 * (n // 2) + n % 2], clear_sems.at[n]
        )

    @pl.when(step == 0)
    def _():
        stage[0, 0] = jnp.zeros((128, 128), BF)
        for n in range(8):
            clear(n).start()
        for n in range(8):
            clear(n).wait()
        sides(1, -1)
        scaled_t[1, :, 128:1152] = before_x_ref[...].T
        spread(1, 3)

    for u in range(4):
        plane = step * 4 + u
        slot = u % 2
        turned = basis_ref[u].T
        basis_t[slot] = turned
        scaled_t[slot, :, 128:1152] = (turned.astype(F32) * link_ref[plane]).astype(BF)
        sides(slot, plane)
        spread(slot, u)
        if u < 3:
            pl.when(step > 0)(functools.partial(wait, 1 - slot))
        else:
            wait(1 - slot)
        finish(jnp.maximum(plane - 1, 0), 1 - slot, (u + 2) % 4, (u + 3) % 4, u)
        if u == 0:
            pl.when(step > 0)(functools.partial(start, 1 - slot, plane - 1))
        else:
            start(1 - slot, plane - 1)

    @pl.when(step == pl.num_programs(0) - 1)
    def _():
        sides(0, 32)
        scaled_t[0, :, 128:1152] = after_x_ref[...].T
        spread(0, 0)
        wait(1)
        finish(31, 1, 2, 3, 0)
        start(1, 31)
        wait(0)
        wait(1)


def galerkin_tiles(slots, basis, link, diag, before_y, after_y, before_x, after_x):
    k = np.arange(512)[:, None]
    n = np.arange(256)[None, :]
    near = (abs(k // 32 - 4 - n // 32) <= 1) & (abs(k % 32 - n % 32) <= 1)
    stencil = jnp.asarray(near.astype(np.float32), BF)
    cube = lambda t, s: (0, 0, 0)
    flat = lambda t, s: (0, 0)
    return pl.pallas_call(
        tile_kernel,
        out_shape=jax.ShapeDtypeStruct((256, 128, 128), BF),
        grid_spec=pltpu.PrefetchScalarGridSpec(
            num_scalar_prefetch=1,
            grid=(8,),
            in_specs=[
                pl.BlockSpec((4, 1024, 128), lambda t, s: (t, 0, 0)),
                pl.BlockSpec((32, 1, 1024), cube),
                pl.BlockSpec((32, 1, 1024), cube),
                pl.BlockSpec((34, 32, 128), cube),
                pl.BlockSpec((34, 32, 128), cube),
                pl.BlockSpec((1024, 128), flat),
                pl.BlockSpec((1024, 128), flat),
                pl.BlockSpec((512, 256), flat),
            ],
            out_specs=pl.BlockSpec(memory_space=pl.ANY),
            scratch_shapes=[
                pltpu.VMEM((2, 128, 1280), BF),
                pltpu.VMEM((2, 128, 1024), BF),
                pltpu.VMEM((4, 128, 1024), F32),
                pltpu.VMEM((2, 4, 128, 128), BF),
                pltpu.SemaphoreType.DMA((2, 4)),
                pltpu.SemaphoreType.DMA((8,)),
            ],
        ),
        compiler_params=pltpu.CompilerParams(
            dimension_semantics=("arbitrary",), vmem_limit_bytes=60 * 2**20
        ),
        name="galerkin_tiles",
    )(slots, basis, link, diag, before_y, after_y, before_x, after_x, stencil)


def factor_kernel(pivot_ref, factor_ref, inverse_ref, work):
    size = pivot_ref.shape[0]
    count = size // 128
    rows = lax.broadcasted_iota(jnp.int32, (128, 128), 0)
    lanes = lax.broadcasted_iota(jnp.int32, (128, 128), 1)
    sub8 = lax.broadcasted_iota(jnp.int32, (8, 128), 0)
    lane8 = lax.broadcasted_iota(jnp.int32, (8, 128), 1)
    all_rows = lax.broadcasted_iota(jnp.int32, (size, 1), 0)
    work[...] = pivot_ref[...]
    factor_ref[...] = jnp.zeros_like(factor_ref)
    inverse_ref[...] = jnp.zeros_like(inverse_ref)

    def one_block(b, carry):
        own = pl.ds(pl.multiple_of(128 * b, 128), 128)
        block = work[own, own]
        parts = [block[8 * i:8 * i + 8] for i in range(16)]
        for panel in range(16):
            cols = []
            for k in range(8):
                lane = slice(8 * panel + k, 8 * panel + k + 1)
                cols.append([jnp.broadcast_to(parts[i][:, lane], (8, 128)) for i in range(panel, 16)])
            for k in range(8):
                lane = 8 * panel + k
                pivot_row = jnp.broadcast_to(parts[panel][k:k + 1], (8, 128))
                pivot_row = jnp.where(lane8 == lane, 1.0, pivot_row)
                inverse = 1.0 / jnp.broadcast_to(cols[k][0][k:k + 1], (8, 128))
                heads = [None] * 8
                for l in range(k + 1, 8):
                    heads[l] = jnp.broadcast_to(cols[l][0][k:k + 1], (8, 128))
                for i in range(panel, 16):
                    ratio = cols[k][i - panel] * inverse
                    clear = lane8 == lane
                    if i == panel:
                        ratio = jnp.where(sub8 > k, ratio, 0.0)
                        clear = clear & (sub8 > k)
                    for l in range(k + 1, 8):
                        cols[l][i - panel] = cols[l][i - panel] - ratio * heads[l]
                    parts[i] = jnp.where(clear, 0.0, parts[i]) - ratio * pivot_row
        full = jnp.concatenate(parts, axis=0)
        pivots = jnp.sum(jnp.where(rows == lanes, full, 0.0), axis=1, keepdims=True)
        scale = 1.0 / jnp.sqrt(pivots)
        upper = jnp.where(rows <= lanes, full * scale, 0.0)
        inv = jnp.where(rows > lanes, full * scale, jnp.where(rows == lanes, scale, 0.0))
        below = dot32(work[:, own], inv, NT)
        below = jnp.where(all_rows >= 128 * b + 128, below, 0.0)
        factor_ref[:, own] = below
        factor_ref[own, own] = upper.T
        inverse_ref[own, own] = inv
        work[...] = work[...] - dot32(below, below, NT)
        return carry

    lax.fori_loop(0, count, one_block, 0)
    for b in range(1, count):
        own = slice(128 * b, 128 * b + 128)
        left = slice(0, 128 * b)
        product = dot32(factor_ref[own, left], inverse_ref[left, left], NN)
        inverse_ref[own, left] = -dot32(inverse_ref[own, own], product, NN)


def pivot_factor(pivot_matrix):
    size = pivot_matrix.shape[0]
    return pl.pallas_call(
        factor_kernel,
        out_shape=[jax.ShapeDtypeStruct((size, size), F32)] * 2,
        in_specs=[pl.BlockSpec(memory_space=pltpu.VMEM)],
        out_specs=[pl.BlockSpec(memory_space=pltpu.VMEM)] * 2,
        scratch_shapes=[pltpu.VMEM((size, size), F32)],
        compiler_params=pltpu.CompilerParams(vmem_limit_bytes=32 * 2**20),
        name="pivot_factor",
    )(pivot_matrix)


def final_kernel(
    place_ref, order_ref, start_ref, row_ref, col_ref, base_ref, received_ref, out_ref, sums
):
    step = pl.program_id(0)
    group = lax.axis_index("grp")
    member = lax.axis_index("sub")
    first_row = group * 4096 + step * 512
    col_start = member * 512
    live = (member > 0) & (first_row + 511 >= col_start)

    @pl.when(live)
    def _():
        sums[...] = jnp.zeros_like(sums)

        def add(k, carry):
            slot = order_ref[k]
            place = place_ref[slot] - 16 * step
            sums[place] = sums[place] + received_ref[slot].astype(F32)
            return carry

        lax.fori_loop(start_ref[step], start_ref[step + 1], add, 0)
        update = dotb(row_ref[...], col_ref[...], NT)
        rows = first_row + lax.broadcasted_iota(jnp.int32, (128, 128), 0)
        cols = col_start + lax.broadcasted_iota(jnp.int32, (128, 128), 1)
        for i in range(4):
            for j in range(4):
                r = slice(128 * i, 128 * i + 128)
                c = slice(128 * j, 128 * j + 128)
                value = base_ref[r, c].astype(F32) + sums[i * 4 + j] - update[r, c]
                out_ref[r, c] = jnp.where(rows + 128 * i >= cols + 128 * j, value, 0.0)

    @pl.when(jnp.logical_not(live))
    def _():
        out_ref[...] = jnp.zeros_like(out_ref)


def trailing_front(place, panel_rows, panel_cols, base, received):
    key = jnp.where(place < 0, 1 << 20, place)
    ids = jnp.arange(256, dtype=jnp.int32)
    before = (key[None, :] < key[:, None]) | (
        (key[None, :] == key[:, None]) & (ids[None, :] < ids[:, None])
    )
    rank = jnp.sum(before.astype(jnp.int32), axis=1)
    order = jnp.sum(jnp.where(rank[:, None] == ids[None, :], ids[:, None], 0), axis=0)
    edges = 16 * jnp.arange(9, dtype=jnp.int32)
    starts = jnp.sum((key[None, :] < edges[:, None]).astype(jnp.int32), axis=1)
    once = pl.Buffered(1)
    return pl.pallas_call(
        final_kernel,
        out_shape=jax.ShapeDtypeStruct((4096, 512), F32),
        grid_spec=pltpu.PrefetchScalarGridSpec(
            num_scalar_prefetch=3,
            grid=(8,),
            in_specs=[
                pl.BlockSpec((512, 512), lambda t, *_: (t, 0)),
                pl.BlockSpec((512, 512), lambda t, *_: (0, 0), pipeline_mode=once),
                pl.BlockSpec((512, 512), lambda t, *_: (t, 0)),
                pl.BlockSpec((256, 128, 128), lambda t, *_: (0, 0, 0), pipeline_mode=once),
            ],
            out_specs=pl.BlockSpec((512, 512), lambda t, *_: (t, 0)),
            scratch_shapes=[pltpu.VMEM((16, 128, 128), F32)],
        ),
        compiler_params=pltpu.CompilerParams(
            dimension_semantics=("arbitrary",), vmem_limit_bytes=60 * 2**20
        ),
        name="trailing_front",
    )(place, order, starts, panel_rows, panel_cols, base, received)


def at(group, member):
    return {"grp": group, "sub": member}


def opening_kernel(
    high_x, low_x, high_y, low_y, base_ref,
    before_x, after_x, before_y, after_y, lead_ref, rows_ref,
    halo_send, halo_recv, lead_send, lead_recv, base_send, base_recv, own_sem,
):
    groups, members = 4, 32
    group = lax.axis_index("grp")
    member = lax.axis_index("sub")
    barrier = pltpu.get_barrier_semaphore()
    sides = [(dg, ds) for dg in (-1, 0, 1) for ds in (-1, 0, 1) if (dg, ds) != (0, 0)]

    def exists(dg, ds):
        g, s = group + dg, member + ds
        return (g >= 0) & (g < groups) & (s >= 0) & (s < members)

    def greet(d, carry):
        pl.semaphore_signal(barrier, 1, device_id=at(group, lax.rem(member + d, members)))
        return carry

    lax.fori_loop(1, members, greet, 0)
    for d in range(1, groups):
        pl.semaphore_signal(barrier, 1, device_id=at(lax.rem(group + d, groups), member))
    for dg, ds in sides:
        if dg and ds:
            @pl.when(exists(dg, ds))
            def _():
                pl.semaphore_signal(barrier, 1, device_id=at(group + dg, member + ds))

    near_groups = 2 - jnp.where(group == 0, 1, 0) - jnp.where(group == groups - 1, 1, 0)
    near_members = 2 - jnp.where(member == 0, 1, 0) - jnp.where(member == members - 1, 1, 0)
    pl.semaphore_wait(barrier, members - 1 + groups - 1 + near_groups * near_members)

    def piece(m):
        return pl.ds(pl.multiple_of(16 * m, 16), 16)

    def lead_copy(source, m, k, g, s):
        return pltpu.make_async_remote_copy(
            source.at[piece(m)], lead_ref.at[piece(m)], lead_send.at[k], lead_recv.at[m],
            device_id=at(g, s),
        )

    def base_copy(m):
        rows = pl.ds(pl.multiple_of(128 * m, 128), 128)
        return pltpu.make_async_remote_copy(
            base_ref.at[rows], rows_ref, base_send.at[m], base_recv, device_id=at(group, m)
        )

    own_lead = pltpu.make_async_copy(base_ref.at[pl.ds(0, 16)], lead_ref.at[pl.ds(0, 16)], own_sem.at[0])
    own_rows = pltpu.make_async_copy(base_ref.at[pl.ds(0, 128)], rows_ref, own_sem.at[1])
    root = (group == 0) & (member == 0)

    @pl.when(root)
    def _():
        own_lead.start()

        def send(m, carry):
            lead_copy(base_ref, m, m, 0, m).start()
            return carry

        lax.fori_loop(1, members, send, 0)

    def halo(dg, ds):
        k = sides.index((dg, ds))
        if ds == 0:
            source, target = (high_x, before_x) if dg == 1 else (low_x, after_x)
        else:
            if dg == 0:
                source = high_y if ds == 1 else low_y
                place = pl.ds(32, 1024)
            else:
                face = high_x if dg == 1 else low_x
                source = face.at[pl.ds(992 if ds == 1 else 0, 32)]
                place = pl.ds(0 if dg == 1 else 1056, 32)
            target = (before_y if ds == 1 else after_y).at[place]
        return pltpu.make_async_remote_copy(
            source, target, halo_send.at[k], halo_recv.at[k], device_id=at(group + dg, member + ds)
        )

    for dg, ds in sides:
        @pl.when(exists(dg, ds))
        def _():
            halo(dg, ds).start()

        @pl.when(jnp.logical_not(exists(-dg, -ds)))
        def _():
            if ds == 0:
                target = before_x if dg == 1 else after_x
                target[...] = jnp.zeros_like(target)
            else:
                target = before_y if ds == 1 else after_y
                place = pl.ds(32, 1024) if dg == 0 else pl.ds(0 if dg == 1 else 1056, 32)
                target[place, :] = jnp.zeros((1024 if dg == 0 else 32, 128), BF)

    @pl.when(member == 0)
    def _():
        own_rows.start()

        def send(m, carry):
            base_copy(m).start()
            return carry

        lax.fori_loop(1, EARLY, send, 0)

    @pl.when(root)
    def _():
        own_lead.wait()

    @pl.when(jnp.logical_not(root))
    def _():
        lead_copy(lead_ref, member, 0, group, member).wait_recv()

    @pl.when(group == 0)
    def _():
        for g in range(1, groups):
            lead_copy(lead_ref, member, 64 + g, g, member).start()

    def spread(d, carry):
        lead_copy(lead_ref, member, 32 + d, group, lax.rem(member + d, members)).start()
        return carry

    lax.fori_loop(1, members, spread, 0)

    for dg, ds in sides:
        @pl.when(exists(-dg, -ds))
        def _():
            halo(dg, ds).wait_recv()

        @pl.when(exists(dg, ds))
        def _():
            halo(dg, ds).wait_send()

    def gather(d, carry):
        lead_copy(lead_ref, lax.rem(member + d, members), 0, group, member).wait_recv()
        lead_copy(lead_ref, member, 32 + d, group, member).wait_send()
        return carry

    lax.fori_loop(1, members, gather, 0)

    @pl.when(group == 0)
    def _():
        for g in range(1, groups):
            lead_copy(lead_ref, member, 64 + g, g, member).wait_send()

    @pl.when(root)
    def _():
        def sent(m, carry):
            lead_copy(base_ref, m, m, 0, m).wait_send()
            return carry

        lax.fori_loop(1, members, sent, 0)

    @pl.when(member == 0)
    def _():
        def sent(m, carry):
            base_copy(m).wait_send()
            return carry

        lax.fori_loop(1, EARLY, sent, 0)
        own_rows.wait()

    @pl.when((member > 0) & (member < EARLY))
    def _():
        base_copy(member).wait_recv()


def opening(high_x, low_x, high_y, low_y, base_front):
    vmem = pl.BlockSpec(memory_space=pltpu.VMEM)
    dma = pltpu.SemaphoreType.DMA
    return pl.pallas_call(
        opening_kernel,
        out_shape=[
            jax.ShapeDtypeStruct((1024, 128), BF),
            jax.ShapeDtypeStruct((1024, 128), BF),
            jax.ShapeDtypeStruct((1088, 128), BF),
            jax.ShapeDtypeStruct((1088, 128), BF),
            jax.ShapeDtypeStruct((512, 512), BF),
            jax.ShapeDtypeStruct((128, 512), BF),
        ],
        in_specs=[vmem] * 4 + [pl.BlockSpec(memory_space=pl.ANY)],
        out_specs=[vmem] * 6,
        scratch_shapes=[
            dma((8,)), dma((8,)), dma((68,)), dma((32,)), dma((32,)), dma, dma((2,)),
        ],
        compiler_params=pltpu.CompilerParams(
            collective_id=0, has_side_effects=True, vmem_limit_bytes=60 * 2**20
        ),
        name="opening",
    )(high_x, low_x, high_y, low_y, base_front)


def front_kernel(
    key_ref, tiles_ref, base_front_ref, early_ref, front_ref, strips, sums, added, late,
    strip_send, strip_recv, sum_send, sum_recv, base_send, base_recv, own_sem,
):
    groups, members, devices, parts, base = 4, 32, 128, 8, 8
    group = lax.axis_index("grp")
    member = lax.axis_index("sub")
    me = group * members + member
    takes = (member >= base) & (member < base + parts)
    barrier = pltpu.get_barrier_semaphore()

    @pl.when(takes)
    def _():
        def greet(d, carry):
            other = lax.rem(me + d, devices)
            pl.semaphore_signal(barrier, 1, device_id=at(other // members, lax.rem(other, members)))
            return carry

        lax.fori_loop(1, devices, greet, 0)

    @pl.when(jnp.logical_not(takes))
    def _():
        for r in range(parts):
            pl.semaphore_signal(barrier, 1, device_id=at(group, base + r))

    @pl.when(jnp.logical_not(takes) & (member > 0))
    def _():
        pl.semaphore_signal(barrier, 1, device_id=at(group, 0))

    pl.semaphore_wait(
        barrier, groups * parts + jnp.where(takes | (member == 0), members - parts - 1, 0)
    )

    def source(g, r):
        first = pl.ds(2 * members * g, 2)
        return tiles_ref.at[first, pl.ds(pl.multiple_of(16 * r, 16), 16)]

    def strip_copy(sender, g, r, k):
        return pltpu.make_async_remote_copy(
            source(g, r), strips.at[pl.ds(2 * sender, 2)], strip_send.at[k], strip_recv.at[sender],
            device_id=at(g, base + r),
        )

    own_rank = lax.rem(member, parts)
    own_strip = pltpu.make_async_copy(
        source(group, own_rank), strips.at[pl.ds(2 * me, 2)], own_sem.at[0]
    )

    def target(j):
        t = lax.rem(j + group * parts + own_rank, groups * parts)
        return t // parts, lax.rem(t, parts)

    def start_strip(j, carry):
        g, r = target(j)

        @pl.when((g != group) | (base + r != member))
        def _():
            strip_copy(me, g, r, j).start()

        return carry

    lax.fori_loop(0, groups * parts, start_strip, 0)

    def base_copy(m):
        rows = pl.ds(pl.multiple_of(128 * m, 128), 128)
        return pltpu.make_async_remote_copy(
            base_front_ref.at[rows], late, base_send.at[m], base_recv, device_id=at(group, m)
        )

    @pl.when(member == 0)
    def _():
        def send(m, carry):
            base_copy(m).start()
            return carry

        lax.fori_loop(EARLY, members, send, 0)

    def sum_copy(r, a):
        return pltpu.make_async_remote_copy(
            sums.at[pl.ds(4 * a, 4)], added.at[r], sum_send.at[a], sum_recv.at[r],
            device_id=at(group, a),
        )

    own_sum = pltpu.make_async_copy(
        sums.at[pl.ds(4 * member, 4)],
        added.at[own_rank],
        own_sem.at[1],
    )

    @pl.when(takes)
    def _():
        own_strip.start()

        def arrive(d, carry):
            strip_copy(lax.rem(me + d, devices), group, own_rank, 0).wait_recv()
            return carry

        lax.fori_loop(1, devices, arrive, 0)
        own_strip.wait()
        rows = strips[...].reshape(4096, 128)
        for n in range(8):
            ids = 256 * n + lax.broadcasted_iota(jnp.int32, (256, 4096), 0)
            pick = jnp.where(key_ref[...] == ids, 1.0, 0.0).astype(BF)
            sums[16 * n:16 * n + 16] = dotb(pick, rows, NN).astype(BF).reshape(16, 16, 128)

        def send(d, carry):
            sum_copy(own_rank, lax.rem(member + d, members)).start()
            return carry

        lax.fori_loop(1, members, send, 0)
        own_sum.start()

    for r in range(parts):
        @pl.when(member != base + r)
        def _():
            sum_copy(r, member).wait_recv()

    @pl.when(takes)
    def _():
        own_sum.wait()

    def summed(q):
        return jnp.concatenate([added[r, q] for r in range(parts)], axis=0).astype(F32)

    @pl.when(member < EARLY)
    def _():
        for q in range(4):
            cols = slice(128 * q, 128 * q + 128)
            front_ref[:, cols] = early_ref[:, cols].astype(F32) + summed(q)

    @pl.when(member >= EARLY)
    def _():
        base_copy(member).wait_recv()
        for q in range(4):
            cols = slice(128 * q, 128 * q + 128)
            front_ref[:, cols] = late[:, cols].astype(F32) + summed(q)

    def sent_strip(j, carry):
        g, r = target(j)

        @pl.when((g != group) | (base + r != member))
        def _():
            strip_copy(me, g, r, j).wait_send()

        return carry

    lax.fori_loop(0, groups * parts, sent_strip, 0)

    @pl.when(takes)
    def _():
        def sent(d, carry):
            sum_copy(own_rank, lax.rem(member + d, members)).wait_send()
            return carry

        lax.fori_loop(1, members, sent, 0)

    @pl.when(member == 0)
    def _():
        def sent(m, carry):
            base_copy(m).wait_send()
            return carry

        lax.fori_loop(EARLY, members, sent, 0)


def front_rows_of(key, tiles, base_front, early):
    dma = pltpu.SemaphoreType.DMA
    anywhere = pl.BlockSpec(memory_space=pl.ANY)
    vmem = pl.BlockSpec(memory_space=pltpu.VMEM)
    return pl.pallas_call(
        front_kernel,
        out_shape=jax.ShapeDtypeStruct((128, 512), F32),
        in_specs=[vmem, anywhere, anywhere, vmem],
        out_specs=vmem,
        scratch_shapes=[
            pltpu.VMEM((256, 16, 128), BF),
            pltpu.VMEM((128, 16, 128), BF),
            pltpu.VMEM((8, 4, 16, 128), BF),
            pltpu.VMEM((128, 512), BF),
            dma((32,)), dma((128,)), dma((32,)), dma((8,)), dma((32,)), dma, dma((2,)),
        ],
        compiler_params=pltpu.CompilerParams(
            collective_id=2, has_side_effects=True, vmem_limit_bytes=60 * 2**20
        ),
        name="front_rows",
    )(key, tiles, base_front, early)


def panel_kernel(
    panel_ref, rows_ref, cols_ref,
    send, recv, fold_send, fold_recv, col_send, col_recv, own_sem,
):
    groups, members = 4, 32
    group = lax.axis_index("grp")
    member = lax.axis_index("sub")
    x = member // 8
    z = lax.rem(member // 2, 4)
    core = lax.rem(member, 2)
    source_group = member // 8
    barrier = pltpu.get_barrier_semaphore()

    def greet(d, carry):
        pl.semaphore_signal(barrier, 1, device_id=at(group, lax.rem(member + d, members)))
        return carry

    lax.fori_loop(1, members, greet, 0)

    @pl.when(source_group < group)
    def _():
        for i in range(4):
            pl.semaphore_signal(
                barrier, 1, device_id=at(source_group, lax.rem(member, 8) * 4 + i)
            )

    pl.semaphore_wait(barrier, members - 1 + groups - 1 - group)

    def block(m):
        return pl.ds(pl.multiple_of(128 * m, 128), 128)

    def half_rows(m, half):
        return pl.ds(pl.multiple_of(128 * m + 64 * half, 64), 64)

    def wrap(v):
        return lax.rem(v + 4, 4)

    def where(bx, bz):
        return bx * 8 + bz * 2 + core

    pending = []

    def pass_on(half, bx, bz, own, dx, dz, condition):
        k = len(pending)
        m = where(bx, bz)
        source = panel_ref.at[pl.ds(64 * half, 64)] if own else rows_ref.at[half_rows(m, half)]
        copy = pltpu.make_async_remote_copy(
            source, rows_ref.at[half_rows(m, half)], send.at[k], recv.at[half, bx * 4 + bz],
            device_id=at(group, where(wrap(x + dx), wrap(z + dz))),
        )
        pending.append((copy, condition))
        if condition is None:
            copy.start()
        else:
            pl.when(condition)(copy.start)

    def fold_copy(half, bx, bz, side, source=None):
        m = bx * 8 + bz * 2 + side
        if source is None:
            source = rows_ref.at[half_rows(m, half)]
        return pltpu.make_async_remote_copy(
            source, rows_ref.at[half_rows(m, half)],
            fold_send.at[half, bx * 4 + bz], fold_recv.at[half, bx * 4 + bz],
            device_id=at(group, x * 8 + z * 2 + 1 - core),
        )

    def arrived(half, bx, bz):
        pltpu.make_async_remote_copy(
            panel_ref.at[pl.ds(0, 64)], rows_ref.at[half_rows(where(bx, bz), half)],
            send.at[0], recv.at[half, bx * 4 + bz], device_id=at(group, member),
        ).wait_recv()
        fold_copy(half, bx, bz, core).start()

    steps = (1, -1)
    for d in steps:
        pass_on(0, x, z, True, 0, d, None)
        pass_on(1, x, z, True, d, 0, None)
    for d in steps:
        pass_on(0, x, z, True, d, 0, None)
        pass_on(1, x, z, True, 0, d, None)

    target = group * 8 + member // 4
    quarter = lax.rem(member, 4)

    def col_copy(g, q, s):
        return pltpu.make_async_remote_copy(
            panel_ref, cols_ref.at[block(q)], col_send.at[g], col_recv.at[q], device_id=at(g, s)
        )

    for g in range(groups):
        @pl.when((g >= group) & jnp.logical_not((g == group) & (target == member)))
        def _():
            col_copy(g, quarter, target).start()

    own_cols = pltpu.make_async_copy(panel_ref, cols_ref.at[block(quarter)], own_sem.at[0])
    own_rows = pltpu.make_async_copy(panel_ref, rows_ref.at[block(member)], own_sem.at[1])

    @pl.when(target == member)
    def _():
        own_cols.start()

    own_rows.start()
    for half in range(2):
        fold_copy(half, x, z, core, panel_ref.at[pl.ds(64 * half, 64)]).start()

    even = lambda v: lax.rem(v, 2) == 0
    odd = lambda v: lax.rem(v, 2) == 1
    for d in steps:
        bz = wrap(z - d)
        arrived(0, x, bz)
        pass_on(0, x, bz, False, 0, d, even(bz) if d == 1 else odd(bz))
        bx = wrap(x - d)
        arrived(1, bx, z)
        pass_on(1, bx, z, False, d, 0, even(bx) if d == 1 else odd(bx))
        for e in steps:
            pass_on(0, x, bz, False, e, 0, None)
            pass_on(1, bx, z, False, 0, e, None)
    far_z, far_x = wrap(z + 2), wrap(x + 2)
    arrived(0, x, far_z)
    arrived(1, far_x, z)
    for e in steps:
        pass_on(0, x, far_z, False, e, 0, None)
        pass_on(1, far_x, z, False, 0, e, None)
    for o in (0, 1, 3, 2):
        for d in steps:
            bx, bz = wrap(x - d), wrap(z + o)
            arrived(0, bx, bz)
            pass_on(0, bx, bz, False, d, 0, even(bz) if d == 1 else odd(bz))
            bx, bz = wrap(x + o), wrap(z - d)
            arrived(1, bx, bz)
            pass_on(1, bx, bz, False, 0, d, even(bx) if d == 1 else odd(bx))
    for o in (0, 1, 3, 2):
        arrived(0, far_x, wrap(z + o))
        arrived(1, wrap(x + o), far_z)

    def folded(n, carry):
        for half in range(2):
            fold_copy(half, n // 4, lax.rem(n, 4), 1 - core).wait_recv()
            fold_copy(half, n // 4, lax.rem(n, 4), core).wait_send()
        return carry

    lax.fori_loop(0, 16, folded, 0)
    for copy, condition in pending:
        if condition is None:
            copy.wait_send()
        else:
            pl.when(condition)(copy.wait_send)
    for g in range(groups):
        @pl.when((g >= group) & jnp.logical_not((g == group) & (target == member)))
        def _():
            col_copy(g, quarter, target).wait_send()

    for i in range(4):
        source = lax.rem(member, 8) * 4 + i
        itself = (source_group == group) & (source == member)

        @pl.when((source_group <= group) & jnp.logical_not(itself))
        def _():
            col_copy(group, i, member).wait_recv()

    @pl.when(target == member)
    def _():
        own_cols.wait()

    own_rows.wait()


def panel_spread(panel):
    dma = pltpu.SemaphoreType.DMA
    anywhere = pl.BlockSpec(memory_space=pl.ANY)
    return pl.pallas_call(
        panel_kernel,
        out_shape=[jax.ShapeDtypeStruct((4096, 512), BF), jax.ShapeDtypeStruct((512, 512), BF)],
        in_specs=[pl.BlockSpec(memory_space=pltpu.VMEM)],
        out_specs=[anywhere, anywhere],
        scratch_shapes=[
            dma((40,)), dma((2, 16)), dma((2, 16)), dma((2, 16)), dma((4,)), dma((4,)), dma((2,)),
        ],
        compiler_params=pltpu.CompilerParams(
            collective_id=1, has_side_effects=True, vmem_limit_bytes=60 * 2**20
        ),
        name="panel_spread",
    )(panel)


def arrivals(owner_ids, local_block, owner):
    order = jnp.arange(owner_ids.shape[1], dtype=jnp.int32)[None, :]
    here = owner_ids == owner
    first = jnp.min(jnp.where(here, order, 1 << 20), axis=1, keepdims=True)
    one = jnp.max(jnp.where(here & (order == first), local_block, -1), axis=1)
    two = jnp.max(jnp.where(here & (order > first), local_block, -1), axis=1)
    return jnp.stack([one, two], axis=1).reshape(-1)


def per_device(basis_cols, diag_weight, link_weight, base_front, block_lists):
    groups, members, devices = 4, 32, 128
    group = lax.axis_index("grp")
    member = lax.axis_index("sub")
    me = group * members + member

    def scaled(b, w):
        return (w[..., None] * b.astype(F32)).astype(BF).reshape(1024, 128)

    before_x, after_x, before_y, after_y, lead, base_rows = opening(
        scaled(basis_cols[31], link_weight[31]),
        scaled(basis_cols[0], link_weight[0]),
        scaled(basis_cols[:, 31], link_weight[:, 31]),
        scaled(basis_cols[:, 0], link_weight[:, 0]),
        base_front,
    )

    own_list = lax.dynamic_index_in_dim(block_lists.reshape(devices, 128, 2), me, 0, keepdims=False)
    own_owner = own_list[:, 0] // members * members + own_list[:, 1] // groups
    order = jnp.arange(128)
    rank = jnp.sum(
        (own_owner[:, None] == own_owner[None, :]) & (order[None, :] < order[:, None]), axis=1
    )
    slots = (own_owner * 2 + rank).astype(jnp.int32)

    outgoing = galerkin_tiles(
        slots,
        basis_cols.reshape(32, 1024, 128),
        link_weight.reshape(32, 1, 1024),
        diag_weight.reshape(32, 1, 1024),
        before_y.reshape(34, 32, 128),
        after_y.reshape(34, 32, 128),
        before_x,
        after_x,
    )

    listed = block_lists.reshape(devices, 128, 2)
    row_block = listed[:, :, 0]
    col_block = listed[:, :, 1]
    owner_ids = row_block // members * members + col_block // groups
    local_block = row_block % members * groups + col_block % groups
    panel_place = arrivals(owner_ids, local_block, group * members)
    key = jnp.where(panel_place[:, None] < 0, -1, panel_place[:, None] * 16 + jnp.arange(16)[None, :])
    front_rows = front_rows_of(key.reshape(1, 4096), outgoing, base_front, base_rows)

    outgoing, lead, front_rows, owner_ids, local_block = lax.optimization_barrier(
        (outgoing, lead, front_rows, owner_ids, local_block)
    )
    received = lax.all_to_all(
        outgoing.reshape(devices, 2, 128, 128), ("grp", "sub"), split_axis=0, concat_axis=0, tiled=True
    ).reshape(256, 128, 128)
    place = arrivals(owner_ids, local_block, me)
    lead = lead.astype(F32)
    symmetric = jnp.tril(lead) + jnp.tril(lead, -1).T
    pivot_matrix = symmetric + jnp.diag(jnp.sum(jnp.abs(symmetric), axis=1) + 1.0)
    factor, inverse = pivot_factor(pivot_matrix)
    solved = dot32(front_rows, inverse, NT)
    in_lead = (group == 0) & (member < 4)
    own_factor = lax.dynamic_slice_in_dim(factor, 128 * jnp.minimum(member, 3), 128, 0)
    panel = jnp.where(in_lead, own_factor, solved).astype(BF)
    panel_rows, panel_cols = panel_spread(panel)
    trailing = trailing_front(place, panel_rows, panel_cols, base_front, received)
    return (trailing, panel)


def solution(mesh):
    return jax.shard_map(
        per_device,
        mesh=mesh,
        in_specs=(
            P("grp", "sub", None, None),
            P("grp", "sub", None),
            P("grp", "sub", None),
            P("grp", "sub"),
            P(),
        ),
        out_specs=(P("grp", "sub"), P(("grp", "sub"), None)),
        check_vma=False,
    )
```

```python
import functools

import jax
import jax.numpy as jnp
import numpy as np
from jax import lax
from jax.experimental import pallas as pl
from jax.experimental.pallas import tpu as pltpu
from jax.sharding import PartitionSpec as P

EARLY = 13
NT = (((1,), (1,)), ((), ()))
NN = (((1,), (0,)), ((), ()))
BF = jnp.bfloat16
F32 = jnp.float32


def dot32(a, b, dims):
    return lax.dot_general(a, b, dims, precision=lax.Precision.HIGHEST, preferred_element_type=F32)


def dotb(a, b, dims):
    return lax.dot_general(a, b, dims, preferred_element_type=F32)


def tile_kernel(
    slot_ref, basis_ref, link_ref, diag_ref, before_y_ref, after_y_ref,
    before_x_ref, after_x_ref, stencil_ref, out_ref,
    scaled_t, basis_t, partial, stage, sems, clear_sems,
):
    step = pl.program_id(0)
    gap = jnp.zeros((96, 128), BF)

    def sides(slot, plane):
        first = jnp.concatenate([gap, before_y_ref[plane + 1]], axis=0)
        last = jnp.concatenate([after_y_ref[plane + 1], gap], axis=0)
        scaled_t[slot, :, 0:128] = first.T
        scaled_t[slot, :, 1152:1280] = last.T

    def spread(slot, ring):
        windows = [scaled_t[slot, :, 256 * q:256 * q + 512] for q in range(4)]
        sums = dotb(jnp.concatenate(windows, axis=0), stencil_ref[...], NN)
        for q in range(4):
            partial[ring, :, 256 * q:256 * q + 256] = sums[128 * q:128 * q + 128]

    def copy_out(slot, q, target):
        return pltpu.make_async_copy(stage.at[slot, q], out_ref.at[target], sems.at[slot, q])

    def wait(slot):
        for q in range(4):
            copy_out(slot, q, 0).wait()

    def start(slot, plane):
        for q in range(4):
            copy_out(slot, q, slot_ref[plane * 4 + q]).start()

    def finish(plane, slot, low, mid, high):
        link = link_ref[plane]
        diag = diag_ref[plane]
        for q in range(4):
            cells = slice(256 * q, 256 * q + 256)
            around = partial[low, :, cells] + partial[mid, :, cells] + partial[high, :, cells]
            around = around - scaled_t[slot, :, 128 + 256 * q:384 + 256 * q].astype(F32)
            own = basis_t[slot, :, cells]
            image = diag[:, cells] * own.astype(F32) - link[:, cells] * around
            head = image.astype(BF)
            tail = (image - head.astype(F32)).astype(BF)
            stage[slot, q] = (dotb(own, head, NT) + dotb(own, tail, NT)).astype(BF)

    def clear(n):
        return pltpu.make_async_copy(
            stage.at[0, 0], out_ref.at[64 * (n // 2) + n % 2], clear_sems.at[n]
        )

    @pl.when(step == 0)
    def _():
        stage[0, 0] = jnp.zeros((128, 128), BF)
        for n in range(8):
            clear(n).start()
        for n in range(8):
            clear(n).wait()
        sides(1, -1)
        scaled_t[1, :, 128:1152] = before_x_ref[...].T
        spread(1, 3)

    for u in range(4):
        plane = step * 4 + u
        slot = u % 2
        turned = basis_ref[u].T
        basis_t[slot] = turned
        scaled_t[slot, :, 128:1152] = (turned.astype(F32) * link_ref[plane]).astype(BF)
        sides(slot, plane)
        spread(slot, u)
        if u < 3:
            pl.when(step > 0)(functools.partial(wait, 1 - slot))
        else:
            wait(1 - slot)
        finish(jnp.maximum(plane - 1, 0), 1 - slot, (u + 2) % 4, (u + 3) % 4, u)
        if u == 0:
            pl.when(step > 0)(functools.partial(start, 1 - slot, plane - 1))
        else:
            start(1 - slot, plane - 1)

    @pl.when(step == pl.num_programs(0) - 1)
    def _():
        sides(0, 32)
        scaled_t[0, :, 128:1152] = after_x_ref[...].T
        spread(0, 0)
        wait(1)
        finish(31, 1, 2, 3, 0)
        start(1, 31)
        wait(0)
        wait(1)


def galerkin_tiles(slots, basis, link, diag, before_y, after_y, before_x, after_x):
    k = np.arange(512)[:, None]
    n = np.arange(256)[None, :]
    near = (abs(k // 32 - 4 - n // 32) <= 1) & (abs(k % 32 - n % 32) <= 1)
    stencil = jnp.asarray(near.astype(np.float32), BF)
    cube = lambda t, s: (0, 0, 0)
    flat = lambda t, s: (0, 0)
    return pl.pallas_call(
        tile_kernel,
        out_shape=jax.ShapeDtypeStruct((256, 128, 128), BF),
        grid_spec=pltpu.PrefetchScalarGridSpec(
            num_scalar_prefetch=1,
            grid=(8,),
            in_specs=[
                pl.BlockSpec((4, 1024, 128), lambda t, s: (t, 0, 0)),
                pl.BlockSpec((32, 1, 1024), cube),
                pl.BlockSpec((32, 1, 1024), cube),
                pl.BlockSpec((34, 32, 128), cube),
                pl.BlockSpec((34, 32, 128), cube),
                pl.BlockSpec((1024, 128), flat),
                pl.BlockSpec((1024, 128), flat),
                pl.BlockSpec((512, 256), flat),
            ],
            out_specs=pl.BlockSpec(memory_space=pl.ANY),
            scratch_shapes=[
                pltpu.VMEM((2, 128, 1280), BF),
                pltpu.VMEM((2, 128, 1024), BF),
                pltpu.VMEM((4, 128, 1024), F32),
                pltpu.VMEM((2, 4, 128, 128), BF),
                pltpu.SemaphoreType.DMA((2, 4)),
                pltpu.SemaphoreType.DMA((8,)),
            ],
        ),
        compiler_params=pltpu.CompilerParams(
            dimension_semantics=("arbitrary",), vmem_limit_bytes=60 * 2**20
        ),
        name="galerkin_tiles",
    )(slots, basis, link, diag, before_y, after_y, before_x, after_x, stencil)


def factor_kernel(pivot_ref, factor_ref, inverse_ref, work):
    size = pivot_ref.shape[0]
    count = size // 128
    rows = lax.broadcasted_iota(jnp.int32, (128, 128), 0)
    lanes = lax.broadcasted_iota(jnp.int32, (128, 128), 1)
    sub8 = lax.broadcasted_iota(jnp.int32, (8, 128), 0)
    lane8 = lax.broadcasted_iota(jnp.int32, (8, 128), 1)
    all_rows = lax.broadcasted_iota(jnp.int32, (size, 1), 0)
    work[...] = pivot_ref[...]
    factor_ref[...] = jnp.zeros_like(factor_ref)
    inverse_ref[...] = jnp.zeros_like(inverse_ref)

    def one_block(b, carry):
        own = pl.ds(pl.multiple_of(128 * b, 128), 128)
        block = work[own, own]
        parts = [block[8 * i:8 * i + 8] for i in range(16)]
        for panel in range(16):
            cols = []
            for k in range(8):
                lane = slice(8 * panel + k, 8 * panel + k + 1)
                cols.append([jnp.broadcast_to(parts[i][:, lane], (8, 128)) for i in range(panel, 16)])
            for k in range(8):
                lane = 8 * panel + k
                pivot_row = jnp.broadcast_to(parts[panel][k:k + 1], (8, 128))
                pivot_row = jnp.where(lane8 == lane, 1.0, pivot_row)
                inverse = 1.0 / jnp.broadcast_to(cols[k][0][k:k + 1], (8, 128))
                heads = [None] * 8
                for l in range(k + 1, 8):
                    heads[l] = jnp.broadcast_to(cols[l][0][k:k + 1], (8, 128))
                for i in range(panel, 16):
                    ratio = cols[k][i - panel] * inverse
                    clear = lane8 == lane
                    if i == panel:
                        ratio = jnp.where(sub8 > k, ratio, 0.0)
                        clear = clear & (sub8 > k)
                    for l in range(k + 1, 8):
                        cols[l][i - panel] = cols[l][i - panel] - ratio * heads[l]
                    parts[i] = jnp.where(clear, 0.0, parts[i]) - ratio * pivot_row
        full = jnp.concatenate(parts, axis=0)
        pivots = jnp.sum(jnp.where(rows == lanes, full, 0.0), axis=1, keepdims=True)
        scale = 1.0 / jnp.sqrt(pivots)
        upper = jnp.where(rows <= lanes, full * scale, 0.0)
        inv = jnp.where(rows > lanes, full * scale, jnp.where(rows == lanes, scale, 0.0))
        below = dot32(work[:, own], inv, NT)
        below = jnp.where(all_rows >= 128 * b + 128, below, 0.0)
        factor_ref[:, own] = below
        factor_ref[own, own] = upper.T
        inverse_ref[own, own] = inv
        work[...] = work[...] - dot32(below, below, NT)
        return carry

    lax.fori_loop(0, count, one_block, 0)
    for b in range(1, count):
        own = slice(128 * b, 128 * b + 128)
        left = slice(0, 128 * b)
        product = dot32(factor_ref[own, left], inverse_ref[left, left], NN)
        inverse_ref[own, left] = -dot32(inverse_ref[own, own], product, NN)


def pivot_factor(pivot_matrix):
    size = pivot_matrix.shape[0]
    return pl.pallas_call(
        factor_kernel,
        out_shape=[jax.ShapeDtypeStruct((size, size), F32)] * 2,
        in_specs=[pl.BlockSpec(memory_space=pltpu.VMEM)],
        out_specs=[pl.BlockSpec(memory_space=pltpu.VMEM)] * 2,
        scratch_shapes=[pltpu.VMEM((size, size), F32)],
        compiler_params=pltpu.CompilerParams(vmem_limit_bytes=32 * 2**20),
        name="pivot_factor",
    )(pivot_matrix)


def final_kernel(
    place_ref, order_ref, start_ref, row_ref, col_ref, base_ref, received_ref, out_ref, sums
):
    step = pl.program_id(0)
    group = lax.axis_index("grp")
    member = lax.axis_index("sub")
    first_row = group * 4096 + step * 512
    col_start = member * 512
    live = (member > 0) & (first_row + 511 >= col_start)

    @pl.when(live)
    def _():
        sums[...] = jnp.zeros_like(sums)

        def add(k, carry):
            slot = order_ref[k]
            place = place_ref[slot] - 16 * step
            sums[place] = sums[place] + received_ref[slot].astype(F32)
            return carry

        lax.fori_loop(start_ref[step], start_ref[step + 1], add, 0)
        update = dotb(row_ref[...], col_ref[...], NT)
        rows = first_row + lax.broadcasted_iota(jnp.int32, (128, 128), 0)
        cols = col_start + lax.broadcasted_iota(jnp.int32, (128, 128), 1)
        for i in range(4):
            for j in range(4):
                r = slice(128 * i, 128 * i + 128)
                c = slice(128 * j, 128 * j + 128)
                value = base_ref[r, c].astype(F32) + sums[i * 4 + j] - update[r, c]
                out_ref[r, c] = jnp.where(rows + 128 * i >= cols + 128 * j, value, 0.0)

    @pl.when(jnp.logical_not(live))
    def _():
        out_ref[...] = jnp.zeros_like(out_ref)


def trailing_front(place, panel_rows, panel_cols, base, received):
    key = jnp.where(place < 0, 1 << 20, place)
    ids = jnp.arange(256, dtype=jnp.int32)
    before = (key[None, :] < key[:, None]) | (
        (key[None, :] == key[:, None]) & (ids[None, :] < ids[:, None])
    )
    rank = jnp.sum(before.astype(jnp.int32), axis=1)
    order = jnp.sum(jnp.where(rank[:, None] == ids[None, :], ids[:, None], 0), axis=0)
    edges = 16 * jnp.arange(9, dtype=jnp.int32)
    starts = jnp.sum((key[None, :] < edges[:, None]).astype(jnp.int32), axis=1)
    once = pl.Buffered(1)
    return pl.pallas_call(
        final_kernel,
        out_shape=jax.ShapeDtypeStruct((4096, 512), F32),
        grid_spec=pltpu.PrefetchScalarGridSpec(
            num_scalar_prefetch=3,
            grid=(8,),
            in_specs=[
                pl.BlockSpec((512, 512), lambda t, *_: (t, 0)),
                pl.BlockSpec((512, 512), lambda t, *_: (0, 0), pipeline_mode=once),
                pl.BlockSpec((512, 512), lambda t, *_: (t, 0)),
                pl.BlockSpec((256, 128, 128), lambda t, *_: (0, 0, 0), pipeline_mode=once),
            ],
            out_specs=pl.BlockSpec((512, 512), lambda t, *_: (t, 0)),
            scratch_shapes=[pltpu.VMEM((16, 128, 128), F32)],
        ),
        compiler_params=pltpu.CompilerParams(
            dimension_semantics=("arbitrary",), vmem_limit_bytes=60 * 2**20
        ),
        name="trailing_front",
    )(place, order, starts, panel_rows, panel_cols, base, received)


def at(group, member):
    return {"grp": group, "sub": member}


def opening_kernel(
    high_x, low_x, high_y, low_y, base_ref,
    before_x, after_x, before_y, after_y, lead_ref, rows_ref,
    halo_send, halo_recv, lead_send, lead_recv, base_send, base_recv, own_sem,
):
    groups, members = 4, 32
    group = lax.axis_index("grp")
    member = lax.axis_index("sub")
    barrier = pltpu.get_barrier_semaphore()
    sides = [(dg, ds) for dg in (-1, 0, 1) for ds in (-1, 0, 1) if (dg, ds) != (0, 0)]

    def exists(dg, ds):
        g, s = group + dg, member + ds
        return (g >= 0) & (g < groups) & (s >= 0) & (s < members)

    def greet(d, carry):
        pl.semaphore_signal(barrier, 1, device_id=at(group, lax.rem(member + d, members)))
        return carry

    lax.fori_loop(1, members, greet, 0)
    for d in range(1, groups):
        pl.semaphore_signal(barrier, 1, device_id=at(lax.rem(group + d, groups), member))
    for dg, ds in sides:
        if dg and ds:
            @pl.when(exists(dg, ds))
            def _():
                pl.semaphore_signal(barrier, 1, device_id=at(group + dg, member + ds))

    near_groups = 2 - jnp.where(group == 0, 1, 0) - jnp.where(group == groups - 1, 1, 0)
    near_members = 2 - jnp.where(member == 0, 1, 0) - jnp.where(member == members - 1, 1, 0)
    pl.semaphore_wait(barrier, members - 1 + groups - 1 + near_groups * near_members)

    def piece(m):
        return pl.ds(pl.multiple_of(16 * m, 16), 16)

    def lead_copy(source, m, k, g, s):
        return pltpu.make_async_remote_copy(
            source.at[piece(m)], lead_ref.at[piece(m)], lead_send.at[k], lead_recv.at[m],
            device_id=at(g, s),
        )

    def base_copy(m):
        rows = pl.ds(pl.multiple_of(128 * m, 128), 128)
        return pltpu.make_async_remote_copy(
            base_ref.at[rows], rows_ref, base_send.at[m], base_recv, device_id=at(group, m)
        )

    own_lead = pltpu.make_async_copy(base_ref.at[pl.ds(0, 16)], lead_ref.at[pl.ds(0, 16)], own_sem.at[0])
    own_rows = pltpu.make_async_copy(base_ref.at[pl.ds(0, 128)], rows_ref, own_sem.at[1])
    root = (group == 0) & (member == 0)

    @pl.when(root)
    def _():
        own_lead.start()

        def send(m, carry):
            lead_copy(base_ref, m, m, 0, m).start()
            return carry

        lax.fori_loop(1, members, send, 0)

    def halo(dg, ds):
        k = sides.index((dg, ds))
        if ds == 0:
            source, target = (high_x, before_x) if dg == 1 else (low_x, after_x)
        else:
            if dg == 0:
                source = high_y if ds == 1 else low_y
                place = pl.ds(32, 1024)
            else:
                face = high_x if dg == 1 else low_x
                source = face.at[pl.ds(992 if ds == 1 else 0, 32)]
                place = pl.ds(0 if dg == 1 else 1056, 32)
            target = (before_y if ds == 1 else after_y).at[place]
        return pltpu.make_async_remote_copy(
            source, target, halo_send.at[k], halo_recv.at[k], device_id=at(group + dg, member + ds)
        )

    for dg, ds in sides:
        @pl.when(exists(dg, ds))
        def _():
            halo(dg, ds).start()

        @pl.when(jnp.logical_not(exists(-dg, -ds)))
        def _():
            if ds == 0:
                target = before_x if dg == 1 else after_x
                target[...] = jnp.zeros_like(target)
            else:
                target = before_y if ds == 1 else after_y
                place = pl.ds(32, 1024) if dg == 0 else pl.ds(0 if dg == 1 else 1056, 32)
                target[place, :] = jnp.zeros((1024 if dg == 0 else 32, 128), BF)

    @pl.when(member == 0)
    def _():
        own_rows.start()

        def send(m, carry):
            base_copy(m).start()
            return carry

        lax.fori_loop(1, EARLY, send, 0)

    @pl.when(root)
    def _():
        own_lead.wait()

    @pl.when(jnp.logical_not(root))
    def _():
        lead_copy(lead_ref, member, 0, group, member).wait_recv()

    @pl.when(group == 0)
    def _():
        for g in range(1, groups):
            lead_copy(lead_ref, member, 64 + g, g, member).start()

    def spread(d, carry):
        lead_copy(lead_ref, member, 32 + d, group, lax.rem(member + d, members)).start()
        return carry

    lax.fori_loop(1, members, spread, 0)

    for dg, ds in sides:
        @pl.when(exists(-dg, -ds))
        def _():
            halo(dg, ds).wait_recv()

        @pl.when(exists(dg, ds))
        def _():
            halo(dg, ds).wait_send()

    def gather(d, carry):
        lead_copy(lead_ref, lax.rem(member + d, members), 0, group, member).wait_recv()
        lead_copy(lead_ref, member, 32 + d, group, member).wait_send()
        return carry

    lax.fori_loop(1, members, gather, 0)

    @pl.when(group == 0)
    def _():
        for g in range(1, groups):
            lead_copy(lead_ref, member, 64 + g, g, member).wait_send()

    @pl.when(root)
    def _():
        def sent(m, carry):
            lead_copy(base_ref, m, m, 0, m).wait_send()
            return carry

        lax.fori_loop(1, members, sent, 0)

    @pl.when(member == 0)
    def _():
        def sent(m, carry):
            base_copy(m).wait_send()
            return carry

        lax.fori_loop(1, EARLY, sent, 0)
        own_rows.wait()

    @pl.when((member > 0) & (member < EARLY))
    def _():
        base_copy(member).wait_recv()


def opening(high_x, low_x, high_y, low_y, base_front):
    vmem = pl.BlockSpec(memory_space=pltpu.VMEM)
    dma = pltpu.SemaphoreType.DMA
    return pl.pallas_call(
        opening_kernel,
        out_shape=[
            jax.ShapeDtypeStruct((1024, 128), BF),
            jax.ShapeDtypeStruct((1024, 128), BF),
            jax.ShapeDtypeStruct((1088, 128), BF),
            jax.ShapeDtypeStruct((1088, 128), BF),
            jax.ShapeDtypeStruct((512, 512), BF),
            jax.ShapeDtypeStruct((128, 512), BF),
        ],
        in_specs=[vmem] * 4 + [pl.BlockSpec(memory_space=pl.ANY)],
        out_specs=[vmem] * 6,
        scratch_shapes=[
            dma((8,)), dma((8,)), dma((68,)), dma((32,)), dma((32,)), dma, dma((2,)),
        ],
        compiler_params=pltpu.CompilerParams(
            collective_id=0, has_side_effects=True, vmem_limit_bytes=60 * 2**20
        ),
        name="opening",
    )(high_x, low_x, high_y, low_y, base_front)


def front_kernel(
    key_ref, tiles_ref, base_front_ref, early_ref, front_ref, strips, total, sums, added, late,
    strip_send, strip_recv, sum_send, sum_recv, base_send, base_recv, own_sem,
):
    groups, members, devices, parts, base = 4, 32, 128, 8, 8
    group = lax.axis_index("grp")
    member = lax.axis_index("sub")
    me = group * members + member
    takes = (member >= base) & (member < base + parts)
    barrier = pltpu.get_barrier_semaphore()

    @pl.when(takes)
    def _():
        def greet(d, carry):
            other = lax.rem(me + d, devices)
            pl.semaphore_signal(barrier, 1, device_id=at(other // members, lax.rem(other, members)))
            return carry

        lax.fori_loop(1, devices, greet, 0)

    @pl.when(jnp.logical_not(takes))
    def _():
        for r in range(parts):
            pl.semaphore_signal(barrier, 1, device_id=at(group, base + r))

    @pl.when(jnp.logical_not(takes) & (member > 0))
    def _():
        pl.semaphore_signal(barrier, 1, device_id=at(group, 0))

    pl.semaphore_wait(
        barrier, groups * parts + jnp.where(takes | (member == 0), members - parts - 1, 0)
    )

    def source(g, r):
        first = pl.ds(2 * members * g, 2)
        return tiles_ref.at[first, pl.ds(pl.multiple_of(16 * r, 16), 16)]

    def strip_copy(sender, g, r, k):
        return pltpu.make_async_remote_copy(
            source(g, r), strips.at[pl.ds(2 * sender, 2)], strip_send.at[k], strip_recv.at[sender],
            device_id=at(g, base + r),
        )

    own_rank = lax.rem(member, parts)
    own_strip = pltpu.make_async_copy(
        source(group, own_rank), strips.at[pl.ds(2 * me, 2)], own_sem.at[0]
    )

    def target(j):
        t = lax.rem(j + group * parts + own_rank, groups * parts)
        return t // parts, lax.rem(t, parts)

    def start_strip(j, carry):
        g, r = target(j)

        @pl.when((g != group) | (base + r != member))
        def _():
            strip_copy(me, g, r, j).start()

        return carry

    lax.fori_loop(0, groups * parts, start_strip, 0)

    def base_copy(m):
        rows = pl.ds(pl.multiple_of(128 * m, 128), 128)
        return pltpu.make_async_remote_copy(
            base_front_ref.at[rows], late, base_send.at[m], base_recv, device_id=at(group, m)
        )

    @pl.when(member == 0)
    def _():
        def send(m, carry):
            base_copy(m).start()
            return carry

        lax.fori_loop(EARLY, members, send, 0)

    def sum_copy(r, a):
        return pltpu.make_async_remote_copy(
            sums.at[pl.ds(4 * a, 4)], added.at[r], sum_send.at[a], sum_recv.at[r],
            device_id=at(group, a),
        )

    own_sum = pltpu.make_async_copy(
        sums.at[pl.ds(4 * member, 4)],
        added.at[own_rank],
        own_sem.at[1],
    )

    @pl.when(takes)
    def _():
        own_strip.start()

        ids = lax.broadcasted_iota(jnp.int32, (2048, 512), 0)
        for n in range(8):
            def arrive(k, carry):
                sender = 16 * n + k

                @pl.when(sender != me)
                def _():
                    strip_copy(sender, group, own_rank, 0).wait_recv()

                return carry

            lax.fori_loop(0, 16, arrive, 0)

            @pl.when(me // 16 == n)
            def _():
                own_strip.wait()

            rows = strips[32 * n:32 * n + 32].reshape(512, 128)
            pick = jnp.where(key_ref[:, 512 * n:512 * n + 512] == ids, 1.0, 0.0).astype(BF)
            part = dotb(pick, rows, NN)
            if n == 0:
                total[...] = part
            elif n < 7:
                total[...] += part
            else:
                sums[...] = (total[...] + part).astype(BF).reshape(128, 16, 128)

        def send(d, carry):
            sum_copy(own_rank, lax.rem(member + d, members)).start()
            return carry

        lax.fori_loop(1, members, send, 0)
        own_sum.start()

    for r in range(parts):
        @pl.when(member != base + r)
        def _():
            sum_copy(r, member).wait_recv()

    @pl.when(takes)
    def _():
        own_sum.wait()

    def summed(q):
        return jnp.concatenate([added[r, q] for r in range(parts)], axis=0).astype(F32)

    @pl.when(member < EARLY)
    def _():
        for q in range(4):
            cols = slice(128 * q, 128 * q + 128)
            front_ref[:, cols] = early_ref[:, cols].astype(F32) + summed(q)

    @pl.when(member >= EARLY)
    def _():
        base_copy(member).wait_recv()
        for q in range(4):
            cols = slice(128 * q, 128 * q + 128)
            front_ref[:, cols] = late[:, cols].astype(F32) + summed(q)

    def sent_strip(j, carry):
        g, r = target(j)

        @pl.when((g != group) | (base + r != member))
        def _():
            strip_copy(me, g, r, j).wait_send()

        return carry

    lax.fori_loop(0, groups * parts, sent_strip, 0)

    @pl.when(takes)
    def _():
        def sent(d, carry):
            sum_copy(own_rank, lax.rem(member + d, members)).wait_send()
            return carry

        lax.fori_loop(1, members, sent, 0)

    @pl.when(member == 0)
    def _():
        def sent(m, carry):
            base_copy(m).wait_send()
            return carry

        lax.fori_loop(EARLY, members, sent, 0)


def front_rows_of(key, tiles, base_front, early):
    dma = pltpu.SemaphoreType.DMA
    anywhere = pl.BlockSpec(memory_space=pl.ANY)
    vmem = pl.BlockSpec(memory_space=pltpu.VMEM)
    return pl.pallas_call(
        front_kernel,
        out_shape=jax.ShapeDtypeStruct((128, 512), F32),
        in_specs=[vmem, anywhere, anywhere, vmem],
        out_specs=vmem,
        scratch_shapes=[
            pltpu.VMEM((256, 16, 128), BF),
            pltpu.VMEM((2048, 128), F32),
            pltpu.VMEM((128, 16, 128), BF),
            pltpu.VMEM((8, 4, 16, 128), BF),
            pltpu.VMEM((128, 512), BF),
            dma((32,)), dma((128,)), dma((32,)), dma((8,)), dma((32,)), dma, dma((2,)),
        ],
        compiler_params=pltpu.CompilerParams(
            collective_id=2, has_side_effects=True, vmem_limit_bytes=60 * 2**20
        ),
        name="front_rows",
    )(key, tiles, base_front, early)


def panel_kernel(
    panel_ref, rows_ref, cols_ref,
    send, recv, fold_send, fold_recv, col_send, col_recv, own_sem,
):
    groups, members = 4, 32
    group = lax.axis_index("grp")
    member = lax.axis_index("sub")
    x = member // 8
    z = lax.rem(member // 2, 4)
    core = lax.rem(member, 2)
    source_group = member // 8
    barrier = pltpu.get_barrier_semaphore()

    def greet(d, carry):
        pl.semaphore_signal(barrier, 1, device_id=at(group, lax.rem(member + d, members)))
        return carry

    lax.fori_loop(1, members, greet, 0)

    @pl.when(source_group < group)
    def _():
        for i in range(4):
            pl.semaphore_signal(
                barrier, 1, device_id=at(source_group, lax.rem(member, 8) * 4 + i)
            )

    pl.semaphore_wait(barrier, members - 1 + groups - 1 - group)

    def block(m):
        return pl.ds(pl.multiple_of(128 * m, 128), 128)

    def half_rows(m, half):
        return pl.ds(pl.multiple_of(128 * m + 64 * half, 64), 64)

    def wrap(v):
        return lax.rem(v + 4, 4)

    def where(bx, bz):
        return bx * 8 + bz * 2 + core

    pending = []

    def pass_on(half, bx, bz, own, dx, dz, condition):
        k = len(pending)
        m = where(bx, bz)
        source = panel_ref.at[pl.ds(64 * half, 64)] if own else rows_ref.at[half_rows(m, half)]
        copy = pltpu.make_async_remote_copy(
            source, rows_ref.at[half_rows(m, half)], send.at[k], recv.at[half, bx * 4 + bz],
            device_id=at(group, where(wrap(x + dx), wrap(z + dz))),
        )
        pending.append((copy, condition))
        if condition is None:
            copy.start()
        else:
            pl.when(condition)(copy.start)

    def fold_copy(half, bx, bz, side, source=None):
        m = bx * 8 + bz * 2 + side
        if source is None:
            source = rows_ref.at[half_rows(m, half)]
        return pltpu.make_async_remote_copy(
            source, rows_ref.at[half_rows(m, half)],
            fold_send.at[half, bx * 4 + bz], fold_recv.at[half, bx * 4 + bz],
            device_id=at(group, x * 8 + z * 2 + 1 - core),
        )

    def arrived(half, bx, bz):
        pltpu.make_async_remote_copy(
            panel_ref.at[pl.ds(0, 64)], rows_ref.at[half_rows(where(bx, bz), half)],
            send.at[0], recv.at[half, bx * 4 + bz], device_id=at(group, member),
        ).wait_recv()
        fold_copy(half, bx, bz, core).start()

    steps = (1, -1)
    for d in steps:
        pass_on(0, x, z, True, 0, d, None)
        pass_on(1, x, z, True, d, 0, None)
    for d in steps:
        pass_on(0, x, z, True, d, 0, None)
        pass_on(1, x, z, True, 0, d, None)

    target = group * 8 + member // 4
    quarter = lax.rem(member, 4)

    def col_copy(g, q, s):
        return pltpu.make_async_remote_copy(
            panel_ref, cols_ref.at[block(q)], col_send.at[g], col_recv.at[q], device_id=at(g, s)
        )

    for g in range(groups):
        @pl.when((g >= group) & jnp.logical_not((g == group) & (target == member)))
        def _():
            col_copy(g, quarter, target).start()

    own_cols = pltpu.make_async_copy(panel_ref, cols_ref.at[block(quarter)], own_sem.at[0])
    own_rows = pltpu.make_async_copy(panel_ref, rows_ref.at[block(member)], own_sem.at[1])

    @pl.when(target == member)
    def _():
        own_cols.start()

    own_rows.start()
    for half in range(2):
        fold_copy(half, x, z, core, panel_ref.at[pl.ds(64 * half, 64)]).start()

    even = lambda v: lax.rem(v, 2) == 0
    odd = lambda v: lax.rem(v, 2) == 1
    for d in steps:
        bz = wrap(z - d)
        arrived(0, x, bz)
        pass_on(0, x, bz, False, 0, d, even(bz) if d == 1 else odd(bz))
        bx = wrap(x - d)
        arrived(1, bx, z)
        pass_on(1, bx, z, False, d, 0, even(bx) if d == 1 else odd(bx))
        for e in steps:
            pass_on(0, x, bz, False, e, 0, None)
            pass_on(1, bx, z, False, 0, e, None)
    far_z, far_x = wrap(z + 2), wrap(x + 2)
    arrived(0, x, far_z)
    arrived(1, far_x, z)
    for e in steps:
        pass_on(0, x, far_z, False, e, 0, None)
        pass_on(1, far_x, z, False, 0, e, None)
    for o in (0, 1, 3, 2):
        for d in steps:
            bx, bz = wrap(x - d), wrap(z + o)
            arrived(0, bx, bz)
            pass_on(0, bx, bz, False, d, 0, even(bz) if d == 1 else odd(bz))
            bx, bz = wrap(x + o), wrap(z - d)
            arrived(1, bx, bz)
            pass_on(1, bx, bz, False, 0, d, even(bx) if d == 1 else odd(bx))
    for o in (0, 1, 3, 2):
        arrived(0, far_x, wrap(z + o))
        arrived(1, wrap(x + o), far_z)

    def folded(n, carry):
        for half in range(2):
            fold_copy(half, n // 4, lax.rem(n, 4), 1 - core).wait_recv()
            fold_copy(half, n // 4, lax.rem(n, 4), core).wait_send()
        return carry

    lax.fori_loop(0, 16, folded, 0)
    for copy, condition in pending:
        if condition is None:
            copy.wait_send()
        else:
            pl.when(condition)(copy.wait_send)
    for g in range(groups):
        @pl.when((g >= group) & jnp.logical_not((g == group) & (target == member)))
        def _():
            col_copy(g, quarter, target).wait_send()

    for i in range(4):
        source = lax.rem(member, 8) * 4 + i
        itself = (source_group == group) & (source == member)

        @pl.when((source_group <= group) & jnp.logical_not(itself))
        def _():
            col_copy(group, i, member).wait_recv()

    @pl.when(target == member)
    def _():
        own_cols.wait()

    own_rows.wait()


def panel_spread(panel):
    dma = pltpu.SemaphoreType.DMA
    anywhere = pl.BlockSpec(memory_space=pl.ANY)
    return pl.pallas_call(
        panel_kernel,
        out_shape=[jax.ShapeDtypeStruct((4096, 512), BF), jax.ShapeDtypeStruct((512, 512), BF)],
        in_specs=[pl.BlockSpec(memory_space=pltpu.VMEM)],
        out_specs=[anywhere, anywhere],
        scratch_shapes=[
            dma((40,)), dma((2, 16)), dma((2, 16)), dma((2, 16)), dma((4,)), dma((4,)), dma((2,)),
        ],
        compiler_params=pltpu.CompilerParams(
            collective_id=1, has_side_effects=True, vmem_limit_bytes=60 * 2**20
        ),
        name="panel_spread",
    )(panel)


def arrivals(owner_ids, local_block, owner):
    order = jnp.arange(owner_ids.shape[1], dtype=jnp.int32)[None, :]
    here = owner_ids == owner
    first = jnp.min(jnp.where(here, order, 1 << 20), axis=1, keepdims=True)
    one = jnp.max(jnp.where(here & (order == first), local_block, -1), axis=1)
    two = jnp.max(jnp.where(here & (order > first), local_block, -1), axis=1)
    return jnp.stack([one, two], axis=1).reshape(-1)


def per_device(basis_cols, diag_weight, link_weight, base_front, block_lists):
    groups, members, devices = 4, 32, 128
    group = lax.axis_index("grp")
    member = lax.axis_index("sub")
    me = group * members + member

    def scaled(b, w):
        return (w[..., None] * b.astype(F32)).astype(BF).reshape(1024, 128)

    before_x, after_x, before_y, after_y, lead, base_rows = opening(
        scaled(basis_cols[31], link_weight[31]),
        scaled(basis_cols[0], link_weight[0]),
        scaled(basis_cols[:, 31], link_weight[:, 31]),
        scaled(basis_cols[:, 0], link_weight[:, 0]),
        base_front,
    )

    own_list = lax.dynamic_index_in_dim(block_lists.reshape(devices, 128, 2), me, 0, keepdims=False)
    own_owner = own_list[:, 0] // members * members + own_list[:, 1] // groups
    order = jnp.arange(128)
    rank = jnp.sum(
        (own_owner[:, None] == own_owner[None, :]) & (order[None, :] < order[:, None]), axis=1
    )
    slots = (own_owner * 2 + rank).astype(jnp.int32)

    outgoing = galerkin_tiles(
        slots,
        basis_cols.reshape(32, 1024, 128),
        link_weight.reshape(32, 1, 1024),
        diag_weight.reshape(32, 1, 1024),
        before_y.reshape(34, 32, 128),
        after_y.reshape(34, 32, 128),
        before_x,
        after_x,
    )

    listed = block_lists.reshape(devices, 128, 2)
    row_block = listed[:, :, 0]
    col_block = listed[:, :, 1]
    owner_ids = row_block // members * members + col_block // groups
    local_block = row_block % members * groups + col_block % groups
    panel_place = arrivals(owner_ids, local_block, group * members)
    key = jnp.where(panel_place[:, None] < 0, -1, panel_place[:, None] * 16 + jnp.arange(16)[None, :])
    front_rows = front_rows_of(key.reshape(1, 4096), outgoing, base_front, base_rows)

    outgoing, lead, front_rows, owner_ids, local_block = lax.optimization_barrier(
        (outgoing, lead, front_rows, owner_ids, local_block)
    )
    received = lax.all_to_all(
        outgoing.reshape(devices, 2, 128, 128), ("grp", "sub"), split_axis=0, concat_axis=0, tiled=True
    ).reshape(256, 128, 128)
    place = arrivals(owner_ids, local_block, me)
    lead = lead.astype(F32)
    symmetric = jnp.tril(lead) + jnp.tril(lead, -1).T
    pivot_matrix = symmetric + jnp.diag(jnp.sum(jnp.abs(symmetric), axis=1) + 1.0)
    factor, inverse = pivot_factor(pivot_matrix)
    solved = dot32(front_rows, inverse, NT)
    in_lead = (group == 0) & (member < 4)
    own_factor = lax.dynamic_slice_in_dim(factor, 128 * jnp.minimum(member, 3), 128, 0)
    panel = jnp.where(in_lead, own_factor, solved).astype(BF)
    panel_rows, panel_cols = panel_spread(panel)
    trailing = trailing_front(place, panel_rows, panel_cols, base_front, received)
    return (trailing, panel)


def solution(mesh):
    return jax.shard_map(
        per_device,
        mesh=mesh,
        in_specs=(
            P("grp", "sub", None, None),
            P("grp", "sub", None),
            P("grp", "sub", None),
            P("grp", "sub"),
            P(),
        ),
        out_specs=(P("grp", "sub"), P(("grp", "sub"), None)),
        check_vma=False,
    )
```
